512 devices in a mesh: gx: 8 (over y, x_hi), gy: 4 (over x_lo, core), gz: 16 (over z).
Axes of the slice: x: 4 (x_hi: 2, x_lo: 2; x = x_hi * 2 + x_lo), y: 4, z: 16, core: 2. Of those that a mesh axis runs over, the one named last changes fastest.
Arguments:
- noise_vectors: bfloat16 [9, 65536, 128], P(None, ('gx', 'gy', 'gz')), may hold values from -6 to 6
- hamiltonian: bfloat16 [15, 9, 9, 65536], P(None, None, None, ('gx', 'gy', 'gz')), may hold values from -0.25 to 0.25
- derivative: bfloat16 [3, 15, 9, 9, 65536], P(None, None, None, None, ('gx', 'gy', 'gz')), may hold values from -0.625 to 0.625
- neighbours: int32 [65536, 15], P(('gx', 'gy', 'gz')), may hold values from 0 to 65535, as said below
- coefficients: float32 [4], replicated, may hold values from -1 to 1
Outputs:
- weighted: float32 [9, 65536, 128], P(None, ('gx', 'gy', 'gz'))
- forces: float32 [3, 65536], P(None, ('gx', 'gy', 'gz'))
The draws below stay inside these ranges and needn't reach their ends.
Inputs may be any that keep to these rules, and one draw needn't show every extreme that they name: `neighbours`: slot 0 of every atom's list is the atom itself; the other 14 slots name distinct other atoms whose cells differ from its own by at most one along each dimension, periodically on the grid of 32 x 16 x 64 cells with two atoms a cell. Atom ids run over domains in the order gx, gy, gz, each domain holding 128 atoms numbered by (atom of the cell, first, second, third cell index within the domain).
All inputs are finite; a program needn't handle non-finite values.
Results may differ from the reference program's by a relative error of at most 0.0003.
Values may be sent and summed in bfloat16 or wider, within the bound.
No kernel may reach another device: no remote copies, remote signals or barrier semaphores. Data moves between devices by JAX's collectives and lax.ppermute only.
A program may use at most 128 MiB of HBM per device.

```python
import jax
import jax.numpy as jnp
from jax import lax

CX = 4
CY = 4
CZ = 4
NV = 128
ORB = 9
NEIGH = 15
ORDER = 3
NXC = 32
NYC = 16
NZC = 64
ATOM_DEV = 128
ATOMS = 65536
N_GY = 4
N_GZ = 16


def atom_place(atom_ids):
    cell_count = CX * CY * CZ
    domain = atom_ids // ATOM_DEV
    within = atom_ids % ATOM_DEV
    dom_x = domain // (N_GY * N_GZ)
    dom_y = domain // N_GZ % N_GY
    dom_z = domain % N_GZ
    basis_index = within // cell_count
    remain = within % cell_count
    cell_x = dom_x * CX + remain // (CY * CZ)
    cell_y = dom_y * CY + remain // CZ % CY
    cell_z = dom_z * CZ + remain % CZ
    return (basis_index, cell_x, cell_y, cell_z)


def atom_number(basis_index, cell_x, cell_y, cell_z):
    domain = (cell_x // CX * N_GY + cell_y // CY) * N_GZ + cell_z // CZ
    within = ((basis_index * CX + cell_x % CX) * CY + cell_y % CY) * CZ + cell_z % CZ
    return domain * ATOM_DEV + within


def draw_neighbours(key, part):
    key = jax.random.fold_in(key, 7)
    atom_ids = jnp.arange(ATOMS, dtype=jnp.int32)
    candidates = jnp.arange(54, dtype=jnp.int32)
    shift_x = candidates // 18 - 1
    shift_y = candidates // 6 % 3 - 1
    shift_z = candidates // 2 % 3 - 1
    cand_basis = candidates % 2
    basis_index, cell_x, cell_y, cell_z = atom_place(atom_ids)
    scores = jax.random.randint(key, (ATOMS, 54), 0, 1 << 20, dtype=jnp.int32) * 64 + candidates[None, :]
    is_self = (shift_x == 0) & (shift_y == 0) & (shift_z == 0)
    is_self = is_self[None, :] & (cand_basis[None, :] == basis_index[:, None])
    scores = jnp.where(is_self, jnp.int32(1 << 30), scores)
    ranking, chosen = lax.top_k(scores, NEIGH)
    part_x = jnp.remainder(cell_x[:, None] + shift_x[chosen], NXC)
    part_y = jnp.remainder(cell_y[:, None] + shift_y[chosen], NYC)
    part_z = jnp.remainder(cell_z[:, None] + shift_z[chosen], NZC)
    return atom_number(cand_basis[chosen], part_x, part_y, part_z).astype(jnp.int32)


def steps_of(stream_key, extent, cuts, low, top_value):
    def one(axis_at, shards_of):
        steps = jax.random.uniform(jax.random.fold_in(jax.random.fold_in(stream_key, 6), axis_at), (shards_of,), jnp.float32, low / len(cuts), top_value / len(cuts))
        return jnp.repeat(jnp.exp(steps), extent[axis_at] // shards_of).reshape((-1,) + (1,) * (len(extent) - axis_at - 1))

    gain = one(*cuts[0])
    for cut in cuts[1:]:
        gain = gain * one(*cut)
    return gain


def bell_draw(own_key, extent, spread, limit, split=(), held_as=jnp.bfloat16):
    entries = jax.random.normal(own_key, extent, jnp.float32) * spread
    if len(split) > 0:
        entries = steps_of(own_key, extent, split, -0.22, 0.18) * entries
    return jnp.clip(entries, min=-limit, max=limit).astype(held_as)


def setup_inputs(seed: int = 0) -> dict:
    key_of = jax.random.split(jax.random.key(seed), 6)
    noise_vectors = bell_draw(key_of[0], (ORB, ATOMS, NV), 1.0, 6.0, ((1, 512),))
    hamiltonian = bell_draw(key_of[1], (NEIGH, ORB, ORB, ATOMS), (4 * NEIGH * ORB) ** -0.5, 0.25, ((3, 512),))
    derivative = bell_draw(key_of[2], (3, NEIGH, ORB, ORB, ATOMS), (ORB * ORB) ** -0.5, 0.625, ((4, 512),))
    neighbours = draw_neighbours(jax.random.fold_in(key_of[5], 71), 0)
    coefficients = jnp.clip(jax.random.uniform(key_of[4], (ORDER + 1,), jnp.float32, -1.0, 1.0), -1.0, 1.0)
    return {"noise_vectors": noise_vectors, "hamiltonian": hamiltonian, "derivative": derivative, "neighbours": neighbours, "coefficients": coefficients}


def reference(noise_vectors, hamiltonian, derivative, neighbours, coefficients):
    highest = lax.Precision.HIGHEST

    def apply_blocks(vectors_in):
        summed = jnp.zeros(vectors_in.shape, jnp.float32)
        for slot_index in range(NEIGH):
            gathered = vectors_in[:, neighbours[:, slot_index]]
            blocks = hamiltonian[slot_index].astype(jnp.float32)
            summed = summed + jnp.einsum("abi,biv->aiv", blocks, gathered, precision=highest)
        return summed

    current = noise_vectors.astype(jnp.float32)
    result = coefficients[0] * current
    following = apply_blocks(current)
    result = result + coefficients[1] * following
    chain_prev = current
    chain_now = following
    for order_index in range(2, ORDER + 1):
        following = 2.0 * apply_blocks(chain_now) - chain_prev
        result = result + coefficients[order_index] * following
        chain_prev = chain_now
        chain_now = following

    forces = jnp.zeros((ATOMS, 3), jnp.float32)
    for slot_index in range(1, NEIGH):
        partner = neighbours[:, slot_index]
        gathered = current[:, partner]
        density = jnp.einsum("aiv,biv->iab", result, gathered, precision=highest) / NV
        pair_force = jnp.einsum("cabi,iab->ic", derivative[:, slot_index].astype(jnp.float32), density, precision=highest)
        forces = forces + jax.ops.segment_sum(pair_force, partner, num_segments=ATOMS) - pair_force
    return result, forces.T
```

```python
import functools

import jax
import jax.numpy as jnp
from jax import lax
from jax.experimental import pallas as pl
from jax.experimental.pallas import tpu as pltpu
from jax.sharding import PartitionSpec as P

CX = 4
CY = 4
CZ = 4
ORB = 9
NEIGH = 15
ATOMS = 2 * CX * CY * CZ
VECS = 128
NX = 2 * CY * CZ
NY = 2 * (CX + 2) * CZ
NZ = 2 * (CX + 2) * (CY + 2)
NZ_PAD = 80
BEFORE_Y = ATOMS + 2 * NX
BEFORE_Z = BEFORE_Y + 2 * NY
SLOTS = BEFORE_Z + 2 * NZ
LANES_Z = 384
LANES = 640
F32 = jnp.float32
BF16 = jnp.bfloat16
VMEM = pl.BlockSpec(memory_space=pltpu.VMEM)
SMEM = pl.BlockSpec(memory_space=pltpu.SMEM)


def call(kernel, outs, in_specs, args, scratch=(), flops=0, mib=16):
    shapes = [jax.ShapeDtypeStruct(shape, dtype) for shape, dtype in outs]
    moved = sum(a.size * a.dtype.itemsize for a in args) + sum(s.size * s.dtype.itemsize for s in shapes)
    return pl.pallas_call(
        kernel,
        out_shape=shapes,
        in_specs=in_specs,
        out_specs=[VMEM] * len(shapes),
        scratch_shapes=list(scratch),
        compiler_params=pltpu.CompilerParams(vmem_limit_bytes=mib << 20),
        cost_estimate=pl.CostEstimate(flops=flops, bytes_accessed=moved, transcendentals=0),
    )(*args)


def shifted(value, axis, steps):
    count = lax.axis_size(axis)
    return lax.ppermute(value, axis, [(i, (i + steps) % count) for i in range(count)])


def prep_kernel(ham, rows, turned, wide):
    turned[...] = jnp.zeros_like(turned)
    wide[...] = jnp.zeros_like(wide)
    for a in range(ORB):
        for b in range(ORB):
            turned[pl.ds(b, NEIGH, stride=16), :] = ham[a, b].astype(F32)
        flat = turned[...].T
        wide[0, pl.ds(a, ATOMS, stride=16), :] = flat[:, 0:128]
        wide[1, pl.ds(a, ATOMS, stride=16), :] = flat[:, 128:256]

    def pack(i, carry):
        at = pl.ds(pl.multiple_of(i * 16, 16), 16)
        rows[i, :, 0:128] = wide[0, at, :].astype(BF16)
        rows[i, :, 128:256] = wide[1, at, :].astype(BF16)
        return carry

    lax.fori_loop(0, ATOMS, pack, 0, unroll=8)


def faces_y_kernel(own, x_low, x_high, low, high, held, picked):
    for b in range(ORB):
        held[0:ATOMS] = own[b].astype(F32)
        held[ATOMS : ATOMS + NX] = x_low[b].astype(F32)
        held[ATOMS + NX : BEFORE_Y] = x_high[b].astype(F32)
        for out, y in ((low, 0), (high, CY - 1)):
            for q in range(NY // CZ):
                picked[4 * q : 4 * q + 4] = held[16 * q + 4 * y : 16 * q + 4 * y + 4]
            out[b] = picked[...].astype(out.dtype)


def faces_z_kernel(own, x_low, x_high, y_low, y_high, low, high, held):
    pieces = ((own, ATOMS), (x_low, NX), (x_high, NX), (y_low, NY), (y_high, NY))
    rows = low.shape[1]
    held[BEFORE_Z:] = jnp.zeros((4 * NZ_PAD - BEFORE_Z, VECS), F32)
    for b in range(ORB):
        base = 0
        for ref, count in pieces:
            held[base : base + count] = ref[b].astype(F32)
            base += count
        for out, z in ((low, 0), (high, CZ - 1)):
            out[b] = held[pl.ds(z, rows, stride=4), :].astype(out.dtype)


def load_tiles(pieces, loose):
    zero = jnp.zeros((8, VECS), F32)

    def clear(j, carry):
        loose[pl.ds(pl.multiple_of(j * 16 + 8, 8), 8), :] = zero
        return carry

    lax.fori_loop(0, SLOTS, clear, 0, unroll=16)
    for b in range(ORB):
        base = 0
        for ref, count in pieces:
            loose[pl.ds(base * 16 + b, count, stride=16), :] = ref[b].astype(F32)[0:count]
            base += count


def split_tiles(loose, tiles):
    def split(j, carry):
        value = loose[pl.ds(pl.multiple_of(j * 16, 16), 16), :]
        high = value.astype(BF16)
        tiles[j, :, 0:128] = high
        if tiles.shape[2] == 256:
            tiles[j, :, 128:256] = (value - high.astype(F32)).astype(BF16)
        return carry

    lax.fori_loop(0, SLOTS, split, 0, unroll=16)


def gather(slots, tiles, i):
    taken = [tiles[slots[m, i]] for m in range(NEIGH)]
    return jnp.concatenate(taken + taken[:1], axis=0)


def apply_atoms(slots, rows, tiles, applied):
    def atom(i, carry):
        product = jnp.dot(rows[i], gather(slots, tiles, i), preferred_element_type=F32)
        if tiles.shape[2] == 256:
            product = product[:, 0:128] + product[:, 128:256]
        applied[pl.ds(pl.multiple_of(i * 16, 16), 16), :] = product
        return carry

    lax.fori_loop(0, ATOMS, atom, 0, unroll=16)


def put_faces(b, value, low, high):
    for p in range(2):
        low[b, 16 * p : 16 * p + 16] = value[64 * p : 64 * p + 16]
        high[b, 16 * p : 16 * p + 16] = value[64 * p + 48 : 64 * p + 64]


def first_kernel(coef, slots, rows, own, xl, xh, yl, yh, zl, zh, now, total, low, high, tiles, loose, applied):
    pieces = ((own, ATOMS), (xl, NX), (xh, NX), (yl, NY), (yh, NY), (zl, NZ), (zh, NZ))
    load_tiles(pieces, loose)
    split_tiles(loose, tiles)
    apply_atoms(slots, rows, tiles, applied)
    for a in range(ORB):
        value = applied[pl.ds(a, ATOMS, stride=16), :]
        now[a] = value
        total[a] = coef[0] * own[a].astype(F32) + coef[1] * value
        put_faces(a, value, low, high)


def second_kernel(coef, slots, rows, prev, sum_in, own, xl, xh, yl, yh, zl, zh, now, total, low, high, loose, tiles, applied):
    pieces = ((own, ATOMS), (xl, NX), (xh, NX), (yl, NY), (yh, NY), (zl, NZ), (zh, NZ))
    load_tiles(pieces, loose)
    split_tiles(loose, tiles)
    apply_atoms(slots, rows, tiles, applied)
    for a in range(ORB):
        value = 2.0 * applied[pl.ds(a, ATOMS, stride=16), :] - prev[a].astype(F32)
        now[a] = value
        total[a] = sum_in[a] + coef[2] * value
        put_faces(a, value, low, high)


def third_kernel(coef, slots, lanes, rows, prev, sum_in, noise_tiles, deriv, own, xl, xh, yl, yh, zl, zh,
                 total, forces, loose, tiles, applied, dense, turned, stacked):
    pieces = ((own, ATOMS), (xl, NX), (xh, NX), (yl, NY), (yh, NY), (zl, NZ), (zh, NZ))
    load_tiles(pieces, loose)
    split_tiles(loose, tiles)
    apply_atoms(slots, rows, tiles, applied)
    for a in range(ORB):
        at = pl.ds(a, ATOMS, stride=16)
        value = sum_in[a] + coef[3] * (2.0 * applied[at, :] - prev[a])
        total[a] = value
        applied[at, :] = value

    def atom(i, carry):
        at = pl.ds(pl.multiple_of(i * 16, 16), 16)
        value = applied[at, :]
        high = value.astype(BF16)
        low = (value - high.astype(F32)).astype(BF16)
        product = lax.dot_general(
            jnp.concatenate([high, low], axis=0),
            gather(slots, noise_tiles, i),
            (((1,), (1,)), ((), ())),
            preferred_element_type=F32,
        )
        product = product[0:16] + product[16:32]
        dense[0, at, :] = product[:, 0:128]
        dense[1, at, :] = product[:, 128:256]
        return carry

    lax.fori_loop(0, ATOMS, atom, 0, unroll=16)
    pair = [jnp.zeros((NEIGH, ATOMS), F32) for _ in range(3)]
    for a in range(ORB):
        at = pl.ds(a, ATOMS, stride=16)
        turned[0:128] = dense[0, at, :].T
        turned[128:256] = dense[1, at, :].T
        for b in range(ORB):
            density = turned[pl.ds(b, NEIGH, stride=16), :]
            for c in range(3):
                pair[c] = pair[c] + deriv[c, a, b].astype(F32) * density
    others = lax.broadcasted_iota(jnp.int32, (NEIGH, ATOMS), 0) > 0
    stacked[...] = jnp.zeros_like(stacked)
    own_rows = []
    for c in range(3):
        value = jnp.where(others, pair[c] * (1.0 / VECS), 0.0)
        high = value.astype(BF16).astype(F32)
        stacked[pl.ds(c, NEIGH, stride=16), :] = high
        stacked[pl.ds(8 + c, NEIGH, stride=16), :] = value - high
        own_rows.append(jnp.sum(value, axis=0, keepdims=True))
    lane = lax.broadcasted_iota(jnp.int32, (LANES, ATOMS), 0)
    summed = jnp.zeros((16, LANES), F32)
    for m in range(1, NEIGH):
        hit = jnp.where(lane == lanes[m : m + 1, :], 1.0, 0.0).astype(BF16)
        summed = summed + lax.dot_general(
            stacked[16 * m : 16 * m + 16].astype(BF16), hit, (((1,), (1,)), ((), ())), preferred_element_type=F32
        )
    forces[...] = summed[0:8] + summed[8:16]
    for c in range(3):
        forces[c : c + 1, 0:ATOMS] = forces[c : c + 1, 0:ATOMS] - own_rows[c]


def spread(value, place, width):
    row = lax.broadcasted_iota(jnp.int32, (VECS, width), 0)
    lane = lax.broadcasted_iota(jnp.int32, (VECS, width), 1)
    hit = jnp.where((lane == place(row)), 1.0, 0.0)
    return jnp.dot(value, hit, precision=lax.Precision.HIGHEST, preferred_element_type=F32)


def place_z(z):
    return lambda r: jnp.where(r < NZ, 4 * r + z, -1)


def place_y(y):
    return lambda r: jnp.where(r < NY, (r >> 2) * 16 + 4 * y + (r & 3), -1)


def place_x(x):
    return lambda r: jnp.where(r < NX, (r >> 4) * 64 + 16 * x + (r & 15), -1)


def merge_z_kernel(held, above, below, out, low, high):
    width = LANES_Z
    out[...] = held[:, 0:width] + spread(above[...], place_z(CZ - 1), width) + spread(below[...], place_z(0), width)
    low[...] = jnp.zeros_like(low)
    high[...] = jnp.zeros_like(high)
    low[:, 0:NY] = out[:, BEFORE_Y : BEFORE_Y + NY]
    high[:, 0:NY] = out[:, BEFORE_Y + NY : BEFORE_Z]


def merge_y_kernel(held, above, below, out, low, high):
    width = 256
    out[...] = held[:, 0:width] + spread(above[...], place_y(CY - 1), width) + spread(below[...], place_y(0), width)
    low[...] = jnp.zeros_like(low)
    high[...] = jnp.zeros_like(high)
    low[:, 0:NX] = out[:, ATOMS : ATOMS + NX]
    high[:, 0:NX] = out[:, ATOMS + NX : BEFORE_Y]


def merge_x_kernel(held, above, below, out):
    width = ATOMS
    value = held[:, 0:width] + spread(above[...], place_x(CX - 1), width) + spread(below[...], place_x(0), width)
    out[...] = value[0:3]


def slots_of(neighbours):
    cells = CX * CY * CZ
    size_x, size_y, size_z = (lax.axis_size(axis) for axis in ("gx", "gy", "gz"))
    partner = neighbours.T
    domain = partner // ATOMS
    within = partner % ATOMS
    basis = within // cells
    remain = within % cells
    ex = domain // (size_y * size_z) * CX + remain // (CY * CZ) - lax.axis_index("gx") * CX + 1
    ey = domain // size_z % size_y * CY + remain // CZ % CY - lax.axis_index("gy") * CY + 1
    ez = domain % size_z * CZ + remain % CZ - lax.axis_index("gz") * CZ + 1
    ex = jnp.remainder(ex, CX * size_x)
    ey = jnp.remainder(ey, CY * size_y)
    ez = jnp.remainder(ez, CZ * size_z)
    x_out = (ex == 0) | (ex == CX + 1)
    y_out = (ey == 0) | (ey == CY + 1)
    z_out = (ez == 0) | (ez == CZ + 1)
    q = jnp.where(x_out, 2 * CX + 2 * (ex == CX + 1) + basis, basis * CX + ex - 1)
    r_in = q * CY + ey - 1
    r_out = 2 * (CX + 2) * CY + (ey == CY + 1) * (2 * (CX + 2)) + q
    r = jnp.where(y_out, r_out, r_in)
    slots = jnp.where(z_out, BEFORE_Z + (ez == CZ + 1) * NZ + r, r * CZ + ez - 1)
    lanes = jnp.where(z_out, LANES_Z + (ez == CZ + 1) * 128 + r, r * CZ + ez - 1)
    return slots.astype(jnp.int32), lanes.astype(jnp.int32)


def exchange(own, low, high):
    dtype = own.dtype
    rows_z = NZ_PAD if dtype == BF16 else NZ
    face = lambda rows: ((ORB, rows, VECS), dtype)
    xl, xh = shifted(high, "gx", 1), shifted(low, "gx", -1)
    low, high = call(
        faces_y_kernel, [face(NY)] * 2, [VMEM] * 3, (own, xl, xh),
        [pltpu.VMEM((BEFORE_Y, VECS), F32), pltpu.VMEM((NY, VECS), F32)],
    )
    yl, yh = shifted(high, "gy", 1), shifted(low, "gy", -1)
    low, high = call(
        faces_z_kernel, [face(rows_z)] * 2, [VMEM] * 5, (own, xl, xh, yl, yh),
        [pltpu.VMEM((4 * NZ_PAD, VECS), F32)],
    )
    zl, zh = shifted(high, "gz", 1), shifted(low, "gz", -1)
    return xl, xh, yl, yh, zl, zh


def shards(noise_vectors, hamiltonian, derivative, neighbours, coefficients):
    slots, lanes = slots_of(neighbours)
    lattice = noise_vectors.reshape(ORB, 2, CX, CY * CZ, VECS)
    low = lattice[:, :, 0].reshape(ORB, NX, VECS)
    high = lattice[:, :, CX - 1].reshape(ORB, NX, VECS)
    (rows,) = call(
        prep_kernel, [((ATOMS, 16, 256), BF16)], [VMEM], (hamiltonian.transpose(1, 2, 0, 3),),
        [pltpu.VMEM((256, ATOMS), F32), pltpu.VMEM((2, ATOMS * 16, 128), F32)],
        flops=1 << 22,
    )
    whole = ((ORB, ATOMS, VECS), F32)
    plane = ((ORB, NX, VECS), F32)
    loose = pltpu.VMEM((SLOTS * 16, VECS), F32)
    applied = pltpu.VMEM((ATOMS * 16, VECS), F32)
    split = pltpu.VMEM((SLOTS, 16, 256), BF16)
    ghosts = exchange(noise_vectors, low, high)
    first, total, low, high, noise_tiles = call(
        first_kernel, [whole, whole, plane, plane, ((SLOTS, 16, VECS), BF16)], [SMEM, SMEM] + [VMEM] * 8,
        (coefficients, slots, rows, noise_vectors) + ghosts, [loose, applied], flops=1 << 30, mib=24,
    )
    ghosts = exchange(first, low, high)
    second, total, low, high = call(
        second_kernel, [whole, whole, plane, plane], [SMEM, SMEM] + [VMEM] * 10,
        (coefficients, slots, rows, noise_vectors, total, first) + ghosts, [loose, split, applied], flops=1 << 30, mib=24,
    )
    ghosts = exchange(second, low, high)
    weighted, held = call(
        third_kernel, [whole, ((8, LANES), F32)], [SMEM, SMEM] + [VMEM] * 13,
        (coefficients, slots, lanes, rows, first, total, noise_tiles, derivative.transpose(0, 2, 3, 1, 4), second) + ghosts,
        [loose, split, applied, pltpu.VMEM((2, ATOMS * 16, 128), F32), pltpu.VMEM((256, ATOMS), F32),
         pltpu.VMEM((NEIGH * 16, ATOMS), F32)],
        flops=1 << 31, mib=32,
    )
    tile = ((8, 128), F32)
    low, high = held[:, LANES_Z : LANES_Z + 128], held[:, LANES_Z + 128 :]
    above, below = shifted(low, "gz", -1), shifted(high, "gz", 1)
    held, low, high = call(merge_z_kernel, [((8, LANES_Z), F32), tile, tile], [VMEM] * 3, (held, above, below))
    above, below = shifted(low, "gy", -1), shifted(high, "gy", 1)
    held, low, high = call(merge_y_kernel, [((8, 256), F32), tile, tile], [VMEM] * 3, (held, above, below))
    above, below = shifted(low, "gx", -1), shifted(high, "gx", 1)
    (forces,) = call(merge_x_kernel, [((3, ATOMS), F32)], [VMEM] * 3, (held, above, below))
    return weighted, forces


def solution(mesh):
    in_specs = (
        P(None, ("gx", "gy", "gz"), None),
        P(None, None, None, ("gx", "gy", "gz")),
        P(None, None, None, None, ("gx", "gy", "gz")),
        P(("gx", "gy", "gz"), None),
        P(),
    )
    out_specs = (P(None, ("gx", "gy", "gz"), None), P(None, ("gx", "gy", "gz")))
    return jax.shard_map(shards, mesh=mesh, in_specs=in_specs, out_specs=out_specs, check_vma=False)
```

```python
import functools

import jax
import jax.numpy as jnp
from jax import lax
from jax.experimental import pallas as pl
from jax.experimental.pallas import tpu as pltpu
from jax.sharding import PartitionSpec as P

CX = 4
CY = 4
CZ = 4
ORB = 9
NEIGH = 15
ATOMS = 2 * CX * CY * CZ
VECS = 128
NX = 2 * CY * CZ
NY = 2 * (CX + 2) * CZ
NZ = 2 * (CX + 2) * (CY + 2)
ROWS_X = ORB * NX + 16
ROWS_Y = ORB * NY + 16
ROWS_Z = ORB * NZ + 8
BEFORE_Y = ATOMS + 2 * NX
BEFORE_Z = BEFORE_Y + 2 * NY
SLOTS = BEFORE_Z + 2 * NZ
LANES_Z = 384
LANES = 640
F32 = jnp.float32
BF16 = jnp.bfloat16
VMEM = pl.BlockSpec(memory_space=pltpu.VMEM)
SMEM = pl.BlockSpec(memory_space=pltpu.SMEM)


def call(kernel, outs, in_specs, args, scratch=(), flops=0, mib=16):
    shapes = [jax.ShapeDtypeStruct(shape, dtype) for shape, dtype in outs]
    moved = sum(a.size * a.dtype.itemsize for a in args) + sum(s.size * s.dtype.itemsize for s in shapes)
    return pl.pallas_call(
        kernel,
        out_shape=shapes,
        in_specs=in_specs,
        out_specs=[VMEM] * len(shapes),
        scratch_shapes=list(scratch),
        compiler_params=pltpu.CompilerParams(vmem_limit_bytes=mib << 20),
        cost_estimate=pl.CostEstimate(flops=flops, bytes_accessed=moved, transcendentals=0),
    )(*args)


def swapped(value, axis, second):
    count = lax.axis_size(axis)
    pairs = [((k + second) % count, (k + 1 + second) % count) for k in range(0, count, 2)]
    return lax.ppermute(value, axis, pairs + [(b, a) for a, b in pairs])


def prep_kernel(ham, rows, turned, wide):
    turned[...] = jnp.zeros_like(turned)
    wide[...] = jnp.zeros_like(wide)
    for a in range(ORB):
        for b in range(ORB):
            turned[pl.ds(b, NEIGH, stride=16), :] = ham[a, b].astype(F32)
        flat = turned[...].T
        wide[0, pl.ds(a, ATOMS, stride=16), :] = flat[:, 0:128]
        wide[1, pl.ds(a, ATOMS, stride=16), :] = flat[:, 128:256]

    def pack(i, carry):
        at = pl.ds(pl.multiple_of(i * 16, 16), 16)
        rows[i, :, 0:128] = wide[0, at, :].astype(BF16)
        rows[i, :, 128:256] = wide[1, at, :].astype(BF16)
        return carry

    lax.fori_loop(0, ATOMS, pack, 0, unroll=8)


def scale_of(level):
    return jnp.exp2(level * 0.25) * (1.0 / 32767.0)


def packed_of(level):
    return jnp.exp2(level * -0.25) * 32767.0


def level_of(message):
    rows = message.shape[0]
    return message[rows - 16 : rows, :].astype(jnp.int32).astype(F32)[8:16]


def pack(plain, message, level):
    fixed = message.dtype == jnp.int16
    rows = message.shape[0]
    if fixed:
        factor = jnp.concatenate([packed_of(level)] * 2, axis=0)
    for t in range(0, rows, 16):
        value = plain[t : t + 16, :]
        if fixed:
            value = jnp.round(value * factor)
            if t == rows - 16:
                value = jnp.concatenate([value[0:8], level], axis=0)
            message[t : t + 16, :] = value.astype(jnp.int32).astype(jnp.int16)
        else:
            message[t : t + 16, :] = value.astype(BF16)


def unpack(message, plain):
    if message.dtype != jnp.int16:
        for t in range(0, message.shape[0], 16):
            plain[t : t + 16, :] = message[t : t + 16, :].astype(F32)
        return
    factor = jnp.concatenate([scale_of(level_of(message))] * 2, axis=0)
    for t in range(0, message.shape[0], 16):
        plain[t : t + 16, :] = message[t : t + 16, :].astype(jnp.int32).astype(F32) * factor


def highest(levels):
    return functools.reduce(jnp.maximum, levels)


def faces_y_kernel(parity, level, own, x1, x2, out1, out2, held, u1, u2, p1, p2):
    fixed = out1.dtype == jnp.int16
    unpack(x1, u1)
    unpack(x2, u2)
    even = parity[1] == 0
    p1[ROWS_Y - 16 :] = jnp.zeros((16, VECS), F32)
    p2[ROWS_Y - 16 :] = jnp.zeros((16, VECS), F32)
    for b in range(ORB):
        if fixed:
            take = [own[b, 16 * q : 16 * q + 16] for q in range(2 * CX)]
        else:
            held[...] = own[b].astype(F32)
            take = [held[16 * q : 16 * q + 16] for q in range(2 * CX)]
        take += [u[b * NX + 16 * q : b * NX + 16 * q + 16] for u in (u1, u2) for q in range(2)]
        for q, rows in enumerate(take):
            at = b * NY + 4 * q
            low, high = rows[0:4], rows[12:16]
            p1[at : at + 4] = jnp.where(even, high, low)
            p2[at : at + 4] = jnp.where(even, low, high)
    if fixed:
        level = highest([level[...], level_of(x1), level_of(x2)])
    pack(p1, out1, level)
    pack(p2, out2, level)


def faces_z_kernel(parity, level, own, x1, x2, y1, y2, out1, out2, held, u1, u2, v1, v2, p1, p2):
    fixed = out1.dtype == jnp.int16
    for message, plain in ((x1, u1), (x2, u2), (y1, v1), (y2, v2)):
        unpack(message, plain)
    even = parity[2] == 0
    p1[ROWS_Z - 8 :] = jnp.zeros((8, VECS), F32)
    p2[ROWS_Z - 8 :] = jnp.zeros((8, VECS), F32)
    ghosts = ((u1, NX), (u2, NX), (v1, NY), (v2, NY))
    for b in range(ORB):
        faces = []
        if not fixed:
            held[...] = own[b].astype(F32)
        for z in (0, CZ - 1):
            at = pl.ds(z, ATOMS // CZ, stride=CZ)
            faces.append([own[b, at, :] if fixed else held[at, :]])
            faces[-1] += [ref[pl.ds(b * rows + z, rows // CZ, stride=CZ), :] for ref, rows in ghosts]
        at = b * NZ
        for low, high in zip(*faces):
            rows = low.shape[0]
            p1[at : at + rows] = jnp.where(even, high, low)
            p2[at : at + rows] = jnp.where(even, low, high)
            at += rows
    if fixed:
        level = highest([level[...]] + [level_of(m) for m in (x1, x2, y1, y2)])
    pack(p1, out1, level)
    pack(p2, out2, level)


def load_tiles(own, ghosts, plains, loose):
    zero = jnp.zeros((8, VECS), F32)

    def clear(j, carry):
        loose[pl.ds(pl.multiple_of(j * 16 + 8, 8), 8), :] = zero
        return carry

    lax.fori_loop(0, SLOTS, clear, 0, unroll=16)
    for message, plain in zip(ghosts, plains):
        unpack(message, plain)
    counts = (NX, NX, NY, NY, NZ, NZ)
    for b in range(ORB):
        loose[pl.ds(b, ATOMS, stride=16), :] = own[b].astype(F32)
        base = ATOMS
        for plain, count in zip(plains, counts):
            loose[pl.ds(base * 16 + b, count, stride=16), :] = plain[b * count : b * count + count]
            base += count


def split_tiles(loose, tiles):
    def split(j, carry):
        value = loose[pl.ds(pl.multiple_of(j * 16, 16), 16), :]
        high = value.astype(BF16)
        tiles[j, :, 0:128] = high
        if tiles.shape[2] == 256:
            tiles[j, :, 128:256] = (value - high.astype(F32)).astype(BF16)
        return carry

    lax.fori_loop(0, SLOTS, split, 0, unroll=16)


def gather(slots, tiles, i):
    taken = [tiles[slots[m, i]] for m in range(NEIGH)]
    return jnp.concatenate(taken + taken[:1], axis=0)


def apply_atoms(slots, rows, tiles, applied):
    def atom(i, carry):
        product = jnp.dot(rows[i], gather(slots, tiles, i), preferred_element_type=F32)
        if tiles.shape[2] == 256:
            product = product[:, 0:128] + product[:, 128:256]
        applied[pl.ds(pl.multiple_of(i * 16, 16), 16), :] = product
        return carry

    lax.fori_loop(0, ATOMS, atom, 0, unroll=16)


def put_faces(parity, now, out1, out2, level, p1, p2):
    even = parity[0] == 0
    p1[ROWS_X - 16 :] = jnp.zeros((16, VECS), F32)
    p2[ROWS_X - 16 :] = jnp.zeros((16, VECS), F32)
    most = jnp.zeros((8, VECS), F32)
    for b in range(ORB):
        value = now[b]
        for row in range(0, ATOMS, 8):
            most = jnp.maximum(most, jnp.abs(value[row : row + 8]))
        for p in range(2):
            low, high = value[64 * p : 64 * p + 16], value[64 * p + 48 : 64 * p + 64]
            at = b * NX + 16 * p
            p1[at : at + 16] = jnp.where(even, high, low)
            p2[at : at + 16] = jnp.where(even, low, high)
    most = jnp.maximum(jnp.max(most, axis=0, keepdims=True), 1e-30)
    steps = jnp.ceil(jnp.log2(most) * 4.0 + 0.01)
    level[...] = jnp.broadcast_to(steps, (8, VECS))
    pack(p1, out1, level[...])
    pack(p2, out2, level[...])


def first_kernel(parity, coef, slots, rows, own, x1, x2, y1, y2, z1, z2, now, total, out1, out2, level, tiles,
                 loose, applied, p1, p2, *plains):
    load_tiles(own, (x1, x2, y1, y2, z1, z2), plains, loose)
    split_tiles(loose, tiles)
    apply_atoms(slots, rows, tiles, applied)
    for a in range(ORB):
        value = applied[pl.ds(a, ATOMS, stride=16), :]
        now[a] = value
        total[a] = coef[0] * own[a].astype(F32) + coef[1] * value
    put_faces(parity, now, out1, out2, level, p1, p2)


def second_kernel(parity, coef, slots, rows, prev, sum_in, own, x1, x2, y1, y2, z1, z2, now, total, out1, out2, level,
                  loose, tiles, applied, p1, p2, *plains):
    load_tiles(own, (x1, x2, y1, y2, z1, z2), plains, loose)
    split_tiles(loose, tiles)
    apply_atoms(slots, rows, tiles, applied)
    for a in range(ORB):
        value = 2.0 * applied[pl.ds(a, ATOMS, stride=16), :] - prev[a].astype(F32)
        now[a] = value
        total[a] = sum_in[a] + coef[2] * value
    put_faces(parity, now, out1, out2, level, p1, p2)


def third_kernel(coef, slots, lanes, rows, prev, sum_in, noise_tiles, deriv, own, x1, x2, y1, y2, z1, z2,
                 total, forces, loose, tiles, applied, dense, turned, stacked, *plains):
    load_tiles(own, (x1, x2, y1, y2, z1, z2), plains, loose)
    split_tiles(loose, tiles)
    apply_atoms(slots, rows, tiles, applied)
    for a in range(ORB):
        at = pl.ds(a, ATOMS, stride=16)
        value = sum_in[a] + coef[3] * (2.0 * applied[at, :] - prev[a])
        total[a] = value
        applied[at, :] = value

    def atom(i, carry):
        at = pl.ds(pl.multiple_of(i * 16, 16), 16)
        value = applied[at, :]
        high = value.astype(BF16)
        low = (value - high.astype(F32)).astype(BF16)
        product = lax.dot_general(
            jnp.concatenate([high, low], axis=0),
            gather(slots, noise_tiles, i),
            (((1,), (1,)), ((), ())),
            preferred_element_type=F32,
        )
        product = product[0:16] + product[16:32]
        dense[0, at, :] = product[:, 0:128]
        dense[1, at, :] = product[:, 128:256]
        return carry

    lax.fori_loop(0, ATOMS, atom, 0, unroll=16)
    pair = [jnp.zeros((NEIGH, ATOMS), F32) for _ in range(3)]
    for a in range(ORB):
        at = pl.ds(a, ATOMS, stride=16)
        turned[0:128] = dense[0, at, :].T
        turned[128:256] = dense[1, at, :].T
        for b in range(ORB):
            density = turned[pl.ds(b, NEIGH, stride=16), :]
            for c in range(3):
                pair[c] = pair[c] + deriv[c, a, b].astype(F32) * density
    others = lax.broadcasted_iota(jnp.int32, (NEIGH, ATOMS), 0) > 0
    stacked[...] = jnp.zeros_like(stacked)
    own_rows = []
    for c in range(3):
        value = jnp.where(others, pair[c] * (1.0 / VECS), 0.0)
        high = value.astype(BF16).astype(F32)
        stacked[pl.ds(c, NEIGH, stride=16), :] = high
        stacked[pl.ds(8 + c, NEIGH, stride=16), :] = value - high
        own_rows.append(jnp.sum(value, axis=0, keepdims=True))
    lane = lax.broadcasted_iota(jnp.int32, (LANES, ATOMS), 0)
    summed = jnp.zeros((16, LANES), F32)
    for m in range(1, NEIGH):
        hit = jnp.where(lane == lanes[m : m + 1, :], 1.0, 0.0).astype(BF16)
        summed = summed + lax.dot_general(
            stacked[16 * m : 16 * m + 16].astype(BF16), hit, (((1,), (1,)), ((), ())), preferred_element_type=F32
        )
    forces[...] = summed[0:8] + summed[8:16]
    for c in range(3):
        forces[c : c + 1, 0:ATOMS] = forces[c : c + 1, 0:ATOMS] - own_rows[c]


def spread(value, place, width):
    row = lax.broadcasted_iota(jnp.int32, (VECS, width), 0)
    lane = lax.broadcasted_iota(jnp.int32, (VECS, width), 1)
    hit = jnp.where((lane == place(row)), 1.0, 0.0)
    return jnp.dot(value, hit, precision=lax.Precision.HIGHEST, preferred_element_type=F32)


def place_z(z):
    return lambda r: jnp.where(r < NZ, 4 * r + z, -1)


def place_y(y):
    return lambda r: jnp.where(r < NY, (r >> 2) * 16 + 4 * y + (r & 3), -1)


def place_x(x):
    return lambda r: jnp.where(r < NX, (r >> 4) * 64 + 16 * x + (r & 15), -1)


def merged(held, from1, from2, place, top, parity, width):
    plane1 = jnp.where(parity == 0, top, 0)
    return held[:, 0:width] + spread(from1[...], place(plane1), width) + spread(from2[...], place(top - plane1), width)


def merge_z_kernel(parity, held, from1, from2, out, out1, out2):
    out[...] = merged(held, from1, from2, place_z, CZ - 1, parity[2], LANES_Z)
    out1[...] = jnp.zeros_like(out1)
    out2[...] = jnp.zeros_like(out2)
    out1[:, 0:NY] = out[:, BEFORE_Y : BEFORE_Y + NY]
    out2[:, 0:NY] = out[:, BEFORE_Y + NY : BEFORE_Z]


def merge_y_kernel(parity, held, from1, from2, out, out1, out2):
    out[...] = merged(held, from1, from2, place_y, CY - 1, parity[1], 256)
    out1[...] = jnp.zeros_like(out1)
    out2[...] = jnp.zeros_like(out2)
    out1[:, 0:NX] = out[:, ATOMS : ATOMS + NX]
    out2[:, 0:NX] = out[:, ATOMS + NX : BEFORE_Y]


def merge_x_kernel(parity, held, from1, from2, out):
    out[...] = merged(held, from1, from2, place_x, CX - 1, parity[0], ATOMS)[0:3]


def slots_of(neighbours, parity):
    cells = CX * CY * CZ
    size_x, size_y, size_z = (lax.axis_size(axis) for axis in ("gx", "gy", "gz"))
    partner = neighbours.T
    domain = partner // ATOMS
    within = partner % ATOMS
    basis = within // cells
    remain = within % cells
    ex = domain // (size_y * size_z) * CX + remain // (CY * CZ) - lax.axis_index("gx") * CX + 1
    ey = domain // size_z % size_y * CY + remain // CZ % CY - lax.axis_index("gy") * CY + 1
    ez = domain % size_z * CZ + remain % CZ - lax.axis_index("gz") * CZ + 1
    ex = jnp.remainder(ex, CX * size_x)
    ey = jnp.remainder(ey, CY * size_y)
    ez = jnp.remainder(ez, CZ * size_z)
    x_out = (ex == 0) | (ex == CX + 1)
    y_out = (ey == 0) | (ey == CY + 1)
    z_out = (ez == 0) | (ez == CZ + 1)
    x_trade = ((ex == 0) == (parity[0] == 0)).astype(jnp.int32)
    y_trade = ((ey == 0) == (parity[1] == 0)).astype(jnp.int32)
    z_trade = ((ez == 0) == (parity[2] == 0)).astype(jnp.int32)
    q = jnp.where(x_out, 2 * CX + 2 * x_trade + basis, basis * CX + ex - 1)
    r_in = q * CY + ey - 1
    r_out = 2 * (CX + 2) * CY + y_trade * (2 * (CX + 2)) + q
    r = jnp.where(y_out, r_out, r_in)
    slots = jnp.where(z_out, BEFORE_Z + z_trade * NZ + r, r * CZ + ez - 1)
    lanes = jnp.where(z_out, LANES_Z + z_trade * 128 + r, r * CZ + ez - 1)
    return slots.astype(jnp.int32), lanes.astype(jnp.int32)


def plain(rows):
    return pltpu.VMEM((rows, VECS), F32)


GHOST_PLAINS = [plain(r) for r in (ROWS_X, ROWS_X, ROWS_Y, ROWS_Y, ROWS_Z, ROWS_Z)]


def exchange(parity, level, own, out1, out2):
    dtype = out1.dtype
    x1, x2 = swapped(out1, "gx", 0), swapped(out2, "gx", 1)
    out1, out2 = call(
        faces_y_kernel, [((ROWS_Y, VECS), dtype)] * 2, [SMEM] + [VMEM] * 4, (parity, level, own, x1, x2),
        [plain(ATOMS), plain(ROWS_X), plain(ROWS_X), plain(ROWS_Y), plain(ROWS_Y)],
    )
    y1, y2 = swapped(out1, "gy", 0), swapped(out2, "gy", 1)
    out1, out2 = call(
        faces_z_kernel, [((ROWS_Z, VECS), dtype)] * 2, [SMEM] + [VMEM] * 6, (parity, level, own, x1, x2, y1, y2),
        [plain(ATOMS)] + GHOST_PLAINS,
    )
    z1, z2 = swapped(out1, "gz", 0), swapped(out2, "gz", 1)
    return x1, x2, y1, y2, z1, z2


def shards(noise_vectors, hamiltonian, derivative, neighbours, coefficients):
    parity = jnp.stack([lax.axis_index(axis) % 2 for axis in ("gx", "gy", "gz")]).astype(jnp.int32)
    slots, lanes = slots_of(neighbours, parity)
    lattice = noise_vectors.reshape(ORB, 2, CX, CY * CZ, VECS)
    low = lattice[:, :, 0].reshape(ORB * NX, VECS)
    high = lattice[:, :, CX - 1].reshape(ORB * NX, VECS)
    room = jnp.zeros((16, VECS), BF16)
    even = parity[0] == 0
    out1 = jnp.concatenate([jnp.where(even, high, low), room])
    out2 = jnp.concatenate([jnp.where(even, low, high), room])
    (rows,) = call(
        prep_kernel, [((ATOMS, 16, 256), BF16)], [VMEM], (hamiltonian.transpose(1, 2, 0, 3),),
        [plain(256), pltpu.VMEM((2, ATOMS * 16, 128), F32)], flops=1 << 22,
    )
    whole = ((ORB, ATOMS, VECS), F32)
    plane = ((ROWS_X, VECS), jnp.int16)
    tile = ((8, 128), F32)
    loose = plain(SLOTS * 16)
    applied = plain(ATOMS * 16)
    split = pltpu.VMEM((SLOTS, 16, 256), BF16)
    ghosts = exchange(parity, jnp.zeros((8, VECS), F32), noise_vectors, out1, out2)
    first, total, out1, out2, level, noise_tiles = call(
        first_kernel, [whole, whole, plane, plane, tile, ((SLOTS, 16, VECS), BF16)], [SMEM] * 3 + [VMEM] * 8,
        (parity, coefficients, slots, rows, noise_vectors) + ghosts,
        [loose, applied, plain(ROWS_X), plain(ROWS_X)] + GHOST_PLAINS, flops=1 << 30, mib=24,
    )
    ghosts = exchange(parity, level, first, out1, out2)
    second, total, out1, out2, level = call(
        second_kernel, [whole, whole, plane, plane, tile], [SMEM] * 3 + [VMEM] * 10,
        (parity, coefficients, slots, rows, noise_vectors, total, first) + ghosts,
        [loose, split, applied, plain(ROWS_X), plain(ROWS_X)] + GHOST_PLAINS, flops=1 << 30, mib=24,
    )
    ghosts = exchange(parity, level, second, out1, out2)
    weighted, held = call(
        third_kernel, [whole, ((8, LANES), F32)], [SMEM] * 2 + [VMEM] * 13,
        (coefficients, slots, lanes, rows, first, total, noise_tiles, derivative.transpose(0, 2, 3, 1, 4), second) + ghosts,
        [loose, split, applied, pltpu.VMEM((2, ATOMS * 16, 128), F32), plain(256), plain(NEIGH * 16)] + GHOST_PLAINS,
        flops=1 << 31, mib=32,
    )
    out1, out2 = held[:, LANES_Z : LANES_Z + 128], held[:, LANES_Z + 128 :]
    from1, from2 = swapped(out1, "gz", 0), swapped(out2, "gz", 1)
    held, out1, out2 = call(
        merge_z_kernel, [((8, LANES_Z), F32), tile, tile], [SMEM] + [VMEM] * 3, (parity, held, from1, from2)
    )
    from1, from2 = swapped(out1, "gy", 0), swapped(out2, "gy", 1)
    held, out1, out2 = call(
        merge_y_kernel, [((8, 256), F32), tile, tile], [SMEM] + [VMEM] * 3, (parity, held, from1, from2)
    )
    from1, from2 = swapped(out1, "gx", 0), swapped(out2, "gx", 1)
    (forces,) = call(merge_x_kernel, [((3, ATOMS), F32)], [SMEM] + [VMEM] * 3, (parity, held, from1, from2))
    return weighted, forces


def solution(mesh):
    in_specs = (
        P(None, ("gx", "gy", "gz"), None),
        P(None, None, None, ("gx", "gy", "gz")),
        P(None, None, None, None, ("gx", "gy", "gz")),
        P(("gx", "gy", "gz"), None),
        P(),
    )
    out_specs = (P(None, ("gx", "gy", "gz"), None), P(None, ("gx", "gy", "gz")))
    return jax.shard_map(shards, mesh=mesh, in_specs=in_specs, out_specs=out_specs, check_vma=False)
```

```python
import functools

import jax
import jax.numpy as jnp
from jax import lax
from jax.experimental import pallas as pl
from jax.experimental.pallas import tpu as pltpu
from jax.sharding import PartitionSpec as P

CX = 4
CY = 4
CZ = 4
ORB = 9
NEIGH = 15
ATOMS = 2 * CX * CY * CZ
VECS = 128
NX = 2 * CY * CZ
NY = 2 * (CX + 2) * CZ
NZ = 2 * (CX + 2) * (CY + 2)
ROWS_X = ORB * NX + 16
ROWS_Y = ORB * NY + 16
ROWS_Z = ORB * NZ + 8
BEFORE_Y = ATOMS + 2 * NX
BEFORE_Z = BEFORE_Y + 2 * NY
SLOTS = BEFORE_Z + 2 * NZ
LANES_Z = 384
LANES = 640
F32 = jnp.float32
BF16 = jnp.bfloat16
VMEM = pl.BlockSpec(memory_space=pltpu.VMEM)
SMEM = pl.BlockSpec(memory_space=pltpu.SMEM)


def call(kernel, outs, in_specs, args, scratch=(), flops=0, mib=16):
    shapes = [jax.ShapeDtypeStruct(shape, dtype) for shape, dtype in outs]
    moved = sum(a.size * a.dtype.itemsize for a in args) + sum(s.size * s.dtype.itemsize for s in shapes)
    return pl.pallas_call(
        kernel,
        out_shape=shapes,
        in_specs=in_specs,
        out_specs=[VMEM] * len(shapes),
        scratch_shapes=list(scratch),
        compiler_params=pltpu.CompilerParams(vmem_limit_bytes=mib << 20),
        cost_estimate=pl.CostEstimate(flops=flops, bytes_accessed=moved, transcendentals=0),
    )(*args)


def swapped(value, axis, second):
    count = lax.axis_size(axis)
    pairs = [((k + second) % count, (k + 1 + second) % count) for k in range(0, count, 2)]
    return lax.ppermute(value, axis, pairs + [(b, a) for a, b in pairs])


def prep_kernel(ham, rows, turned, wide):
    turned[...] = jnp.zeros_like(turned)
    wide[...] = jnp.zeros_like(wide)
    for a in range(ORB):
        for b in range(ORB):
            turned[pl.ds(b, NEIGH, stride=16), :] = ham[a, b].astype(F32)
        flat = turned[...].T
        wide[0, pl.ds(a, ATOMS, stride=16), :] = flat[:, 0:128]
        wide[1, pl.ds(a, ATOMS, stride=16), :] = flat[:, 128:256]

    def pack(i, carry):
        at = pl.ds(pl.multiple_of(i * 16, 16), 16)
        rows[i, :, 0:128] = wide[0, at, :].astype(BF16)
        rows[i, :, 128:256] = wide[1, at, :].astype(BF16)
        return carry

    lax.fori_loop(0, ATOMS, pack, 0, unroll=8)


def scale_of(level):
    return jnp.exp2(level * 0.25) * (1.0 / 32767.0)


def packed_of(level):
    return jnp.exp2(level * -0.25) * 32767.0


def level_of(message):
    rows = message.shape[0]
    return message[rows - 16 : rows, :].astype(jnp.int32).astype(F32)[8:16]


def pack(plain, message, level):
    fixed = message.dtype == jnp.int16
    rows = message.shape[0]
    if fixed:
        factor = jnp.concatenate([packed_of(level)] * 2, axis=0)
    for t in range(0, rows, 16):
        value = plain[t : t + 16, :]
        if fixed:
            value = jnp.round(value * factor)
            if t == rows - 16:
                value = jnp.concatenate([value[0:8], level], axis=0)
            message[t : t + 16, :] = value.astype(jnp.int32).astype(jnp.int16)
        else:
            message[t : t + 16, :] = value.astype(BF16)


def unpack(message, plain):
    if message.dtype != jnp.int16:
        for t in range(0, message.shape[0], 16):
            plain[t : t + 16, :] = message[t : t + 16, :].astype(F32)
        return
    factor = jnp.concatenate([scale_of(level_of(message))] * 2, axis=0)
    for t in range(0, message.shape[0], 16):
        plain[t : t + 16, :] = message[t : t + 16, :].astype(jnp.int32).astype(F32) * factor


def highest(levels):
    return functools.reduce(jnp.maximum, levels)


def faces_y_kernel(trade, parity, level, own, x1, x2, out, held, u1, u2, picked):
    fixed = out.dtype == jnp.int16
    unpack(x1, u1)
    unpack(x2, u2)
    upper = parity[1] == trade
    picked[ROWS_Y - 16 :] = jnp.zeros((16, VECS), F32)
    for b in range(ORB):
        if fixed:
            take = [own[b, 16 * q : 16 * q + 16] for q in range(2 * CX)]
        else:
            held[...] = own[b].astype(F32)
            take = [held[16 * q : 16 * q + 16] for q in range(2 * CX)]
        take += [u[b * NX + 16 * q : b * NX + 16 * q + 16] for u in (u1, u2) for q in range(2)]
        for q, rows in enumerate(take):
            picked[b * NY + 4 * q : b * NY + 4 * q + 4] = jnp.where(upper, rows[12:16], rows[0:4])
    if fixed:
        level = highest([level[...], level_of(x1), level_of(x2)])
    pack(picked, out, level)


def faces_z_kernel(parity, level, own, x1, x2, y1, y2, out1, out2, held, u1, u2, v1, v2, p1, p2):
    fixed = out1.dtype == jnp.int16
    for message, plain in ((x1, u1), (x2, u2), (y1, v1), (y2, v2)):
        unpack(message, plain)
    even = parity[2] == 0
    p1[ROWS_Z - 8 :] = jnp.zeros((8, VECS), F32)
    p2[ROWS_Z - 8 :] = jnp.zeros((8, VECS), F32)
    ghosts = ((u1, NX), (u2, NX), (v1, NY), (v2, NY))
    for b in range(ORB):
        faces = []
        if not fixed:
            held[...] = own[b].astype(F32)
        for z in (0, CZ - 1):
            at = pl.ds(z, ATOMS // CZ, stride=CZ)
            faces.append([own[b, at, :] if fixed else held[at, :]])
            faces[-1] += [ref[pl.ds(b * rows + z, rows // CZ, stride=CZ), :] for ref, rows in ghosts]
        at = b * NZ
        for low, high in zip(*faces):
            rows = low.shape[0]
            p1[at : at + rows] = jnp.where(even, high, low)
            p2[at : at + rows] = jnp.where(even, low, high)
            at += rows
    if fixed:
        level = highest([level[...]] + [level_of(m) for m in (x1, x2, y1, y2)])
    pack(p1, out1, level)
    pack(p2, out2, level)


def loop(count, body, unroll):
    def step(k, carry):
        body(k)
        return carry

    lax.fori_loop(0, count, step, 0, unroll=unroll)


def aligned(row, count=16):
    return pl.ds(pl.multiple_of(row, count), count)


def make_tiles(pieces, loose, tiles, base):
    slots = sum(count for _, count in pieces)
    zero = jnp.zeros((8, VECS), F32)

    def clear(j):
        loose[aligned(j * 16 + 8, 8), :] = zero

    loop(slots, clear, 16)
    for b in range(ORB):
        at = 0
        for rows_of, count in pieces:
            loose[pl.ds(at * 16 + b, count, stride=16), :] = rows_of(b)
            at += count

    def split(j):
        value = loose[aligned(j * 16), :]
        high = value.astype(BF16)
        tiles[base + j, :, 0:128] = high
        if tiles.shape[2] == 256:
            tiles[base + j, :, 128:256] = (value - high.astype(F32)).astype(BF16)

    loop(slots, split, 16)


def front_tiles(own, messages, plains, loose, tiles):
    pieces = [(lambda b: own[b].astype(F32), ATOMS)]
    for message, plain, count in zip(messages, plains, (NX, NX, NY, NY)):
        unpack(message, plain)
        pieces.append((lambda b, plain=plain, count=count: plain[b * count : b * count + count], count))
    make_tiles(pieces, loose, tiles, 0)


def back_tiles(front, messages, plains, loose, tiles):
    def copy(j):
        tiles[j] = front[j]

    loop(BEFORE_Z, copy, 16)
    pieces = []
    for message, plain in zip(messages, plains):
        unpack(message, plain)
        pieces.append((lambda b, plain=plain: plain[b * NZ : b * NZ + NZ], NZ))
    make_tiles(pieces, loose, tiles, BEFORE_Z)


def middle(k):
    return 4 * (k >> 1) + 1 + (k & 1)


def outer(k):
    return 4 * (k >> 1) + 3 * (k & 1)


def gather(slots, tiles, i):
    taken = [tiles[slots[m, i]] for m in range(NEIGH)]
    return jnp.concatenate(taken + taken[:1], axis=0)


def apply_atoms(slots, rows, tiles, applied, which, place):
    def atom(k):
        i = which(k)
        product = jnp.dot(rows[i], gather(slots, tiles, i), preferred_element_type=F32)
        if tiles.shape[2] == 256:
            product = product[:, 0:128] + product[:, 128:256]
        applied[aligned(place(k) * 16), :] = product

    loop(ATOMS // 2, atom, 16)


def densities(slots, noise_tiles, values, dense, which, place):
    def atom(k):
        i = which(k)
        value = values[aligned(i * 16), :]
        high = value.astype(BF16)
        low = (value - high.astype(F32)).astype(BF16)
        product = lax.dot_general(
            jnp.concatenate([high, low], axis=0),
            gather(slots, noise_tiles, i),
            (((1,), (1,)), ((), ())),
            preferred_element_type=F32,
        )
        product = product[0:16] + product[16:32]
        dense[0, aligned(place(k) * 16), :] = product[:, 0:128]
        dense[1, aligned(place(k) * 16), :] = product[:, 128:256]

    loop(ATOMS // 2, atom, 16)


def spread_middle(half, applied):
    def put(k):
        applied[aligned(middle(k) * 16), :] = half[aligned(k * 16), :]

    loop(ATOMS // 2, put, 16)


def front_kernel(slots, rows, own, x1, x2, y1, y2, front, half, loose, *plains):
    front_tiles(own, (x1, x2, y1, y2), plains, loose, front)
    apply_atoms(slots, rows, front, half, middle, lambda k: k)


def front_third_kernel(coef, slots, rows, prev, sum_in, noise_tiles, own, x1, x2, y1, y2, front, half, dense,
                       loose, applied, *plains):
    front_tiles(own, (x1, x2, y1, y2), plains, loose, front)
    apply_atoms(slots, rows, front, half, middle, lambda k: k)
    applied[...] = jnp.zeros_like(applied)
    spread_middle(half, applied)
    for a in range(ORB):
        at = pl.ds(a, ATOMS, stride=16)
        applied[at, :] = sum_in[a] + coef[3] * (2.0 * applied[at, :] - prev[a])
    densities(slots, noise_tiles, applied, dense, middle, lambda k: k)


def put_faces(parity, now, out1, out2, level, p1, p2):
    even = parity[0] == 0
    p1[ROWS_X - 16 :] = jnp.zeros((16, VECS), F32)
    p2[ROWS_X - 16 :] = jnp.zeros((16, VECS), F32)
    most = jnp.zeros((8, VECS), F32)
    for b in range(ORB):
        value = now[b]
        for row in range(0, ATOMS, 8):
            most = jnp.maximum(most, jnp.abs(value[row : row + 8]))
        for p in range(2):
            low, high = value[64 * p : 64 * p + 16], value[64 * p + 48 : 64 * p + 64]
            at = b * NX + 16 * p
            p1[at : at + 16] = jnp.where(even, high, low)
            p2[at : at + 16] = jnp.where(even, low, high)
    most = jnp.maximum(jnp.max(most, axis=0, keepdims=True), 1e-30)
    steps = jnp.ceil(jnp.log2(most) * 4.0 + 0.01)
    level[...] = jnp.broadcast_to(steps, (8, VECS))
    pack(p1, out1, level[...])
    pack(p2, out2, level[...])


def rest(slots, rows, front, half, messages, plains, loose, tiles, applied):
    back_tiles(front, messages, plains, loose, tiles)
    apply_atoms(slots, rows, tiles, applied, outer, outer)
    spread_middle(half, applied)


def first_kernel(parity, coef, slots, rows, own, front, half, z1, z2, now, total, out1, out2, level, tiles,
                 loose, applied, p1, p2, *plains):
    rest(slots, rows, front, half, (z1, z2), plains, loose, tiles, applied)
    for a in range(ORB):
        value = applied[pl.ds(a, ATOMS, stride=16), :]
        now[a] = value
        total[a] = coef[0] * own[a].astype(F32) + coef[1] * value
    put_faces(parity, now, out1, out2, level, p1, p2)


def second_kernel(parity, coef, slots, rows, prev, sum_in, front, half, z1, z2, now, total, out1, out2, level,
                  tiles, loose, applied, p1, p2, *plains):
    rest(slots, rows, front, half, (z1, z2), plains, loose, tiles, applied)
    for a in range(ORB):
        value = 2.0 * applied[pl.ds(a, ATOMS, stride=16), :] - prev[a].astype(F32)
        now[a] = value
        total[a] = sum_in[a] + coef[2] * value
    put_faces(parity, now, out1, out2, level, p1, p2)


def third_kernel(coef, slots, lanes, rows, prev, sum_in, noise_tiles, deriv, front, half, dense_half, z1, z2,
                 total, forces, tiles, loose, applied, dense, turned, stacked, *plains):
    rest(slots, rows, front, half, (z1, z2), plains, loose, tiles, applied)
    for a in range(ORB):
        at = pl.ds(a, ATOMS, stride=16)
        value = sum_in[a] + coef[3] * (2.0 * applied[at, :] - prev[a])
        total[a] = value
        applied[at, :] = value
    densities(slots, noise_tiles, applied, dense, outer, outer)
    for side in range(2):
        spread_middle(dense_half.at[side], dense.at[side])
    pair = [jnp.zeros((NEIGH, ATOMS), F32) for _ in range(3)]
    for a in range(ORB):
        at = pl.ds(a, ATOMS, stride=16)
        turned[0:128] = dense[0, at, :].T
        turned[128:256] = dense[1, at, :].T
        for b in range(ORB):
            density = turned[pl.ds(b, NEIGH, stride=16), :]
            for c in range(3):
                pair[c] = pair[c] + deriv[c, a, b].astype(F32) * density
    others = lax.broadcasted_iota(jnp.int32, (NEIGH, ATOMS), 0) > 0
    stacked[...] = jnp.zeros_like(stacked)
    own_rows = []
    for c in range(3):
        value = jnp.where(others, pair[c] * (1.0 / VECS), 0.0)
        high = value.astype(BF16).astype(F32)
        stacked[pl.ds(c, NEIGH, stride=16), :] = high
        stacked[pl.ds(8 + c, NEIGH, stride=16), :] = value - high
        own_rows.append(jnp.sum(value, axis=0, keepdims=True))
    lane = lax.broadcasted_iota(jnp.int32, (LANES, ATOMS), 0)
    summed = jnp.zeros((16, LANES), F32)
    for m in range(1, NEIGH):
        hit = jnp.where(lane == lanes[m : m + 1, :], 1.0, 0.0).astype(BF16)
        summed = summed + lax.dot_general(
            stacked[16 * m : 16 * m + 16].astype(BF16), hit, (((1,), (1,)), ((), ())), preferred_element_type=F32
        )
    forces[...] = summed[0:8] + summed[8:16]
    for c in range(3):
        forces[c : c + 1, 0:ATOMS] = forces[c : c + 1, 0:ATOMS] - own_rows[c]


def spread(value, place, width):
    row = lax.broadcasted_iota(jnp.int32, (VECS, width), 0)
    lane = lax.broadcasted_iota(jnp.int32, (VECS, width), 1)
    hit = jnp.where((lane == place(row)), 1.0, 0.0)
    return jnp.dot(value, hit, precision=lax.Precision.HIGHEST, preferred_element_type=F32)


def place_z(z):
    return lambda r: jnp.where(r < NZ, 4 * r + z, -1)


def place_y(y):
    return lambda r: jnp.where(r < NY, (r >> 2) * 16 + 4 * y + (r & 3), -1)


def place_x(x):
    return lambda r: jnp.where(r < NX, (r >> 4) * 64 + 16 * x + (r & 15), -1)


def merged(held, from1, from2, place, top, parity, width):
    plane1 = jnp.where(parity == 0, top, 0)
    return held[:, 0:width] + spread(from1[...], place(plane1), width) + spread(from2[...], place(top - plane1), width)


def merge_z_kernel(parity, held, from1, from2, out, out1, out2):
    out[...] = merged(held, from1, from2, place_z, CZ - 1, parity[2], LANES_Z)
    out1[...] = jnp.zeros_like(out1)
    out2[...] = jnp.zeros_like(out2)
    out1[:, 0:NY] = out[:, BEFORE_Y : BEFORE_Y + NY]
    out2[:, 0:NY] = out[:, BEFORE_Y + NY : BEFORE_Z]


def merge_y_kernel(parity, held, from1, from2, out, out1, out2):
    out[...] = merged(held, from1, from2, place_y, CY - 1, parity[1], 256)
    out1[...] = jnp.zeros_like(out1)
    out2[...] = jnp.zeros_like(out2)
    out1[:, 0:NX] = out[:, ATOMS : ATOMS + NX]
    out2[:, 0:NX] = out[:, ATOMS + NX : BEFORE_Y]


def merge_x_kernel(parity, held, from1, from2, out):
    out[...] = merged(held, from1, from2, place_x, CX - 1, parity[0], ATOMS)[0:3]


def slots_of(neighbours, parity):
    cells = CX * CY * CZ
    size_x, size_y, size_z = (lax.axis_size(axis) for axis in ("gx", "gy", "gz"))
    partner = neighbours.T
    domain = partner // ATOMS
    within = partner % ATOMS
    basis = within // cells
    remain = within % cells
    ex = domain // (size_y * size_z) * CX + remain // (CY * CZ) - lax.axis_index("gx") * CX + 1
    ey = domain // size_z % size_y * CY + remain // CZ % CY - lax.axis_index("gy") * CY + 1
    ez = domain % size_z * CZ + remain % CZ - lax.axis_index("gz") * CZ + 1
    ex = jnp.remainder(ex, CX * size_x)
    ey = jnp.remainder(ey, CY * size_y)
    ez = jnp.remainder(ez, CZ * size_z)
    x_out = (ex == 0) | (ex == CX + 1)
    y_out = (ey == 0) | (ey == CY + 1)
    z_out = (ez == 0) | (ez == CZ + 1)
    x_trade = ((ex == 0) == (parity[0] == 0)).astype(jnp.int32)
    y_trade = ((ey == 0) == (parity[1] == 0)).astype(jnp.int32)
    z_trade = ((ez == 0) == (parity[2] == 0)).astype(jnp.int32)
    q = jnp.where(x_out, 2 * CX + 2 * x_trade + basis, basis * CX + ex - 1)
    r_in = q * CY + ey - 1
    r_out = 2 * (CX + 2) * CY + y_trade * (2 * (CX + 2)) + q
    r = jnp.where(y_out, r_out, r_in)
    slots = jnp.where(z_out, BEFORE_Z + z_trade * NZ + r, r * CZ + ez - 1)
    lanes = jnp.where(z_out, LANES_Z + z_trade * 128 + r, r * CZ + ez - 1)
    return slots.astype(jnp.int32), lanes.astype(jnp.int32)


def plain(rows):
    return pltpu.VMEM((rows, VECS), F32)


FRONT_PLAINS = [plain(r) for r in (ROWS_X, ROWS_X, ROWS_Y, ROWS_Y)]
BACK_PLAINS = [plain(ROWS_Z), plain(ROWS_Z)]


def exchange(parity, level, own, out1, out2, work):
    dtype = out1.dtype
    x2, x1 = swapped(out2, "gx", 1), swapped(out1, "gx", 0)
    outs = []
    for trade in (1, 0):
        (out,) = call(
            functools.partial(faces_y_kernel, trade), [((ROWS_Y, VECS), dtype)], [SMEM] + [VMEM] * 4,
            (parity, level, own, x1, x2), [plain(ATOMS), plain(ROWS_X), plain(ROWS_X), plain(ROWS_Y)],
        )
        outs.append(swapped(out, "gy", trade))
    y2, y1 = outs
    out1, out2 = call(
        faces_z_kernel, [((ROWS_Z, VECS), dtype)] * 2, [SMEM] + [VMEM] * 6, (parity, level, own, x1, x2, y1, y2),
        [plain(ATOMS)] + FRONT_PLAINS + BACK_PLAINS,
    )
    z1, z2 = swapped(out1, "gz", 0), swapped(out2, "gz", 1)
    return work(own, x1, x2, y1, y2), (z1, z2)


def shards(noise_vectors, hamiltonian, derivative, neighbours, coefficients):
    parity = jnp.stack([lax.axis_index(axis) % 2 for axis in ("gx", "gy", "gz")]).astype(jnp.int32)
    slots, lanes = slots_of(neighbours, parity)
    lattice = noise_vectors.reshape(ORB, 2, CX, CY * CZ, VECS)
    low = lattice[:, :, 0].reshape(ORB * NX, VECS)
    high = lattice[:, :, CX - 1].reshape(ORB * NX, VECS)
    room = jnp.zeros((16, VECS), BF16)
    even = parity[0] == 0
    out1 = jnp.concatenate([jnp.where(even, high, low), room])
    out2 = jnp.concatenate([jnp.where(even, low, high), room])
    (rows,) = call(
        prep_kernel, [((ATOMS, 16, 256), BF16)], [VMEM], (hamiltonian.transpose(1, 2, 0, 3),),
        [plain(256), pltpu.VMEM((2, ATOMS * 16, 128), F32)], flops=1 << 22,
    )
    whole = ((ORB, ATOMS, VECS), F32)
    plane = ((ROWS_X, VECS), jnp.int16)
    tile = ((8, 128), F32)
    half = ((ATOMS // 2 * 16, VECS), F32)
    front_loose, loose, applied = plain(BEFORE_Z * 16), plain((SLOTS - BEFORE_Z) * 16), plain(ATOMS * 16)
    faces = [plain(ROWS_X), plain(ROWS_X)]

    def work(*vectors):
        width = 128 if vectors[0].dtype == BF16 else 256
        return call(
            front_kernel, [((BEFORE_Z, 16, width), BF16), half], [SMEM] + [VMEM] * 6, (slots, rows) + vectors,
            [front_loose] + FRONT_PLAINS, flops=1 << 29,
        )

    fronts, ghosts = exchange(parity, jnp.zeros((8, VECS), F32), noise_vectors, out1, out2, work)
    first, total, out1, out2, level, noise_tiles = call(
        first_kernel, [whole, whole, plane, plane, tile, ((SLOTS, 16, VECS), BF16)], [SMEM] * 3 + [VMEM] * 6,
        (parity, coefficients, slots, rows, noise_vectors, *fronts, *ghosts),
        [loose, applied] + faces + BACK_PLAINS, flops=1 << 29, mib=24,
    )
    fronts, ghosts = exchange(parity, level, first, out1, out2, work)
    second, total, out1, out2, level = call(
        second_kernel, [whole, whole, plane, plane, tile], [SMEM] * 3 + [VMEM] * 7,
        (parity, coefficients, slots, rows, noise_vectors, total, *fronts, *ghosts),
        [pltpu.VMEM((SLOTS, 16, 256), BF16), loose, applied] + faces + BACK_PLAINS, flops=1 << 29, mib=24,
    )

    def last_work(*vectors):
        return call(
            front_third_kernel, [((BEFORE_Z, 16, 256), BF16), half, ((2,) + half[0], F32)], [SMEM] * 2 + [VMEM] * 9,
            (coefficients, slots, rows, first, total, noise_tiles) + vectors,
            [front_loose, applied] + FRONT_PLAINS, flops=1 << 30, mib=24,
        )

    fronts, ghosts = exchange(parity, level, second, out1, out2, last_work)
    weighted, held = call(
        third_kernel, [whole, ((8, LANES), F32)], [SMEM] * 2 + [VMEM] * 11,
        (coefficients, slots, lanes, rows, first, total, noise_tiles, derivative.transpose(0, 2, 3, 1, 4), *fronts, *ghosts),
        [pltpu.VMEM((SLOTS, 16, 256), BF16), loose, applied, pltpu.VMEM((2, ATOMS * 16, 128), F32), plain(256),
         plain(NEIGH * 16)] + BACK_PLAINS,
        flops=1 << 30, mib=32,
    )
    out1, out2 = held[:, LANES_Z : LANES_Z + 128], held[:, LANES_Z + 128 :]
    from1, from2 = swapped(out1, "gz", 0), swapped(out2, "gz", 1)
    held, out1, out2 = call(
        merge_z_kernel, [((8, LANES_Z), F32), tile, tile], [SMEM] + [VMEM] * 3, (parity, held, from1, from2)
    )
    from1, from2 = swapped(out1, "gy", 0), swapped(out2, "gy", 1)
    held, out1, out2 = call(
        merge_y_kernel, [((8, 256), F32), tile, tile], [SMEM] + [VMEM] * 3, (parity, held, from1, from2)
    )
    from1, from2 = swapped(out1, "gx", 0), swapped(out2, "gx", 1)
    (forces,) = call(merge_x_kernel, [((3, ATOMS), F32)], [SMEM] + [VMEM] * 3, (parity, held, from1, from2))
    return weighted, forces


def solution(mesh):
    in_specs = (
        P(None, ("gx", "gy", "gz"), None),
        P(None, None, None, ("gx", "gy", "gz")),
        P(None, None, None, None, ("gx", "gy", "gz")),
        P(("gx", "gy", "gz"), None),
        P(),
    )
    out_specs = (P(None, ("gx", "gy", "gz"), None), P(None, ("gx", "gy", "gz")))
    return jax.shard_map(shards, mesh=mesh, in_specs=in_specs, out_specs=out_specs, check_vma=False)
```

```python
import functools

import jax
import jax.numpy as jnp
from jax import lax
from jax.experimental import pallas as pl
from jax.experimental.pallas import tpu as pltpu
from jax.sharding import PartitionSpec as P

CX = 4
CY = 4
CZ = 4
ORB = 9
NEIGH = 15
ATOMS = 2 * CX * CY * CZ
VECS = 128
NX = 2 * CY * CZ
NY = 2 * (CX + 2) * CZ
NZ = 2 * (CX + 2) * (CY + 2)
BEFORE_Y = ATOMS + 2 * NX
BEFORE_Z = BEFORE_Y + 2 * NY
SLOTS = BEFORE_Z + 2 * NZ
ROWS_X = ORB * NX + 16
ROWS_Y = ORB * NY + 16
ROWS_Z = ORB * NZ + 8
SECOND = ATOMS
FIRST = SECOND + 8 * 32
LANES = FIRST + 8 * 64
AXES = ("gx", "gy", "gz")
F32 = jnp.float32
BF16 = jnp.bfloat16
VMEM = pl.BlockSpec(memory_space=pltpu.VMEM)
SMEM = pl.BlockSpec(memory_space=pltpu.SMEM)


def call(kernel, outs, in_specs, args, scratch=(), flops=0, mib=16):
    shapes = [jax.ShapeDtypeStruct(shape, dtype) for shape, dtype in outs]
    moved = sum(a.size * a.dtype.itemsize for a in args) + sum(s.size * s.dtype.itemsize for s in shapes)
    return pl.pallas_call(
        kernel,
        out_shape=shapes,
        in_specs=in_specs,
        out_specs=[VMEM] * len(shapes),
        scratch_shapes=list(scratch),
        compiler_params=pltpu.CompilerParams(vmem_limit_bytes=mib << 20),
        cost_estimate=pl.CostEstimate(flops=flops, bytes_accessed=moved, transcendentals=0),
    )(*args)


def swapped(value, axis, second):
    count = lax.axis_size(axis)
    pairs = [((k + second) % count, (k + 1 + second) % count) for k in range(0, count, 2)]
    return lax.ppermute(value, axis, pairs + [(b, a) for a, b in pairs])


def prep_kernel(ham, rows, turned, wide):
    turned[...] = jnp.zeros_like(turned)
    wide[...] = jnp.zeros_like(wide)
    for a in range(ORB):
        for b in range(ORB):
            turned[pl.ds(b, NEIGH, stride=16), :] = ham[a, b].astype(F32)
        flat = turned[...].T
        wide[0, pl.ds(a, ATOMS, stride=16), :] = flat[:, 0:128]
        wide[1, pl.ds(a, ATOMS, stride=16), :] = flat[:, 128:256]

    def pack(i, carry):
        at = pl.ds(pl.multiple_of(i * 16, 16), 16)
        rows[i, :, 0:128] = wide[0, at, :].astype(BF16)
        rows[i, :, 128:256] = wide[1, at, :].astype(BF16)
        return carry

    lax.fori_loop(0, ATOMS, pack, 0, unroll=8)


def scale_of(level):
    return jnp.exp2(level * 0.25) * (1.0 / 32767.0)


def packed_of(level):
    return jnp.exp2(level * -0.25) * 32767.0


def level_of(message):
    rows = message.shape[0]
    return message[rows - 16 : rows, :].astype(jnp.int32).astype(F32)[8:16]


def pack(plain, message, level):
    fixed = message.dtype == jnp.int16
    rows = message.shape[0]
    if fixed:
        factor = jnp.concatenate([packed_of(level)] * 2, axis=0)
    for t in range(0, rows, 16):
        value = plain[t : t + 16, :]
        if fixed:
            value = jnp.round(value * factor)
            if t == rows - 16:
                value = jnp.concatenate([value[0:8], level], axis=0)
            message[t : t + 16, :] = value.astype(jnp.int32).astype(jnp.int16)
        else:
            message[t : t + 16, :] = value.astype(BF16)


def unpack(message, plain):
    if message.dtype != jnp.int16:
        for t in range(0, message.shape[0], 16):
            plain[t : t + 16, :] = message[t : t + 16, :].astype(F32)
        return
    factor = jnp.concatenate([scale_of(level_of(message))] * 2, axis=0)
    for t in range(0, message.shape[0], 16):
        plain[t : t + 16, :] = message[t : t + 16, :].astype(jnp.int32).astype(F32) * factor


def highest(levels):
    return functools.reduce(jnp.maximum, levels)


def pick_y(upper, own, u1, u2, held, picked):
    picked[ROWS_Y - 16 :] = jnp.zeros((16, VECS), F32)
    for b in range(ORB):
        if own.dtype == F32:
            take = [own[b, 16 * q : 16 * q + 16] for q in range(2 * CX)]
        else:
            held[...] = own[b].astype(F32)
            take = [held[16 * q : 16 * q + 16] for q in range(2 * CX)]
        take += [u[b * NX + 16 * q : b * NX + 16 * q + 16] for u in (u1, u2) for q in range(2)]
        for q, rows in enumerate(take):
            picked[b * NY + 4 * q : b * NY + 4 * q + 4] = jnp.where(upper, rows[12:16], rows[0:4])


def second_y_kernel(parity, x2, x1, level, own, out, u1, u2, tall, held, picked):
    unpack(x1, u1)
    unpack(x2, u2)
    tall[...] = level[...]
    if out.dtype == jnp.int16:
        tall[...] = highest([level[...], level_of(x1), level_of(x2)])
    pick_y(parity[1] == 1, own, u1, u2, held, picked)
    pack(picked, out, tall[...])


def first_y_kernel(parity, tall, own, u1, u2, out, held, picked):
    pick_y(parity[1] == 0, own, u1, u2, held, picked)
    pack(picked, out, tall[...])


def faces_z_kernel(parity, y2, y1, level, own, u1, u2, out1, out2, v1, v2, held, p1, p2):
    fixed = out1.dtype == jnp.int16
    unpack(y1, v1)
    unpack(y2, v2)
    even = parity[2] == 0
    p1[ROWS_Z - 8 :] = jnp.zeros((8, VECS), F32)
    p2[ROWS_Z - 8 :] = jnp.zeros((8, VECS), F32)
    ghosts = ((u1, NX), (u2, NX), (v1, NY), (v2, NY))
    for b in range(ORB):
        faces = []
        if not fixed:
            held[...] = own[b].astype(F32)
        for z in (0, CZ - 1):
            at = pl.ds(z, ATOMS // CZ, stride=CZ)
            faces.append([own[b, at, :] if fixed else held[at, :]])
            faces[-1] += [ref[pl.ds(b * rows + z, rows // CZ, stride=CZ), :] for ref, rows in ghosts]
        at = b * NZ
        for low, high in zip(*faces):
            rows = low.shape[0]
            p1[at : at + rows] = jnp.where(even, high, low)
            p2[at : at + rows] = jnp.where(even, low, high)
            at += rows
    level = highest([level[...], level_of(y1), level_of(y2)]) if fixed else level[...]
    pack(p1, out1, level)
    pack(p2, out2, level)


def loop(count, body, unroll):
    def step(k, carry):
        body(k)
        return carry

    lax.fori_loop(0, count, step, 0, unroll=unroll)


def aligned(row, count=16):
    return pl.ds(pl.multiple_of(row, count), count)


def make_tiles(pieces, loose, tiles, base):
    slots = sum(count for _, count in pieces)
    zero = jnp.zeros((8, VECS), F32)

    def clear(j):
        loose[aligned(j * 16 + 8, 8), :] = zero

    loop(slots, clear, 16)
    for b in range(ORB):
        at = 0
        for rows_of, count in pieces:
            loose[pl.ds(at * 16 + b, count, stride=16), :] = rows_of(b)
            at += count

    def split(j):
        value = loose[aligned(j * 16), :]
        high = value.astype(BF16)
        tiles[base + j, :, 0:128] = high
        if tiles.shape[2] == 256:
            tiles[base + j, :, 128:256] = (value - high.astype(F32)).astype(BF16)

    loop(slots, split, 16)


def front_tiles(own, plains, loose, tiles):
    pieces = [(lambda b: own[b].astype(F32), ATOMS)]
    for plain, count in zip(plains, (NX, NX, NY, NY)):
        pieces.append((lambda b, plain=plain, count=count: plain[b * count : b * count + count], count))
    make_tiles(pieces, loose, tiles, 0)


def back_tiles(front, messages, plains, loose, tiles):
    def copy(j):
        tiles[j] = front[j]

    loop(BEFORE_Z, copy, 16)
    pieces = []
    for message, plain in zip(messages, plains):
        unpack(message, plain)
        pieces.append((lambda b, plain=plain: plain[b * NZ : b * NZ + NZ], NZ))
    make_tiles(pieces, loose, tiles, BEFORE_Z)


def middle(k):
    return 4 * (k >> 1) + 1 + (k & 1)


def outer(k):
    return 4 * (k >> 1) + 3 * (k & 1)


def gather(slots, tiles, i):
    taken = [tiles[slots[m, i]] for m in range(NEIGH)]
    return jnp.concatenate(taken + taken[:1], axis=0)


def apply_atoms(slots, rows, tiles, applied, which, place):
    def atom(k):
        i = which(k)
        product = jnp.dot(rows[i], gather(slots, tiles, i), preferred_element_type=F32)
        if tiles.shape[2] == 256:
            product = product[:, 0:128] + product[:, 128:256]
        applied[aligned(place(k) * 16), :] = product

    loop(ATOMS // 2, atom, 16)


def densities(slots, noise_tiles, values, dense, which, place):
    def atom(k):
        i = which(k)
        value = values[aligned(i * 16), :]
        high = value.astype(BF16)
        low = (value - high.astype(F32)).astype(BF16)
        product = lax.dot_general(
            jnp.concatenate([high, low], axis=0),
            gather(slots, noise_tiles, i),
            (((1,), (1,)), ((), ())),
            preferred_element_type=F32,
        )
        product = product[0:16] + product[16:32]
        dense[0, aligned(place(k) * 16), :] = product[:, 0:128]
        dense[1, aligned(place(k) * 16), :] = product[:, 128:256]

    loop(ATOMS // 2, atom, 16)


def spread_middle(half, applied):
    def put(k):
        applied[aligned(middle(k) * 16), :] = half[aligned(k * 16), :]

    loop(ATOMS // 2, put, 16)


def front_kernel(slots, rows, own, u1, u2, v1, v2, front, half, loose):
    front_tiles(own, (u1, u2, v1, v2), loose, front)
    apply_atoms(slots, rows, front, half, middle, lambda k: k)


def front_third_kernel(coef, slots, rows, prev, sum_in, noise_tiles, own, u1, u2, v1, v2, front, half, dense,
                       loose, applied):
    front_tiles(own, (u1, u2, v1, v2), loose, front)
    apply_atoms(slots, rows, front, half, middle, lambda k: k)
    applied[...] = jnp.zeros_like(applied)
    spread_middle(half, applied)
    for a in range(ORB):
        at = pl.ds(a, ATOMS, stride=16)
        applied[at, :] = sum_in[a] + coef[3] * (2.0 * applied[at, :] - prev[a])
    densities(slots, noise_tiles, applied, dense, middle, lambda k: k)


def put_faces(parity, now, out1, out2, level, p1, p2):
    even = parity[0] == 0
    p1[ROWS_X - 16 :] = jnp.zeros((16, VECS), F32)
    p2[ROWS_X - 16 :] = jnp.zeros((16, VECS), F32)
    most = jnp.zeros((8, VECS), F32)
    for b in range(ORB):
        value = now[b]
        for row in range(0, ATOMS, 8):
            most = jnp.maximum(most, jnp.abs(value[row : row + 8]))
        for p in range(2):
            low, high = value[64 * p : 64 * p + 16], value[64 * p + 48 : 64 * p + 64]
            at = b * NX + 16 * p
            p1[at : at + 16] = jnp.where(even, high, low)
            p2[at : at + 16] = jnp.where(even, low, high)
    most = jnp.maximum(jnp.max(most, axis=0, keepdims=True), 1e-30)
    steps = jnp.ceil(jnp.log2(most) * 4.0 + 0.01)
    level[...] = jnp.broadcast_to(steps, (8, VECS))
    pack(p1, out1, level[...])
    pack(p2, out2, level[...])


def rest(slots, rows, front, half, messages, plains, loose, tiles, applied):
    back_tiles(front, messages, plains, loose, tiles)
    apply_atoms(slots, rows, tiles, applied, outer, outer)
    spread_middle(half, applied)


def first_kernel(parity, coef, slots, rows, own, front, half, z1, z2, now, total, out1, out2, level, tiles,
                 loose, applied, p1, p2, *plains):
    rest(slots, rows, front, half, (z1, z2), plains, loose, tiles, applied)
    for a in range(ORB):
        value = applied[pl.ds(a, ATOMS, stride=16), :]
        now[a] = value
        total[a] = coef[0] * own[a].astype(F32) + coef[1] * value
    put_faces(parity, now, out1, out2, level, p1, p2)


def second_kernel(parity, coef, slots, rows, prev, sum_in, front, half, z1, z2, now, total, out1, out2, level,
                  tiles, loose, applied, p1, p2, *plains):
    rest(slots, rows, front, half, (z1, z2), plains, loose, tiles, applied)
    for a in range(ORB):
        value = 2.0 * applied[pl.ds(a, ATOMS, stride=16), :] - prev[a].astype(F32)
        now[a] = value
        total[a] = sum_in[a] + coef[2] * value
    put_faces(parity, now, out1, out2, level, p1, p2)


def third_kernel(parity, coef, slots, lanes, rows, prev, sum_in, noise_tiles, deriv, front, half, dense_half, z1, z2,
                 total, forces, sent, tiles, loose, applied, dense, turned, stacked, *plains):
    rest(slots, rows, front, half, (z1, z2), plains, loose, tiles, applied)
    for a in range(ORB):
        at = pl.ds(a, ATOMS, stride=16)
        value = sum_in[a] + coef[3] * (2.0 * applied[at, :] - prev[a])
        total[a] = value
        applied[at, :] = value
    densities(slots, noise_tiles, applied, dense, outer, outer)
    for side in range(2):
        spread_middle(dense_half.at[side], dense.at[side])
    pair = [jnp.zeros((NEIGH, ATOMS), F32) for _ in range(3)]
    for a in range(ORB):
        at = pl.ds(a, ATOMS, stride=16)
        turned[0:128] = dense[0, at, :].T
        turned[128:256] = dense[1, at, :].T
        for b in range(ORB):
            density = turned[pl.ds(b, NEIGH, stride=16), :]
            for c in range(3):
                pair[c] = pair[c] + deriv[c, a, b].astype(F32) * density
    others = lax.broadcasted_iota(jnp.int32, (NEIGH, ATOMS), 0) > 0
    stacked[...] = jnp.zeros_like(stacked)
    own_rows = []
    for c in range(3):
        value = jnp.where(others, pair[c] * (1.0 / VECS), 0.0)
        high = value.astype(BF16).astype(F32)
        stacked[pl.ds(c, NEIGH, stride=16), :] = high
        stacked[pl.ds(8 + c, NEIGH, stride=16), :] = value - high
        own_rows.append(jnp.sum(value, axis=0, keepdims=True))
    lane = lax.broadcasted_iota(jnp.int32, (LANES, ATOMS), 0)
    summed = jnp.zeros((16, LANES), F32)
    for m in range(1, NEIGH):
        hit = jnp.where(lane == lanes[m : m + 1, :], 1.0, 0.0).astype(BF16)
        summed = summed + lax.dot_general(
            stacked[16 * m : 16 * m + 16].astype(BF16), hit, (((1,), (1,)), ((), ())), preferred_element_type=F32
        )
    summed = summed[0:8] + summed[8:16]
    forces[...] = summed[:, 0:FIRST]
    for c in range(3):
        forces[c : c + 1, 0:ATOMS] = forces[c : c + 1, 0:ATOMS] - own_rows[c]
    send(sent, summed[:, FIRST:], 64, place_of(parity))


def place_of(parity):
    return 4 * parity[0] + 2 * parity[1] + parity[2]


def send(sent, value, width, place):
    sent[...] = jnp.zeros_like(sent)
    for kind in range(1, 8):
        sent[place ^ kind, :, 0:width] = value[:, width * kind : width * kind + width]


def spread(got, lanes, place, width):
    lane = lax.broadcasted_iota(jnp.int32, (width, VECS), 0)
    summed = jnp.zeros((24, width), F32)
    for kind in range(1, 8):
        value = got[place ^ kind]
        terms = []
        for _ in range(3):
            terms.append(value.astype(BF16))
            value = value - terms[-1].astype(F32)
        hit = jnp.where(lane == lanes[kind : kind + 1, :], 1.0, 0.0).astype(BF16)
        summed = summed + lax.dot_general(
            jnp.concatenate([t.astype(F32) for t in terms], axis=0).astype(BF16), hit,
            (((1,), (1,)), ((), ())), preferred_element_type=F32,
        )
    return summed[0:8] + summed[8:16] + summed[16:24]


def merge_kernel(parity, held, lanes, got, out, sent):
    value = held[...] + spread(got, lanes, place_of(parity), FIRST)
    out[...] = value[:, 0:ATOMS]
    send(sent, value[:, SECOND:], 32, 7 - place_of(parity))


def finish_kernel(parity, held, lanes, got, out):
    value = held[...] + spread(got, lanes, 7 - place_of(parity), ATOMS)
    out[...] = value[0:3]


def blocks(second):
    sizes = [lax.axis_size(axis) for axis in AXES]
    pairs = [[((k + second) % n, (k + 1 + second) % n) for k in range(0, n, 2)] for n in sizes]
    return [
        [(x * sizes[1] + y) * sizes[2] + z for x in px for y in py for z in pz]
        for px in pairs[0] for py in pairs[1] for pz in pairs[2]
    ]


def trade_all(sent, second):
    return lax.all_to_all(sent, AXES, 0, 0, tiled=True, axis_index_groups=blocks(second))


def number(basis, digits, bases):
    for digit, base in zip(digits, bases):
        basis = basis * base + digit
    return basis


def second_lane(basis, cells, kinds):
    inner = number(basis, [jnp.where(k, 0, c) for c, k in zip(cells, kinds)], [jnp.where(k, 1, 4) for k in kinds])
    kind = 4 * kinds[0] + 2 * kinds[1] + kinds[2]
    return jnp.where(kind > 0, SECOND + 32 * kind + inner, number(basis, cells, (CX, CY, CZ)))


def landing_lanes(parity):
    tables = []
    for second in (0, 1):
        base = 4 if second else 5
        kind = lax.broadcasted_iota(jnp.int32, (8, VECS), 0)
        rest = lax.broadcasted_iota(jnp.int32, (8, VECS), 1)
        cells = [None] * 3
        for d in (2, 1, 0):
            traded = (kind >> (2 - d)) % 2 == 1
            radix = jnp.where(traded, 1, base)
            near = jnp.where((parity[d] == 0) != (second == 1), CX - 1, 0)
            cells[d] = jnp.where(traded, near, rest % radix)
            rest = rest // radix
        ghost = [(c == CX).astype(jnp.int32) for c in cells]
        lane = second_lane(rest, cells, ghost)
        tables.append(jnp.where((rest < 2) & (kind > 0), lane, -1).astype(jnp.int32))
    return tables


def slots_of(neighbours, parity):
    cells = CX * CY * CZ
    size_x, size_y, size_z = (lax.axis_size(axis) for axis in ("gx", "gy", "gz"))
    partner = neighbours.T
    domain = partner // ATOMS
    within = partner % ATOMS
    basis = within // cells
    remain = within % cells
    ex = domain // (size_y * size_z) * CX + remain // (CY * CZ) - lax.axis_index("gx") * CX + 1
    ey = domain // size_z % size_y * CY + remain // CZ % CY - lax.axis_index("gy") * CY + 1
    ez = domain % size_z * CZ + remain % CZ - lax.axis_index("gz") * CZ + 1
    ex = jnp.remainder(ex, CX * size_x)
    ey = jnp.remainder(ey, CY * size_y)
    ez = jnp.remainder(ez, CZ * size_z)
    x_out = (ex == 0) | (ex == CX + 1)
    y_out = (ey == 0) | (ey == CY + 1)
    z_out = (ez == 0) | (ez == CZ + 1)
    x_trade = ((ex == 0) == (parity[0] == 0)).astype(jnp.int32)
    y_trade = ((ey == 0) == (parity[1] == 0)).astype(jnp.int32)
    z_trade = ((ez == 0) == (parity[2] == 0)).astype(jnp.int32)
    q = jnp.where(x_out, 2 * CX + 2 * x_trade + basis, basis * CX + ex - 1)
    r_in = q * CY + ey - 1
    r_out = 2 * (CX + 2) * CY + y_trade * (2 * (CX + 2)) + q
    r = jnp.where(y_out, r_out, r_in)
    slots = jnp.where(z_out, BEFORE_Z + z_trade * NZ + r, r * CZ + ez - 1)
    cells = [e - 1 for e in (ex, ey, ez)]
    outside = (x_out, y_out, z_out)
    trades = (x_trade, y_trade, z_trade)
    firsts = [o & (t == 0) for o, t in zip(outside, trades)]
    seconds = [o & (t == 1) for o, t in zip(outside, trades)]
    kind = 4 * firsts[0] + 2 * firsts[1] + firsts[2]
    digits = [jnp.where(f, 0, jnp.where(s, 4, c)) for f, s, c in zip(firsts, seconds, cells)]
    inner = number(basis, digits, [jnp.where(f, 1, 5) for f in firsts])
    lanes = second_lane(basis, cells, [s.astype(jnp.int32) for s in seconds])
    lanes = jnp.where(kind > 0, FIRST + 64 * kind + inner, lanes)
    return slots.astype(jnp.int32), lanes.astype(jnp.int32)


def plain(rows):
    return pltpu.VMEM((rows, VECS), F32)


BACK_PLAINS = [plain(ROWS_Z), plain(ROWS_Z)]


def exchange(parity, level, own, out1, out2, work):
    dtype = out1.dtype
    rows_x, rows_y = ((ROWS_X, VECS), F32), ((ROWS_Y, VECS), F32)
    x2, x1 = swapped(out2, "gx", 1), swapped(out1, "gx", 0)
    out2, u1, u2, level = call(
        second_y_kernel, [((ROWS_Y, VECS), dtype), rows_x, rows_x, ((8, VECS), F32)], [SMEM] + [VMEM] * 4,
        (parity, x2, x1, level, own), [plain(ATOMS), plain(ROWS_Y)],
    )
    y2 = swapped(out2, "gy", 1)
    (out1,) = call(
        first_y_kernel, [((ROWS_Y, VECS), dtype)], [SMEM] + [VMEM] * 4, (parity, level, own, u1, u2),
        [plain(ATOMS), plain(ROWS_Y)],
    )
    y1 = swapped(out1, "gy", 0)
    out1, out2, v1, v2 = call(
        faces_z_kernel, [((ROWS_Z, VECS), dtype)] * 2 + [rows_y] * 2, [SMEM] + [VMEM] * 6,
        (parity, y2, y1, level, own, u1, u2), [plain(ATOMS)] + BACK_PLAINS,
    )
    z1, z2 = swapped(out1, "gz", 0), swapped(out2, "gz", 1)
    return work(own, u1, u2, v1, v2), (z1, z2)


def shards(noise_vectors, hamiltonian, derivative, neighbours, coefficients):
    parity = jnp.stack([lax.axis_index(axis) % 2 for axis in AXES]).astype(jnp.int32)
    slots, lanes = slots_of(neighbours, parity)
    lattice = noise_vectors.reshape(ORB, 2, CX, CY * CZ, VECS)
    low = lattice[:, :, 0].reshape(ORB * NX, VECS)
    high = lattice[:, :, CX - 1].reshape(ORB * NX, VECS)
    room = jnp.zeros((16, VECS), BF16)
    even = parity[0] == 0
    out1 = jnp.concatenate([jnp.where(even, high, low), room])
    out2 = jnp.concatenate([jnp.where(even, low, high), room])
    (rows,) = call(
        prep_kernel, [((ATOMS, 16, 256), BF16)], [VMEM], (hamiltonian.transpose(1, 2, 0, 3),),
        [plain(256), pltpu.VMEM((2, ATOMS * 16, 128), F32)], flops=1 << 22,
    )
    whole = ((ORB, ATOMS, VECS), F32)
    plane = ((ROWS_X, VECS), jnp.int16)
    tile = ((8, 128), F32)
    half = ((ATOMS // 2 * 16, VECS), F32)
    front_loose, loose, applied = plain(BEFORE_Z * 16), plain((SLOTS - BEFORE_Z) * 16), plain(ATOMS * 16)
    faces = [plain(ROWS_X), plain(ROWS_X)]

    def work(*vectors):
        width = 128 if vectors[0].dtype == BF16 else 256
        return call(
            front_kernel, [((BEFORE_Z, 16, width), BF16), half], [SMEM] + [VMEM] * 6, (slots, rows) + vectors,
            [front_loose], flops=1 << 29,
        )

    fronts, ghosts = exchange(parity, jnp.zeros((8, VECS), F32), noise_vectors, out1, out2, work)
    first, total, out1, out2, level, noise_tiles = call(
        first_kernel, [whole, whole, plane, plane, tile, ((SLOTS, 16, VECS), BF16)], [SMEM] * 3 + [VMEM] * 6,
        (parity, coefficients, slots, rows, noise_vectors, *fronts, *ghosts),
        [loose, applied] + faces + BACK_PLAINS, flops=1 << 29, mib=24,
    )
    fronts, ghosts = exchange(parity, level, first, out1, out2, work)
    second, total, out1, out2, level = call(
        second_kernel, [whole, whole, plane, plane, tile], [SMEM] * 3 + [VMEM] * 7,
        (parity, coefficients, slots, rows, noise_vectors, total, *fronts, *ghosts),
        [pltpu.VMEM((SLOTS, 16, 256), BF16), loose, applied] + faces + BACK_PLAINS, flops=1 << 29, mib=24,
    )

    def last_work(*vectors):
        return call(
            front_third_kernel, [((BEFORE_Z, 16, 256), BF16), half, ((2,) + half[0], F32)], [SMEM] * 2 + [VMEM] * 9,
            (coefficients, slots, rows, first, total, noise_tiles) + vectors,
            [front_loose, applied], flops=1 << 30, mib=24,
        )

    fronts, ghosts = exchange(parity, level, second, out1, out2, last_work)
    eight = ((8, 8, 128), F32)
    lanes1, lanes2 = landing_lanes(parity)
    weighted, held, sent = call(
        third_kernel, [whole, ((8, FIRST), F32), eight], [SMEM] * 3 + [VMEM] * 11,
        (parity, coefficients, slots, lanes, rows, first, total, noise_tiles, derivative.transpose(0, 2, 3, 1, 4), *fronts, *ghosts),
        [pltpu.VMEM((SLOTS, 16, 256), BF16), loose, applied, pltpu.VMEM((2, ATOMS * 16, 128), F32), plain(256),
         plain(NEIGH * 16)] + BACK_PLAINS,
        flops=1 << 30, mib=32,
    )
    held, sent = call(merge_kernel, [tile, eight], [SMEM] + [VMEM] * 3, (parity, held, lanes1, trade_all(sent, 0)))
    (forces,) = call(finish_kernel, [((3, ATOMS), F32)], [SMEM] + [VMEM] * 3, (parity, held, lanes2, trade_all(sent, 1)))
    return weighted, forces


def solution(mesh):
    in_specs = (
        P(None, ("gx", "gy", "gz"), None),
        P(None, None, None, ("gx", "gy", "gz")),
        P(None, None, None, None, ("gx", "gy", "gz")),
        P(("gx", "gy", "gz"), None),
        P(),
    )
    out_specs = (P(None, ("gx", "gy", "gz"), None), P(None, ("gx", "gy", "gz")))
    return jax.shard_map(shards, mesh=mesh, in_specs=in_specs, out_specs=out_specs, check_vma=False)
```

```python
import functools

import jax
import jax.numpy as jnp
from jax import lax
from jax.experimental import pallas as pl
from jax.experimental.pallas import tpu as pltpu
from jax.sharding import PartitionSpec as P

CX = 4
CY = 4
CZ = 4
ORB = 9
NEIGH = 15
ATOMS = 2 * CX * CY * CZ
VECS = 128
NX = 2 * CY * CZ
NY = 2 * (CX + 2) * CZ
NZ = 2 * (CX + 2) * (CY + 2)
BEFORE_Y = ATOMS + 2 * NX
BEFORE_Z = BEFORE_Y + 2 * NY
SLOTS = BEFORE_Z + 2 * NZ
ROWS_X = ORB * NX + 16
ROWS_Y = ORB * NY + 16
ROWS_Z = ORB * NZ + 8
KINDS = (1, 2, 4, 3, 5, 6, 7)
SECOND_SIZE = {kind: 2 * 4 ** (3 - kind.bit_count()) for kind in KINDS}
FIRST_SIZE = {kind: 2 * 5 ** (3 - kind.bit_count()) for kind in KINDS}
SECOND_AT = {kind: ATOMS + sum(SECOND_SIZE[k] for k in KINDS[:n]) for n, kind in enumerate(KINDS)}
FIRST = 256
FIRST_AT = {kind: FIRST + sum(FIRST_SIZE[k] for k in KINDS[:n]) for n, kind in enumerate(KINDS)}
LANES = 448
AXES = ("gx", "gy", "gz")
F32 = jnp.float32
BF16 = jnp.bfloat16
VMEM = pl.BlockSpec(memory_space=pltpu.VMEM)
HBM = pl.BlockSpec(memory_space=pltpu.HBM)


def call(kernel, outs, args, scratch=(), flops=0, mib=16, in_hbm=()):
    shapes = [jax.ShapeDtypeStruct(shape, dtype) for shape, dtype in outs]
    moved = sum(a.size * a.dtype.itemsize for a in args) + sum(s.size * s.dtype.itemsize for s in shapes)
    return pl.pallas_call(
        kernel,
        out_shape=shapes,
        in_specs=[HBM if k in in_hbm else VMEM for k in range(len(args))],
        out_specs=[VMEM] * len(shapes),
        scratch_shapes=list(scratch),
        compiler_params=pltpu.CompilerParams(vmem_limit_bytes=mib << 20),
        cost_estimate=pl.CostEstimate(flops=flops, bytes_accessed=moved, transcendentals=0),
    )(*args)


def odd(axis):
    return lax.axis_index(axis) & 1


def swapped(value, axis, second):
    count = lax.axis_size(axis)
    pairs = [((k + second) % count, (k + 1 + second) % count) for k in range(0, count, 2)]
    return lax.ppermute(value, axis, pairs + [(b, a) for a, b in pairs])


def prep_kernel(ham, rows, turned, wide):
    turned[...] = jnp.zeros_like(turned)
    wide[...] = jnp.zeros_like(wide)
    for a in range(ORB):
        for b in range(ORB):
            turned[pl.ds(b, NEIGH, stride=16), :] = ham[a, b].astype(F32)
        flat = turned[...].T
        wide[0, pl.ds(a, ATOMS, stride=16), :] = flat[:, 0:128]
        wide[1, pl.ds(a, ATOMS, stride=16), :] = flat[:, 128:256]

    def pack(i, carry):
        at = pl.ds(pl.multiple_of(i * 16, 16), 16)
        rows[i, :, 0:128] = wide[0, at, :].astype(BF16)
        rows[i, :, 128:256] = wide[1, at, :].astype(BF16)
        return carry

    lax.fori_loop(0, ATOMS, pack, 0, unroll=8)


def scale_of(level):
    return jnp.exp2(level * 0.25) * (1.0 / 32767.0)


def packed_of(level):
    return jnp.exp2(level * -0.25) * 32767.0


def level_of(message):
    rows = message.shape[0]
    return message[rows - 16 : rows, :].astype(jnp.int32).astype(F32)[8:16]


def pack(plain, message, level):
    fixed = message.dtype == jnp.int16
    rows = message.shape[0]
    if fixed:
        factor = jnp.concatenate([packed_of(level)] * 2, axis=0)
    for t in range(0, rows, 16):
        value = plain[t : t + 16, :]
        if fixed:
            value = jnp.round(value * factor)
            if t == rows - 16:
                value = jnp.concatenate([value[0:8], level], axis=0)
            message[t : t + 16, :] = value.astype(jnp.int32).astype(jnp.int16)
        else:
            message[t : t + 16, :] = value.astype(BF16)


def unpack(message, plain):
    if message.dtype != jnp.int16:
        for t in range(0, message.shape[0], 16):
            plain[t : t + 16, :] = message[t : t + 16, :].astype(F32)
        return
    factor = jnp.concatenate([scale_of(level_of(message))] * 2, axis=0)
    for t in range(0, message.shape[0], 16):
        plain[t : t + 16, :] = message[t : t + 16, :].astype(jnp.int32).astype(F32) * factor


def highest(levels):
    return functools.reduce(jnp.maximum, levels)


def pick_y(upper, own, u1, u2, held, picked):
    picked[ROWS_Y - 16 :] = jnp.zeros((16, VECS), F32)
    for b in range(ORB):
        if own.dtype == F32:
            take = [own[b, 16 * q : 16 * q + 16] for q in range(2 * CX)]
        else:
            held[...] = own[b].astype(F32)
            take = [held[16 * q : 16 * q + 16] for q in range(2 * CX)]
        take += [u[b * NX + 16 * q : b * NX + 16 * q + 16] for u in (u1, u2) for q in range(2)]
        for q, rows in enumerate(take):
            picked[b * NY + 4 * q : b * NY + 4 * q + 4] = jnp.where(upper, rows[12:16], rows[0:4])


def second_y_kernel(x2, x1, level, own, out, u1, u2, tall, held, picked):
    unpack(x1, u1)
    unpack(x2, u2)
    tall[...] = level[...]
    if out.dtype == jnp.int16:
        tall[...] = highest([level[...], level_of(x1), level_of(x2)])
    pick_y(odd("gy") == 1, own, u1, u2, held, picked)
    pack(picked, out, tall[...])


def first_y_kernel(tall, own, u1, u2, out, held, picked):
    pick_y(odd("gy") == 0, own, u1, u2, held, picked)
    pack(picked, out, tall[...])


def faces_z_kernel(y2, y1, level, own, u1, u2, out1, out2, v1, v2, held, p1, p2):
    fixed = out1.dtype == jnp.int16
    unpack(y1, v1)
    unpack(y2, v2)
    even = odd("gz") == 0
    p1[ROWS_Z - 8 :] = jnp.zeros((8, VECS), F32)
    p2[ROWS_Z - 8 :] = jnp.zeros((8, VECS), F32)
    ghosts = ((u1, NX), (u2, NX), (v1, NY), (v2, NY))
    for b in range(ORB):
        faces = []
        if not fixed:
            held[...] = own[b].astype(F32)
        for z in (0, CZ - 1):
            at = pl.ds(z, ATOMS // CZ, stride=CZ)
            faces.append([own[b, at, :] if fixed else held[at, :]])
            faces[-1] += [ref[pl.ds(b * rows + z, rows // CZ, stride=CZ), :] for ref, rows in ghosts]
        at = b * NZ
        for low, high in zip(*faces):
            rows = low.shape[0]
            p1[at : at + rows] = jnp.where(even, high, low)
            p2[at : at + rows] = jnp.where(even, low, high)
            at += rows
    level = highest([level[...], level_of(y1), level_of(y2)]) if fixed else level[...]
    pack(p1, out1, level)
    pack(p2, out2, level)


def loop(count, body, unroll):
    def step(k, carry):
        body(k)
        return carry

    lax.fori_loop(0, count, step, 0, unroll=unroll)


def aligned(row, count=16):
    return pl.ds(pl.multiple_of(row, count), count)


def make_tiles(pieces, loose, tiles, base):
    slots = sum(count for _, count in pieces)
    zero = jnp.zeros((8, VECS), F32)

    def clear(j):
        loose[aligned(j * 16 + 8, 8), :] = zero

    loop(slots, clear, 16)
    for b in range(ORB):
        at = 0
        for rows_of, count in pieces:
            loose[pl.ds(at * 16 + b, count, stride=16), :] = rows_of(b)
            at += count

    def split(j):
        value = loose[aligned(j * 16), :]
        high = value.astype(BF16)
        tiles[base + j, :, 0:128] = high
        if tiles.shape[2] == 256:
            tiles[base + j, :, 128:256] = (value - high.astype(F32)).astype(BF16)

    loop(slots, split, 16)


def front_tiles(own, plains, loose, tiles):
    pieces = [(lambda b: own[b].astype(F32), ATOMS)]
    for plain, count in zip(plains, (NX, NX, NY, NY)):
        pieces.append((lambda b, plain=plain, count=count: plain[b * count : b * count + count], count))
    make_tiles(pieces, loose, tiles, 0)


def back_tiles(front, messages, plains, loose, tiles):
    def copy(j):
        tiles[j] = front[j]

    loop(BEFORE_Z, copy, 16)
    pieces = []
    for message, plain in zip(messages, plains):
        unpack(message, plain)
        pieces.append((lambda b, plain=plain: plain[b * NZ : b * NZ + NZ], NZ))
    make_tiles(pieces, loose, tiles, BEFORE_Z)


def middle(k):
    return 4 * (k >> 1) + 1 + (k & 1)


def outer(k):
    return 4 * (k >> 1) + 3 * (k & 1)


def fetch(slots, table, arrived):
    copy = pltpu.make_async_copy(slots, table, arrived)
    copy.start()
    return copy


def gather(slots, tiles, i):
    taken = [tiles[slots[m, i]] for m in range(NEIGH)]
    return jnp.concatenate(taken + taken[:1], axis=0)


def apply_atoms(slots, rows, tiles, applied, which, place):
    def atom(k):
        i = which(k)
        product = jnp.dot(rows[i], gather(slots, tiles, i), preferred_element_type=F32)
        if tiles.shape[2] == 256:
            product = product[:, 0:128] + product[:, 128:256]
        applied[aligned(place(k) * 16), :] = product

    loop(ATOMS // 2, atom, ATOMS // 2)


def densities(slots, noise_tiles, values, dense, which, place):
    def atom(k):
        i = which(k)
        value = values[aligned(i * 16), :]
        high = value.astype(BF16)
        low = (value - high.astype(F32)).astype(BF16)
        product = lax.dot_general(
            jnp.concatenate([high, low], axis=0),
            gather(slots, noise_tiles, i),
            (((1,), (1,)), ((), ())),
            preferred_element_type=F32,
        )
        product = product[0:16] + product[16:32]
        dense[0, aligned(place(k) * 16), :] = product[:, 0:128]
        dense[1, aligned(place(k) * 16), :] = product[:, 128:256]

    loop(ATOMS // 2, atom, ATOMS // 2)


def spread_middle(half, applied):
    def put(k):
        applied[aligned(middle(k) * 16), :] = half[aligned(k * 16), :]

    loop(ATOMS // 2, put, 16)


def front_kernel(slots, rows, own, u1, u2, v1, v2, front, half, table, arrived, loose):
    copy = fetch(slots, table, arrived)
    front_tiles(own, (u1, u2, v1, v2), loose, front)
    copy.wait()
    apply_atoms(table, rows, front, half, middle, lambda k: k)


def front_third_kernel(coef, slots, rows, prev, sum_in, noise_tiles, own, u1, u2, v1, v2, front, half, dense,
                       table, arrived, loose, applied):
    copy = fetch(slots, table, arrived)
    front_tiles(own, (u1, u2, v1, v2), loose, front)
    copy.wait()
    apply_atoms(table, rows, front, half, middle, lambda k: k)
    applied[...] = jnp.zeros_like(applied)
    spread_middle(half, applied)
    for a in range(ORB):
        at = pl.ds(a, ATOMS, stride=16)
        applied[at, :] = sum_in[a] + coef[3 : 4, :] * (2.0 * applied[at, :] - prev[a])
    densities(table, noise_tiles, applied, dense, middle, lambda k: k)


def put_faces(now, out1, out2, level, p1, p2):
    even = odd("gx") == 0
    p1[ROWS_X - 16 :] = jnp.zeros((16, VECS), F32)
    p2[ROWS_X - 16 :] = jnp.zeros((16, VECS), F32)
    most = jnp.zeros((8, VECS), F32)
    for b in range(ORB):
        value = now[b]
        for row in range(0, ATOMS, 8):
            most = jnp.maximum(most, jnp.abs(value[row : row + 8]))
        for p in range(2):
            low, high = value[64 * p : 64 * p + 16], value[64 * p + 48 : 64 * p + 64]
            at = b * NX + 16 * p
            p1[at : at + 16] = jnp.where(even, high, low)
            p2[at : at + 16] = jnp.where(even, low, high)
    most = jnp.maximum(jnp.max(most, axis=0, keepdims=True), 1e-30)
    steps = jnp.ceil(jnp.log2(most) * 4.0 + 0.01)
    level[...] = jnp.broadcast_to(steps, (8, VECS))
    pack(p1, out1, level[...])
    pack(p2, out2, level[...])


def rest(slots, table, arrived, rows, front, half, messages, plains, loose, tiles, applied):
    copy = fetch(slots, table, arrived)
    back_tiles(front, messages, plains, loose, tiles)
    copy.wait()
    apply_atoms(table, rows, tiles, applied, outer, outer)
    spread_middle(half, applied)


def first_kernel(coef, slots, rows, own, front, half, z1, z2, now, total, out1, out2, level, tiles,
                 table, arrived, loose, applied, p1, p2, *plains):
    rest(slots, table, arrived, rows, front, half, (z1, z2), plains, loose, tiles, applied)
    for a in range(ORB):
        value = applied[pl.ds(a, ATOMS, stride=16), :]
        now[a] = value
        total[a] = coef[0 : 1, :] * own[a].astype(F32) + coef[1 : 2, :] * value
    put_faces(now, out1, out2, level, p1, p2)


def second_kernel(coef, slots, rows, prev, sum_in, front, half, z1, z2, now, total, out1, out2, level,
                  table, arrived, tiles, loose, applied, p1, p2, *plains):
    rest(slots, table, arrived, rows, front, half, (z1, z2), plains, loose, tiles, applied)
    for a in range(ORB):
        value = 2.0 * applied[pl.ds(a, ATOMS, stride=16), :] - prev[a].astype(F32)
        now[a] = value
        total[a] = sum_in[a] + coef[2 : 3, :] * value
    put_faces(now, out1, out2, level, p1, p2)


def third_kernel(coef, slots, lanes, rows, prev, sum_in, noise_tiles, deriv, front, half, dense_half, z1, z2,
                 total, forces, sent, table, arrived, tiles, loose, applied, dense, turned, stacked, slopes, loaded, *plains):
    load = pltpu.make_async_copy(deriv, slopes, loaded)
    load.start()
    rest(slots, table, arrived, rows, front, half, (z1, z2), plains, loose, tiles, applied)
    for a in range(ORB):
        at = pl.ds(a, ATOMS, stride=16)
        value = sum_in[a] + coef[3 : 4, :] * (2.0 * applied[at, :] - prev[a])
        total[a] = value
        applied[at, :] = value
    densities(table, noise_tiles, applied, dense, outer, outer)
    for side in range(2):
        spread_middle(dense_half.at[side], dense.at[side])
    load.wait()
    pair = [jnp.zeros((NEIGH, ATOMS), F32) for _ in range(3)]
    for a in range(ORB):
        at = pl.ds(a, ATOMS, stride=16)
        turned[0:128] = dense[0, at, :].T
        turned[128:256] = dense[1, at, :].T
        for b in range(ORB):
            density = turned[pl.ds(b, NEIGH, stride=16), :]
            for c in range(3):
                pair[c] = pair[c] + slopes[c, a, b].astype(F32) * density
    others = lax.broadcasted_iota(jnp.int32, (NEIGH, ATOMS), 0) > 0
    stacked[...] = jnp.zeros_like(stacked)
    own_rows = []
    for c in range(3):
        value = jnp.where(others, pair[c] * (1.0 / VECS), 0.0)
        high = value.astype(BF16).astype(F32)
        stacked[pl.ds(c, NEIGH, stride=16), :] = high
        stacked[pl.ds(8 + c, NEIGH, stride=16), :] = value - high
        own_rows.append(jnp.sum(value, axis=0, keepdims=True))
    lane = lax.broadcasted_iota(jnp.int32, (LANES, ATOMS), 0)
    summed = jnp.zeros((16, LANES), F32)
    for m in range(1, NEIGH):
        hit = jnp.where(lane == lanes[m : m + 1, :], 1.0, 0.0).astype(BF16)
        summed = summed + lax.dot_general(
            stacked[16 * m : 16 * m + 16].astype(BF16), hit, (((1,), (1,)), ((), ())), preferred_element_type=F32
        )
    summed = summed[0:8] + summed[8:16]
    forces[...] = summed[:, 0:FIRST]
    for c in range(3):
        forces[c : c + 1, 0:ATOMS] = forces[c : c + 1, 0:ATOMS] - own_rows[c]
    send(sent, summed, FIRST_AT, FIRST_SIZE, place_of())


def place_of():
    return 4 * odd("gx") + 2 * odd("gy") + odd("gz")


def send(sent, value, starts, sizes, place):
    sent[...] = jnp.zeros_like(sent)
    for kind in KINDS:
        sent[place ^ kind, :, 0 : sizes[kind]] = value[:, starts[kind] : starts[kind] + sizes[kind]]


def spread(got, lanes, place, width):
    lane = lax.broadcasted_iota(jnp.int32, (width, VECS), 0)
    hits, terms = [], []
    for kind in KINDS:
        value = got[place ^ kind]
        parts = []
        for _ in range(3):
            parts.append(value.astype(BF16).astype(F32))
            value = value - parts[-1]
        terms.append(jnp.concatenate(parts, axis=0).astype(BF16))
        hits.append(jnp.where(lane == lanes[kind : kind + 1, :], 1.0, 0.0).astype(BF16))
    summed = lax.dot_general(
        jnp.concatenate(terms, axis=1), jnp.concatenate(hits, axis=1), (((1,), (1,)), ((), ())),
        preferred_element_type=F32,
    )
    return summed[0:8] + summed[8:16] + summed[16:24]


def merge_kernel(held, lanes, got, out, sent):
    value = held[...] + spread(got, lanes, place_of(), FIRST)
    out[...] = value[:, 0:ATOMS]
    send(sent, value, SECOND_AT, SECOND_SIZE, 7 - place_of())


def finish_kernel(held, lanes, got, out):
    value = held[...] + spread(got, lanes, 7 - place_of(), ATOMS)
    out[...] = value[0:3]


def blocks(second):
    sizes = [lax.axis_size(axis) for axis in AXES]
    pairs = [[((k + second) % n, (k + 1 + second) % n) for k in range(0, n, 2)] for n in sizes]
    return [
        [(x * sizes[1] + y) * sizes[2] + z for x in px for y in py for z in pz]
        for px in pairs[0] for py in pairs[1] for pz in pairs[2]
    ]


def trade_all(sent, second):
    return lax.all_to_all(sent, AXES, 0, 0, tiled=True, axis_index_groups=blocks(second))


def number(basis, digits, bases):
    for digit, base in zip(digits, bases):
        basis = basis * base + digit
    return basis


def start_of(kind, starts):
    return sum(jnp.where(kind == k, at, 0) for k, at in starts.items())


def second_lane(basis, cells, kinds):
    inner = number(basis, [jnp.where(k, 0, c) for c, k in zip(cells, kinds)], [jnp.where(k, 1, 4) for k in kinds])
    kind = 4 * kinds[0] + 2 * kinds[1] + kinds[2]
    return jnp.where(kind > 0, start_of(kind, SECOND_AT) + inner, number(basis, cells, (CX, CY, CZ)))


def landing_lanes(parity):
    tables = []
    for second in (0, 1):
        base = 4 if second else 5
        kind = lax.broadcasted_iota(jnp.int32, (8, VECS), 0)
        rest = lax.broadcasted_iota(jnp.int32, (8, VECS), 1)
        cells = [None] * 3
        for d in (2, 1, 0):
            traded = (kind >> (2 - d)) % 2 == 1
            radix = jnp.where(traded, 1, base)
            near = jnp.where((parity[d] == 0) != (second == 1), CX - 1, 0)
            cells[d] = jnp.where(traded, near, rest % radix)
            rest = rest // radix
        ghost = [(c == CX).astype(jnp.int32) for c in cells]
        lane = second_lane(rest, cells, ghost)
        tables.append(jnp.where((rest < 2) & (kind > 0), lane, -1).astype(jnp.int32))
    return tables


def slots_of(neighbours, parity):
    cells = CX * CY * CZ
    size_x, size_y, size_z = (lax.axis_size(axis) for axis in ("gx", "gy", "gz"))
    partner = neighbours.T
    domain = partner // ATOMS
    within = partner % ATOMS
    basis = within // cells
    remain = within % cells
    ex = domain // (size_y * size_z) * CX + remain // (CY * CZ) - lax.axis_index("gx") * CX + 1
    ey = domain // size_z % size_y * CY + remain // CZ % CY - lax.axis_index("gy") * CY + 1
    ez = domain % size_z * CZ + remain % CZ - lax.axis_index("gz") * CZ + 1
    ex = jnp.remainder(ex, CX * size_x)
    ey = jnp.remainder(ey, CY * size_y)
    ez = jnp.remainder(ez, CZ * size_z)
    x_out = (ex == 0) | (ex == CX + 1)
    y_out = (ey == 0) | (ey == CY + 1)
    z_out = (ez == 0) | (ez == CZ + 1)
    x_trade = ((ex == 0) == (parity[0] == 0)).astype(jnp.int32)
    y_trade = ((ey == 0) == (parity[1] == 0)).astype(jnp.int32)
    z_trade = ((ez == 0) == (parity[2] == 0)).astype(jnp.int32)
    q = jnp.where(x_out, 2 * CX + 2 * x_trade + basis, basis * CX + ex - 1)
    r_in = q * CY + ey - 1
    r_out = 2 * (CX + 2) * CY + y_trade * (2 * (CX + 2)) + q
    r = jnp.where(y_out, r_out, r_in)
    slots = jnp.where(z_out, BEFORE_Z + z_trade * NZ + r, r * CZ + ez - 1)
    cells = [e - 1 for e in (ex, ey, ez)]
    outside = (x_out, y_out, z_out)
    trades = (x_trade, y_trade, z_trade)
    firsts = [o & (t == 0) for o, t in zip(outside, trades)]
    seconds = [o & (t == 1) for o, t in zip(outside, trades)]
    kind = 4 * firsts[0] + 2 * firsts[1] + firsts[2]
    digits = [jnp.where(f, 0, jnp.where(s, 4, c)) for f, s, c in zip(firsts, seconds, cells)]
    inner = number(basis, digits, [jnp.where(f, 1, 5) for f in firsts])
    lanes = second_lane(basis, cells, [s.astype(jnp.int32) for s in seconds])
    lanes = jnp.where(kind > 0, start_of(kind, FIRST_AT) + inner, lanes)
    return slots.astype(jnp.int32), lanes.astype(jnp.int32)


def plain(rows):
    return pltpu.VMEM((rows, VECS), F32)


BACK_PLAINS = [plain(ROWS_Z), plain(ROWS_Z)]


def exchange(level, own, out1, out2, work):
    dtype = out1.dtype
    rows_x, rows_y = ((ROWS_X, VECS), F32), ((ROWS_Y, VECS), F32)
    x2, x1 = swapped(out2, "gx", 1), swapped(out1, "gx", 0)
    out2, u1, u2, level = call(
        second_y_kernel, [((ROWS_Y, VECS), dtype), rows_x, rows_x, ((8, VECS), F32)],
        (x2, x1, level, own), [plain(ATOMS), plain(ROWS_Y)],
    )
    y2 = swapped(out2, "gy", 1)
    (out1,) = call(
        first_y_kernel, [((ROWS_Y, VECS), dtype)], (level, own, u1, u2),
        [plain(ATOMS), plain(ROWS_Y)],
    )
    y1 = swapped(out1, "gy", 0)
    out1, out2, v1, v2 = call(
        faces_z_kernel, [((ROWS_Z, VECS), dtype)] * 2 + [rows_y] * 2,
        (y2, y1, level, own, u1, u2), [plain(ATOMS)] + BACK_PLAINS,
    )
    z1, z2 = swapped(out1, "gz", 0), swapped(out2, "gz", 1)
    return work(own, u1, u2, v1, v2), (z1, z2)


def shards(noise_vectors, hamiltonian, derivative, neighbours, coefficients):
    parity = jnp.stack([lax.axis_index(axis) % 2 for axis in AXES]).astype(jnp.int32)
    slots, lanes = slots_of(neighbours, parity)
    coefs = jnp.broadcast_to(coefficients[:, None], (4, VECS))
    lattice = noise_vectors.reshape(ORB, 2, CX, CY * CZ, VECS)
    low = lattice[:, :, 0].reshape(ORB * NX, VECS)
    high = lattice[:, :, CX - 1].reshape(ORB * NX, VECS)
    room = jnp.zeros((16, VECS), BF16)
    even = parity[0] == 0
    out1 = jnp.concatenate([jnp.where(even, high, low), room])
    out2 = jnp.concatenate([jnp.where(even, low, high), room])
    (rows,) = call(
        prep_kernel, [((ATOMS, 16, 256), BF16)], (hamiltonian.transpose(1, 2, 0, 3),),
        [plain(256), pltpu.VMEM((2, ATOMS * 16, 128), F32)], flops=1 << 22,
    )
    whole = ((ORB, ATOMS, VECS), F32)
    plane = ((ROWS_X, VECS), jnp.int16)
    tile = ((8, 128), F32)
    half = ((ATOMS // 2 * 16, VECS), F32)
    front_loose, loose, applied = plain(BEFORE_Z * 16), plain((SLOTS - BEFORE_Z) * 16), plain(ATOMS * 16)
    faces = [plain(ROWS_X), plain(ROWS_X)]
    table = [pltpu.SMEM((NEIGH, ATOMS), jnp.int32), pltpu.SemaphoreType.DMA]

    def work(*vectors):
        width = 128 if vectors[0].dtype == BF16 else 256
        return call(
            front_kernel, [((BEFORE_Z, 16, width), BF16), half], (slots, rows) + vectors,
            table + [front_loose], flops=1 << 29,
        )

    fronts, ghosts = exchange(jnp.zeros((8, VECS), F32), noise_vectors, out1, out2, work)
    first, total, out1, out2, level, noise_tiles = call(
        first_kernel, [whole, whole, plane, plane, tile, ((SLOTS, 16, VECS), BF16)],
        (coefs, slots, rows, noise_vectors, *fronts, *ghosts),
        table + [loose, applied] + faces + BACK_PLAINS, flops=1 << 29,
    )
    fronts, ghosts = exchange(level, first, out1, out2, work)
    second, total, out1, out2, level = call(
        second_kernel, [whole, whole, plane, plane, tile],
        (coefs, slots, rows, noise_vectors, total, *fronts, *ghosts),
        table + [pltpu.VMEM((SLOTS, 16, 256), BF16), loose, applied] + faces + BACK_PLAINS, flops=1 << 29,
    )

    def last_work(*vectors):
        return call(
            front_third_kernel, [((BEFORE_Z, 16, 256), BF16), half, ((2,) + half[0], F32)],
            (coefs, slots, rows, first, total, noise_tiles) + vectors,
            table + [front_loose, applied], flops=1 << 30,
        )

    fronts, ghosts = exchange(level, second, out1, out2, last_work)
    eight = ((8, 8, 128), F32)
    slopes = derivative.transpose(0, 2, 3, 1, 4)
    lanes1, lanes2 = landing_lanes(parity)
    weighted, held, sent = call(
        third_kernel, [whole, ((8, FIRST), F32), eight],
        (coefs, slots, lanes, rows, first, total, noise_tiles, slopes, *fronts, *ghosts),
        table + [pltpu.VMEM((SLOTS, 16, 256), BF16), loose, applied, pltpu.VMEM((2, ATOMS * 16, 128), F32), plain(256),
         plain(NEIGH * 16), pltpu.VMEM(slopes.shape, BF16), pltpu.SemaphoreType.DMA] + BACK_PLAINS,
        flops=1 << 30, in_hbm=(7,),
    )
    held, sent = call(merge_kernel, [tile, eight], (held, lanes1, trade_all(sent, 0)))
    (forces,) = call(finish_kernel, [((3, ATOMS), F32)], (held, lanes2, trade_all(sent, 1)))
    return weighted, forces


def solution(mesh):
    in_specs = (
        P(None, ("gx", "gy", "gz"), None),
        P(None, None, None, ("gx", "gy", "gz")),
        P(None, None, None, None, ("gx", "gy", "gz")),
        P(("gx", "gy", "gz"), None),
        P(),
    )
    out_specs = (P(None, ("gx", "gy", "gz"), None), P(None, ("gx", "gy", "gz")))
    return jax.shard_map(shards, mesh=mesh, in_specs=in_specs, out_specs=out_specs, check_vma=False)
```

```python
import functools

import jax
import jax.numpy as jnp
from jax import lax
from jax.experimental import pallas as pl
from jax.experimental.pallas import tpu as pltpu
from jax.sharding import PartitionSpec as P

CX = 4
CY = 4
CZ = 4
ORB = 9
NEIGH = 15
ATOMS = 2 * CX * CY * CZ
VECS = 128
NX = 2 * CY * CZ
NY = 2 * (CX + 2) * CZ
NZ = 2 * (CX + 2) * (CY + 2)
BEFORE_Y = ATOMS + 2 * NX
BEFORE_Z = BEFORE_Y + 2 * NY
SLOTS = BEFORE_Z + 2 * NZ
ROWS_X = ORB * NX + 16
ROWS_Y = ORB * NY + 16
ROWS_Z = ORB * NZ + 8
KINDS = (1, 2, 4, 3, 5, 6, 7)
SECOND_SIZE = {kind: 2 * 4 ** (3 - kind.bit_count()) for kind in KINDS}
FIRST_SIZE = {kind: 2 * 5 ** (3 - kind.bit_count()) for kind in KINDS}
SECOND_AT = {kind: ATOMS + sum(SECOND_SIZE[k] for k in KINDS[:n]) for n, kind in enumerate(KINDS)}
FIRST = 256
FIRST_AT = {kind: FIRST + sum(FIRST_SIZE[k] for k in KINDS[:n]) for n, kind in enumerate(KINDS)}
LANES = 448
AXES = ("gx", "gy", "gz")
F32 = jnp.float32
BF16 = jnp.bfloat16
VMEM = pl.BlockSpec(memory_space=pltpu.VMEM)
HBM = pl.BlockSpec(memory_space=pltpu.HBM)


def call(kernel, outs, args, scratch=(), flops=0, mib=12, in_hbm=(), out_hbm=()):
    shapes = [jax.ShapeDtypeStruct(shape, dtype) for shape, dtype in outs]
    moved = sum(a.size * a.dtype.itemsize for a in args) + sum(s.size * s.dtype.itemsize for s in shapes)
    return pl.pallas_call(
        kernel,
        out_shape=shapes,
        in_specs=[HBM if k in in_hbm else VMEM for k in range(len(args))],
        out_specs=[HBM if k in out_hbm else VMEM for k in range(len(shapes))],
        scratch_shapes=list(scratch),
        compiler_params=pltpu.CompilerParams(vmem_limit_bytes=mib << 20),
        cost_estimate=pl.CostEstimate(flops=flops, bytes_accessed=moved, transcendentals=0),
    )(*args)


def odd(axis):
    return lax.axis_index(axis) & 1


def swapped(value, axis, second):
    count = lax.axis_size(axis)
    pairs = [((k + second) % count, (k + 1 + second) % count) for k in range(0, count, 2)]
    return lax.ppermute(value, axis, pairs + [(b, a) for a, b in pairs])


def prep_kernel(ham, rows, turned, wide):
    turned[...] = jnp.zeros_like(turned)
    wide[...] = jnp.zeros_like(wide)
    for a in range(ORB):
        for b in range(ORB):
            turned[pl.ds(b, NEIGH, stride=16), :] = ham[a, b].astype(F32)
        flat = turned[...].T
        wide[0, pl.ds(a, ATOMS, stride=16), :] = flat[:, 0:128]
        wide[1, pl.ds(a, ATOMS, stride=16), :] = flat[:, 128:256]

    def pack(i, carry):
        at = pl.ds(pl.multiple_of(i * 16, 16), 16)
        rows[i, :, 0:128] = wide[0, at, :].astype(BF16)
        rows[i, :, 128:256] = wide[1, at, :].astype(BF16)
        return carry

    lax.fori_loop(0, ATOMS, pack, 0, unroll=8)


def scale_of(level):
    return jnp.exp2(level * 0.25) * (1.0 / 32767.0)


def packed_of(level):
    return jnp.exp2(level * -0.25) * 32767.0


def level_of(message):
    rows = message.shape[0]
    return message[rows - 16 : rows, :].astype(jnp.int32).astype(F32)[8:16]


def pack(plain, message, level):
    fixed = message.dtype == jnp.int16
    rows = message.shape[0]
    if fixed:
        factor = jnp.concatenate([packed_of(level)] * 2, axis=0)
    for t in range(0, rows, 16):
        value = plain[t : t + 16, :]
        if fixed:
            value = jnp.round(value * factor)
            if t == rows - 16:
                value = jnp.concatenate([value[0:8], level], axis=0)
            message[t : t + 16, :] = value.astype(jnp.int32).astype(jnp.int16)
        else:
            message[t : t + 16, :] = value.astype(BF16)


def unpack(message, plain):
    if message.dtype != jnp.int16:
        for t in range(0, message.shape[0], 16):
            plain[t : t + 16, :] = message[t : t + 16, :].astype(F32)
        return
    factor = jnp.concatenate([scale_of(level_of(message))] * 2, axis=0)
    for t in range(0, message.shape[0], 16):
        plain[t : t + 16, :] = message[t : t + 16, :].astype(jnp.int32).astype(F32) * factor


def highest(levels):
    return functools.reduce(jnp.maximum, levels)


def pick_y(upper, own, u1, u2, picked):
    picked[ROWS_Y - 16 :] = jnp.zeros((16, VECS), F32)
    for b in range(ORB):
        take = [own[b, 16 * q : 16 * q + 16] for q in range(2 * CX)]
        take += [u[b * NX + 16 * q : b * NX + 16 * q + 16] for u in (u1, u2) for q in range(2)]
        for q, rows in enumerate(take):
            picked[b * NY + 4 * q : b * NY + 4 * q + 4] = jnp.where(upper, rows[12:16], rows[0:4])


def second_y_kernel(x2, x1, level, own, out, u1, u2, tall, picked):
    unpack(x1, u1)
    unpack(x2, u2)
    tall[...] = level[...]
    if out.dtype == jnp.int16:
        tall[...] = highest([level[...], level_of(x1), level_of(x2)])
    pick_y(odd("gy") == 1, own, u1, u2, picked)
    pack(picked, out, tall[...])


def first_y_kernel(tall, own, u1, u2, out, picked):
    pick_y(odd("gy") == 0, own, u1, u2, picked)
    pack(picked, out, tall[...])


def unpack_kernel(message, level, plain, tall):
    unpack(message, plain)
    tall[...] = highest([level[...], level_of(message)]) if message.dtype == jnp.int16 else level[...]


def faces_z_kernel(y1, level, own, u1, u2, v2, out1, out2, v1, p1, p2):
    fixed = out1.dtype == jnp.int16
    unpack(y1, v1)
    even = odd("gz") == 0
    p1[ROWS_Z - 8 :] = jnp.zeros((8, VECS), F32)
    p2[ROWS_Z - 8 :] = jnp.zeros((8, VECS), F32)
    ghosts = ((u1, NX), (u2, NX), (v1, NY), (v2, NY))
    for b in range(ORB):
        faces = []
        for z in (0, CZ - 1):
            at = pl.ds(z, ATOMS // CZ, stride=CZ)
            faces.append([own[b, at, :]])
            faces[-1] += [ref[pl.ds(b * rows + z, rows // CZ, stride=CZ), :] for ref, rows in ghosts]
        at = b * NZ
        for low, high in zip(*faces):
            rows = low.shape[0]
            p1[at : at + rows] = jnp.where(even, high, low)
            p2[at : at + rows] = jnp.where(even, low, high)
            at += rows
    level = highest([level[...], level_of(y1)]) if fixed else level[...]
    pack(p1, out1, level)
    pack(p2, out2, level)


def loop(count, body, unroll):
    def step(k, carry):
        body(k)
        return carry

    lax.fori_loop(0, count, step, 0, unroll=unroll)


def aligned(row, count=16):
    return pl.ds(pl.multiple_of(row, count), count)


def make_tiles(pieces, loose, tiles, base):
    slots = sum(count for _, count in pieces)
    zero = jnp.zeros((8, VECS), F32)

    def clear(j):
        loose[aligned(j * 16 + 8, 8), :] = zero

    loop(slots, clear, 16)
    for b in range(ORB):
        at = 0
        for rows_of, count in pieces:
            loose[pl.ds(at * 16 + b, count, stride=16), :] = rows_of(b)
            at += count

    def split(j):
        value = loose[aligned(j * 16), :]
        high = value.astype(BF16)
        tiles[base + j, :, 0:128] = high
        if tiles.shape[2] == 256:
            tiles[base + j, :, 128:256] = (value - high.astype(F32)).astype(BF16)

    loop(slots, split, 16)


def front_pieces(own, plains):
    pieces = [(lambda b: own[b], ATOMS)]
    for plain, count in zip(plains, (NX, NX, NY, NY)):
        pieces.append((lambda b, plain=plain, count=count: plain[b * count : b * count + count], count))
    return pieces


def back_pieces(messages, plains):
    pieces = []
    for message, plain in zip(messages, plains):
        unpack(message, plain)
        pieces.append((lambda b, plain=plain: plain[b * NZ : b * NZ + NZ], NZ))
    return pieces


def back_tiles(front, messages, plains, loose, tiles):
    def copy(j):
        tiles[j] = front[j]

    loop(BEFORE_Z, copy, 16)
    make_tiles(back_pieces(messages, plains), loose, tiles, BEFORE_Z)


def middle(k):
    return 4 * (k >> 1) + 1 + (k & 1)


def outer(k):
    return 4 * (k >> 1) + 3 * (k & 1)


def fetch(slots, table, arrived):
    copy = pltpu.make_async_copy(slots, table, arrived)
    copy.start()
    return copy


def gather(slots, tiles, i):
    taken = [tiles[slots[m, i]] for m in range(NEIGH)]
    return jnp.concatenate(taken + taken[:1], axis=0)


def apply_atoms(slots, rows, tiles, applied, which, place):
    def atom(k):
        i = which(k)
        product = jnp.dot(rows[i], gather(slots, tiles, i), preferred_element_type=F32)
        if tiles.shape[2] == 256:
            product = product[:, 0:128] + product[:, 128:256]
        applied[aligned(place(k) * 16), :] = product

    loop(ATOMS // 2, atom, ATOMS // 2)


def densities(slots, noise_tiles, values, dense, which, place):
    def atom(k):
        i = which(k)
        value = values[aligned(i * 16), :]
        high = value.astype(BF16)
        low = (value - high.astype(F32)).astype(BF16)
        product = lax.dot_general(
            jnp.concatenate([high, low], axis=0),
            gather(slots, noise_tiles, i),
            (((1,), (1,)), ((), ())),
            preferred_element_type=F32,
        )
        product = product[0:16] + product[16:32]
        dense[0, aligned(place(k) * 16), :] = product[:, 0:128]
        dense[1, aligned(place(k) * 16), :] = product[:, 128:256]

    loop(ATOMS // 2, atom, ATOMS // 2)


def tiles_kernel(level, own, z1, z2, u1, u2, v1, v2, tiles, loose, *plains):
    make_tiles(front_pieces(own, (u1, u2, v1, v2)) + back_pieces((z1, z2), plains), loose, tiles, 0)


def spread_middle(half, applied):
    def put(k):
        applied[aligned(middle(k) * 16), :] = half[aligned(k * 16), :]

    loop(ATOMS // 2, put, 16)


def front_kernel(slots, rows, own, u1, u2, v1, v2, front, half, table, arrived, loose):
    copy = fetch(slots, table, arrived)
    make_tiles(front_pieces(own, (u1, u2, v1, v2)), loose, front, 0)
    copy.wait()
    apply_atoms(table, rows, front, half, middle, lambda k: k)


def front_third_kernel(coef, slots, rows, sum_in, noise_tiles, own, u1, u2, v1, v2, front, half, dense,
                       table, arrived, loose, applied):
    copy = fetch(slots, table, arrived)
    make_tiles(front_pieces(own, (u1, u2, v1, v2)), loose, front, 0)
    copy.wait()
    apply_atoms(table, rows, front, half, middle, lambda k: k)
    applied[...] = jnp.zeros_like(applied)
    spread_middle(half, applied)
    for a in range(ORB):
        at = pl.ds(a, ATOMS, stride=16)
        applied[at, :] = sum_in[a] + (2.0 * coef[3 : 4, :]) * applied[at, :]
    densities(table, noise_tiles, applied, dense, middle, lambda k: k)


def put_faces(now, out1, out2, level, p1, p2):
    even = odd("gx") == 0
    p1[ROWS_X - 16 :] = jnp.zeros((16, VECS), F32)
    p2[ROWS_X - 16 :] = jnp.zeros((16, VECS), F32)
    most = jnp.zeros((8, VECS), F32)
    for b in range(ORB):
        value = now[b]
        for row in range(0, ATOMS, 8):
            most = jnp.maximum(most, jnp.abs(value[row : row + 8]))
        for p in range(2):
            low, high = value[64 * p : 64 * p + 16], value[64 * p + 48 : 64 * p + 64]
            at = b * NX + 16 * p
            p1[at : at + 16] = jnp.where(even, high, low)
            p2[at : at + 16] = jnp.where(even, low, high)
    most = jnp.maximum(jnp.max(most, axis=0, keepdims=True), 1e-30)
    steps = jnp.ceil(jnp.log2(most) * 4.0 + 0.01)
    level[...] = jnp.broadcast_to(steps, (8, VECS))
    pack(p1, out1, level[...])
    pack(p2, out2, level[...])


def rest(slots, table, arrived, rows, front, half, messages, plains, loose, tiles, applied):
    copy = fetch(slots, table, arrived)
    back_tiles(front, messages, plains, loose, tiles)
    copy.wait()
    apply_atoms(table, rows, tiles, applied, outer, outer)
    spread_middle(half, applied)


def first_kernel(coef, slots, rows, own, front, half, z1, z2, now, total, out1, out2, level,
                 table, arrived, tiles, loose, applied, p1, p2, *plains):
    rest(slots, table, arrived, rows, front, half, (z1, z2), plains, loose, tiles, applied)
    for a in range(ORB):
        value = applied[pl.ds(a, ATOMS, stride=16), :]
        now[a] = value
        total[a] = coef[0 : 1, :] * own[a] + coef[1 : 2, :] * value
    put_faces(now, out1, out2, level, p1, p2)


def second_kernel(coef, slots, rows, prev, sum_in, first, front, half, z1, z2, now, total, out1, out2, level,
                  table, arrived, tiles, loose, applied, p1, p2, *plains):
    rest(slots, table, arrived, rows, front, half, (z1, z2), plains, loose, tiles, applied)
    for a in range(ORB):
        value = 2.0 * applied[pl.ds(a, ATOMS, stride=16), :] - prev[a]
        now[a] = value
        total[a] = sum_in[a] + coef[2 : 3, :] * value - coef[3 : 4, :] * first[a]
    put_faces(now, out1, out2, level, p1, p2)


def third_kernel(coef, slots, lanes, rows, sum_in, noise_tiles, deriv, front, half, dense_half, z1, z2,
                 total, forces, sent, table, arrived, tiles, loose, applied, dense, turned, stacked, slopes, loaded, written, left, *plains):
    load = pltpu.make_async_copy(deriv, slopes, loaded)
    load.start()
    rest(slots, table, arrived, rows, front, half, (z1, z2), plains, loose, tiles, applied)
    for a in range(ORB):
        at = pl.ds(a, ATOMS, stride=16)
        value = sum_in[a] + (2.0 * coef[3 : 4, :]) * applied[at, :]
        written[a] = value
        applied[at, :] = value
    leave = pltpu.make_async_copy(written, total, left)
    leave.start()
    densities(table, noise_tiles, applied, dense, outer, outer)
    for side in range(2):
        spread_middle(dense_half.at[side], dense.at[side])
    load.wait()
    pair = [jnp.zeros((NEIGH, ATOMS), F32) for _ in range(3)]
    for a in range(ORB):
        at = pl.ds(a, ATOMS, stride=16)
        turned[0:128] = dense[0, at, :].T
        turned[128:256] = dense[1, at, :].T
        for b in range(ORB):
            density = turned[pl.ds(b, NEIGH, stride=16), :]
            for c in range(3):
                pair[c] = pair[c] + slopes[c, a, b].astype(F32) * density
    others = lax.broadcasted_iota(jnp.int32, (NEIGH, ATOMS), 0) > 0
    stacked[...] = jnp.zeros_like(stacked)
    own_rows = []
    for c in range(3):
        value = jnp.where(others, pair[c] * (1.0 / VECS), 0.0)
        high = value.astype(BF16).astype(F32)
        stacked[pl.ds(c, NEIGH, stride=16), :] = high
        stacked[pl.ds(8 + c, NEIGH, stride=16), :] = value - high
        own_rows.append(jnp.sum(value, axis=0, keepdims=True))
    lane = lax.broadcasted_iota(jnp.int32, (LANES, ATOMS), 0)
    summed = jnp.zeros((16, LANES), F32)
    for m in range(1, NEIGH):
        hit = jnp.where(lane == lanes[m : m + 1, :], 1.0, 0.0).astype(BF16)
        summed = summed + lax.dot_general(
            stacked[16 * m : 16 * m + 16].astype(BF16), hit, (((1,), (1,)), ((), ())), preferred_element_type=F32
        )
    summed = summed[0:8] + summed[8:16]
    forces[...] = summed[:, 0:FIRST]
    for c in range(3):
        forces[c : c + 1, 0:ATOMS] = forces[c : c + 1, 0:ATOMS] - own_rows[c]
    send(sent, summed, FIRST_AT, FIRST_SIZE, place_of())
    leave.wait()


def place_of():
    return 4 * odd("gx") + 2 * odd("gy") + odd("gz")


def send(sent, value, starts, sizes, place):
    sent[...] = jnp.zeros_like(sent)
    for kind in KINDS:
        sent[place ^ kind, :, 0 : sizes[kind]] = value[:, starts[kind] : starts[kind] + sizes[kind]]


def spread(got, lanes, place, width):
    lane = lax.broadcasted_iota(jnp.int32, (width, VECS), 0)
    hits, terms = [], []
    for kind in KINDS:
        value = got[place ^ kind]
        parts = []
        for _ in range(3):
            parts.append(value.astype(BF16).astype(F32))
            value = value - parts[-1]
        terms.append(jnp.concatenate(parts, axis=0).astype(BF16))
        hits.append(jnp.where(lane == lanes[kind : kind + 1, :], 1.0, 0.0).astype(BF16))
    summed = lax.dot_general(
        jnp.concatenate(terms, axis=1), jnp.concatenate(hits, axis=1), (((1,), (1,)), ((), ())),
        preferred_element_type=F32,
    )
    return summed[0:8] + summed[8:16] + summed[16:24]


def merge_kernel(held, got, out, sent):
    value = held[...] + spread(got, landing_lanes(0), place_of(), FIRST)
    out[...] = value[:, 0:ATOMS]
    send(sent, value, SECOND_AT, SECOND_SIZE, 7 - place_of())


def finish_kernel(held, got, out):
    value = held[...] + spread(got, landing_lanes(1), 7 - place_of(), ATOMS)
    out[...] = value[0:3]


def blocks(second):
    sizes = [lax.axis_size(axis) for axis in AXES]
    pairs = [[((k + second) % n, (k + 1 + second) % n) for k in range(0, n, 2)] for n in sizes]
    return [
        [(x * sizes[1] + y) * sizes[2] + z for x in px for y in py for z in pz]
        for px in pairs[0] for py in pairs[1] for pz in pairs[2]
    ]


def trade_all(sent, second):
    return lax.all_to_all(sent, AXES, 0, 0, tiled=True, axis_index_groups=blocks(second))


def number(basis, digits, bases):
    for digit, base in zip(digits, bases):
        basis = basis * base + digit
    return basis


def start_of(kind, starts):
    return sum(jnp.where(kind == k, at, 0) for k, at in starts.items())


def second_lane(basis, cells, kinds):
    inner = number(basis, [jnp.where(k == 1, 0, c) for c, k in zip(cells, kinds)], [jnp.where(k == 1, 1, 4) for k in kinds])
    kind = 4 * kinds[0] + 2 * kinds[1] + kinds[2]
    return jnp.where(kind > 0, start_of(kind, SECOND_AT) + inner, number(basis, cells, (CX, CY, CZ)))


def landing_lanes(second):
    kind = lax.broadcasted_iota(jnp.int32, (8, VECS), 0)
    rest = lax.broadcasted_iota(jnp.int32, (8, VECS), 1)
    cells = [None] * 3
    for d in (2, 1, 0):
        traded = ((kind >> (2 - d)) & 1) == 1
        near = jnp.where(odd(AXES[d]) == second, CX - 1, 0)
        less = rest >> 2 if second else (rest * 205) >> 10
        cells[d] = jnp.where(traded, near, rest - (4 if second else 5) * less)
        rest = jnp.where(traded, rest, less)
    ghost = [jnp.where(c == CX, 1, 0) for c in cells]
    lane = second_lane(rest, cells, ghost)
    return jnp.where((rest < 2) & (kind > 0), lane, -1)


def slots_of(neighbours, parity):
    cells = CX * CY * CZ
    size_x, size_y, size_z = (lax.axis_size(axis) for axis in ("gx", "gy", "gz"))
    partner = neighbours.T
    domain = partner // ATOMS
    within = partner % ATOMS
    basis = within // cells
    remain = within % cells
    ex = domain // (size_y * size_z) * CX + remain // (CY * CZ) - lax.axis_index("gx") * CX + 1
    ey = domain // size_z % size_y * CY + remain // CZ % CY - lax.axis_index("gy") * CY + 1
    ez = domain % size_z * CZ + remain % CZ - lax.axis_index("gz") * CZ + 1
    ex = jnp.remainder(ex, CX * size_x)
    ey = jnp.remainder(ey, CY * size_y)
    ez = jnp.remainder(ez, CZ * size_z)
    x_out = (ex == 0) | (ex == CX + 1)
    y_out = (ey == 0) | (ey == CY + 1)
    z_out = (ez == 0) | (ez == CZ + 1)
    x_trade = ((ex == 0) == (parity[0] == 0)).astype(jnp.int32)
    y_trade = ((ey == 0) == (parity[1] == 0)).astype(jnp.int32)
    z_trade = ((ez == 0) == (parity[2] == 0)).astype(jnp.int32)
    q = jnp.where(x_out, 2 * CX + 2 * x_trade + basis, basis * CX + ex - 1)
    r_in = q * CY + ey - 1
    r_out = 2 * (CX + 2) * CY + y_trade * (2 * (CX + 2)) + q
    r = jnp.where(y_out, r_out, r_in)
    slots = jnp.where(z_out, BEFORE_Z + z_trade * NZ + r, r * CZ + ez - 1)
    cells = [e - 1 for e in (ex, ey, ez)]
    outside = (x_out, y_out, z_out)
    trades = (x_trade, y_trade, z_trade)
    firsts = [o & (t == 0) for o, t in zip(outside, trades)]
    seconds = [o & (t == 1) for o, t in zip(outside, trades)]
    kind = 4 * firsts[0] + 2 * firsts[1] + firsts[2]
    digits = [jnp.where(f, 0, jnp.where(s, 4, c)) for f, s, c in zip(firsts, seconds, cells)]
    inner = number(basis, digits, [jnp.where(f, 1, 5) for f in firsts])
    lanes = second_lane(basis, cells, [s.astype(jnp.int32) for s in seconds])
    lanes = jnp.where(kind > 0, start_of(kind, FIRST_AT) + inner, lanes)
    return slots.astype(jnp.int32), lanes.astype(jnp.int32)


def passing(kernel, count, held):
    def with_held(*refs):
        kernel(*refs[:count], *refs[count + len(held) :])

    return with_held


def plain(rows):
    return pltpu.VMEM((rows, VECS), F32)


BACK_PLAINS = [plain(ROWS_Z), plain(ROWS_Z)]


def exchange(level, own, out1, out2, work, held=()):
    dtype = out1.dtype
    rows_x, rows_y = ((ROWS_X, VECS), F32), ((ROWS_Y, VECS), F32)
    x2, x1 = swapped(out2, "gx", 1), swapped(out1, "gx", 0)
    out2, u1, u2, level = call(
        passing(second_y_kernel, 4, held), [((ROWS_Y, VECS), dtype), rows_x, rows_x, ((8, VECS), F32)],
        (x2, x1, level, own) + held, [plain(ROWS_Y)],
    )
    y2 = swapped(out2, "gy", 1)
    (out1,) = call(
        first_y_kernel, [((ROWS_Y, VECS), dtype)], (level, own, u1, u2),
        [plain(ROWS_Y)],
    )
    y1 = swapped(out1, "gy", 0)
    v2, level = call(unpack_kernel, [rows_y, ((8, VECS), F32)], (y2, level), flops=1 << 31)
    out1, out2, v1 = call(
        faces_z_kernel, [((ROWS_Z, VECS), dtype)] * 2 + [rows_y],
        (y1, level, own, u1, u2, v2), BACK_PLAINS,
    )
    z1, z2 = swapped(out1, "gz", 0), swapped(out2, "gz", 1)
    return work(own, u1, u2, v1, v2), (z1, z2), (u1, u2, v1, v2)


def shards(noise_vectors, hamiltonian, derivative, neighbours, coefficients):
    parity = jnp.stack([lax.axis_index(axis) % 2 for axis in AXES]).astype(jnp.int32)
    slots, lanes = slots_of(neighbours, parity)
    coefs = jnp.broadcast_to(coefficients[:, None], (4, VECS))
    lattice = noise_vectors.reshape(ORB, 2, CX, CY * CZ, VECS)
    low = lattice[:, :, 0].reshape(ORB * NX, VECS)
    high = lattice[:, :, CX - 1].reshape(ORB * NX, VECS)
    room = jnp.zeros((16, VECS), BF16)
    even = parity[0] == 0
    out1 = jnp.concatenate([jnp.where(even, high, low), room])
    out2 = jnp.concatenate([jnp.where(even, low, high), room])
    (rows,) = call(
        prep_kernel, [((ATOMS, 16, 256), BF16)], (hamiltonian.transpose(1, 2, 0, 3),),
        [plain(256), pltpu.VMEM((2, ATOMS * 16, 128), F32)], flops=1 << 22,
    )
    noise = noise_vectors.astype(F32)
    whole = ((ORB, ATOMS, VECS), F32)
    plane = ((ROWS_X, VECS), jnp.int16)
    tile = ((8, 128), F32)
    half = ((ATOMS // 2 * 16, VECS), F32)
    front_loose, loose, applied = plain(BEFORE_Z * 16), plain((SLOTS - BEFORE_Z) * 16), plain(ATOMS * 16)
    faces = [plain(ROWS_X), plain(ROWS_X)]
    table = [pltpu.SMEM((NEIGH, ATOMS), jnp.int32), pltpu.SemaphoreType.DMA]

    def work(*vectors, width=256):
        return call(
            front_kernel, [((BEFORE_Z, 16, width), BF16), half], (slots, rows) + vectors,
            table + [front_loose], flops=1 << 29,
        )

    fronts, ghosts, plains = exchange(jnp.zeros((8, VECS), F32), noise, out1, out2, functools.partial(work, width=128))
    first, total, out1, out2, level = call(
        first_kernel, [whole, whole, plane, plane, tile],
        (coefs, slots, rows, noise, *fronts, *ghosts),
        table + [pltpu.VMEM((SLOTS, 16, VECS), BF16), loose, applied] + faces + BACK_PLAINS, flops=1 << 29,
    )
    (noise_tiles,) = call(
        tiles_kernel, [((SLOTS, 16, VECS), BF16)], (level, noise, *ghosts, *plains), [plain(SLOTS * 16)] + BACK_PLAINS
    )
    fronts, ghosts, _ = exchange(level, first, out1, out2, work, (noise_tiles,))
    second, total, out1, out2, level = call(
        second_kernel, [whole, whole, plane, plane, tile],
        (coefs, slots, rows, noise, total, first, *fronts, *ghosts),
        table + [pltpu.VMEM((SLOTS, 16, 256), BF16), loose, applied] + faces + BACK_PLAINS, flops=1 << 29,
    )

    def last_work(*vectors):
        return call(
            front_third_kernel, [((BEFORE_Z, 16, 256), BF16), half, ((2,) + half[0], F32)],
            (coefs, slots, rows, total, noise_tiles) + vectors,
            table + [front_loose, applied], flops=1 << 30,
        )

    fronts, ghosts, _ = exchange(level, second, out1, out2, last_work)
    eight = ((8, 8, 128), F32)
    slopes = derivative.transpose(0, 2, 3, 1, 4)
    weighted, held, sent = call(
        third_kernel, [whole, ((8, FIRST), F32), eight],
        (coefs, slots, lanes, rows, total, noise_tiles, slopes, *fronts, *ghosts),
        table + [pltpu.VMEM((SLOTS, 16, 256), BF16), loose, applied, pltpu.VMEM((2, ATOMS * 16, 128), F32), plain(256),
         plain(NEIGH * 16), pltpu.VMEM(slopes.shape, BF16), pltpu.SemaphoreType.DMA,
         pltpu.VMEM((ORB, ATOMS, VECS), F32), pltpu.SemaphoreType.DMA] + BACK_PLAINS,
        flops=1 << 30, in_hbm=(6,), out_hbm=(0,),
    )
    held, sent = call(merge_kernel, [tile, eight], (held, trade_all(sent, 0)))
    (forces,) = call(finish_kernel, [((3, ATOMS), F32)], (held, trade_all(sent, 1)))
    return weighted, forces


def solution(mesh):
    in_specs = (
        P(None, ("gx", "gy", "gz"), None),
        P(None, None, None, ("gx", "gy", "gz")),
        P(None, None, None, None, ("gx", "gy", "gz")),
        P(("gx", "gy", "gz"), None),
        P(),
    )
    out_specs = (P(None, ("gx", "gy", "gz"), None), P(None, ("gx", "gy", "gz")))
    return jax.shard_map(shards, mesh=mesh, in_specs=in_specs, out_specs=out_specs, check_vma=False)
```

```python
import functools

import jax
import jax.numpy as jnp
from jax import lax
from jax.experimental import pallas as pl
from jax.experimental.pallas import tpu as pltpu
from jax.sharding import PartitionSpec as P

CX = 4
CY = 4
CZ = 4
ORB = 9
NEIGH = 15
ATOMS = 2 * CX * CY * CZ
VECS = 128
NX = 2 * CY * CZ
NY = 2 * (CX + 2) * CZ
NZ = 2 * (CX + 2) * (CY + 2)
BEFORE_Y = ATOMS + 2 * NX
BEFORE_Z = BEFORE_Y + 2 * NY
SLOTS = BEFORE_Z + 2 * NZ
ROWS_X = ORB * NX + 16
ROWS_Y = ORB * NY + 16
ROWS_Z = ORB * NZ + 8
KINDS = (1, 2, 4, 3, 5, 6, 7)
SECOND_SIZE = {kind: 2 * 4 ** (3 - kind.bit_count()) for kind in KINDS}
FIRST_SIZE = {kind: 2 * 5 ** (3 - kind.bit_count()) for kind in KINDS}
SECOND_AT = {kind: ATOMS + sum(SECOND_SIZE[k] for k in KINDS[:n]) for n, kind in enumerate(KINDS)}
FIRST = 256
FIRST_AT = {kind: FIRST + sum(FIRST_SIZE[k] for k in KINDS[:n]) for n, kind in enumerate(KINDS)}
LANES = 448
AXES = ("gx", "gy", "gz")
F32 = jnp.float32
BF16 = jnp.bfloat16
VMEM = pl.BlockSpec(memory_space=pltpu.VMEM)
HBM = pl.BlockSpec(memory_space=pltpu.HBM)


def call(kernel, outs, args, scratch=(), flops=0, mib=12, in_hbm=(), out_hbm=()):
    shapes = [jax.ShapeDtypeStruct(shape, dtype) for shape, dtype in outs]
    moved = sum(a.size * a.dtype.itemsize for a in args) + sum(s.size * s.dtype.itemsize for s in shapes)
    return pl.pallas_call(
        kernel,
        out_shape=shapes,
        in_specs=[HBM if k in in_hbm else VMEM for k in range(len(args))],
        out_specs=[HBM if k in out_hbm else VMEM for k in range(len(shapes))],
        scratch_shapes=list(scratch),
        compiler_params=pltpu.CompilerParams(vmem_limit_bytes=mib << 20),
        cost_estimate=pl.CostEstimate(flops=flops, bytes_accessed=moved, transcendentals=0),
    )(*args)


def odd(axis):
    return lax.axis_index(axis) & 1


def swapped(value, axis, second):
    count = lax.axis_size(axis)
    pairs = [((k + second) % count, (k + 1 + second) % count) for k in range(0, count, 2)]
    return lax.ppermute(value, axis, pairs + [(b, a) for a, b in pairs])


def prep_kernel(ham, rows, turned, wide):
    turned[...] = jnp.zeros_like(turned)
    wide[...] = jnp.zeros_like(wide)
    for a in range(ORB):
        for b in range(ORB):
            turned[pl.ds(b, NEIGH, stride=16), :] = ham[a, b].astype(F32)
        flat = turned[...].T
        wide[0, pl.ds(a, ATOMS, stride=16), :] = flat[:, 0:128]
        wide[1, pl.ds(a, ATOMS, stride=16), :] = flat[:, 128:256]

    def pack(i, carry):
        at = pl.ds(pl.multiple_of(i * 16, 16), 16)
        rows[i, :, 0:128] = wide[0, at, :].astype(BF16)
        rows[i, :, 128:256] = wide[1, at, :].astype(BF16)
        return carry

    lax.fori_loop(0, ATOMS, pack, 0, unroll=8)


def scale_of(level):
    return jnp.exp2(level * 0.25) * (1.0 / 32767.0)


def packed_of(level):
    return jnp.exp2(level * -0.25) * 32767.0


def level_of(message):
    rows = message.shape[0]
    return message[rows - 16 : rows, :].astype(jnp.int32).astype(F32)[8:16]


def pack(plain, message, level):
    fixed = message.dtype == jnp.int16
    rows = message.shape[0]
    if fixed:
        factor = jnp.concatenate([packed_of(level)] * 2, axis=0)
    for t in range(0, rows, 16):
        value = plain[t : t + 16, :]
        if fixed:
            value = jnp.round(value * factor)
            if t == rows - 16:
                value = jnp.concatenate([value[0:8], level], axis=0)
            message[t : t + 16, :] = value.astype(jnp.int32).astype(jnp.int16)
        else:
            message[t : t + 16, :] = value.astype(BF16)


def unpack(message, plain):
    if message.dtype != jnp.int16:
        for t in range(0, message.shape[0], 16):
            plain[t : t + 16, :] = message[t : t + 16, :].astype(F32)
        return
    factor = jnp.concatenate([scale_of(level_of(message))] * 2, axis=0)
    for t in range(0, message.shape[0], 16):
        plain[t : t + 16, :] = message[t : t + 16, :].astype(jnp.int32).astype(F32) * factor


def highest(levels):
    return functools.reduce(jnp.maximum, levels)


def pick_y(upper, own, u1, u2, picked):
    picked[ROWS_Y - 16 :] = jnp.zeros((16, VECS), F32)
    for b in range(ORB):
        take = [own[b, 16 * q : 16 * q + 16] for q in range(2 * CX)]
        take += [u[b * NX + 16 * q : b * NX + 16 * q + 16] for u in (u1, u2) for q in range(2)]
        for q, rows in enumerate(take):
            picked[b * NY + 4 * q : b * NY + 4 * q + 4] = jnp.where(upper, rows[12:16], rows[0:4])


def second_y_kernel(x2, x1, level, own, out, u1, u2, tall, picked):
    unpack(x1, u1)
    unpack(x2, u2)
    tall[...] = level[...]
    if out.dtype == jnp.int16:
        tall[...] = highest([level[...], level_of(x1), level_of(x2)])
    pick_y(odd("gy") == 1, own, u1, u2, picked)
    pack(picked, out, tall[...])


def first_y_kernel(tall, own, u1, u2, out, picked):
    pick_y(odd("gy") == 0, own, u1, u2, picked)
    pack(picked, out, tall[...])


def unpack_kernel(message, level, plain, tall):
    unpack(message, plain)
    tall[...] = highest([level[...], level_of(message)]) if message.dtype == jnp.int16 else level[...]


def faces_z_kernel(y1, level, own, u1, u2, v2, out1, out2, v1, p1, p2):
    fixed = out1.dtype == jnp.int16
    unpack(y1, v1)
    even = odd("gz") == 0
    p1[ROWS_Z - 8 :] = jnp.zeros((8, VECS), F32)
    p2[ROWS_Z - 8 :] = jnp.zeros((8, VECS), F32)
    ghosts = ((u1, NX), (u2, NX), (v1, NY), (v2, NY))
    for b in range(ORB):
        faces = []
        for z in (0, CZ - 1):
            at = pl.ds(z, ATOMS // CZ, stride=CZ)
            faces.append([own[b, at, :]])
            faces[-1] += [ref[pl.ds(b * rows + z, rows // CZ, stride=CZ), :] for ref, rows in ghosts]
        at = b * NZ
        for low, high in zip(*faces):
            rows = low.shape[0]
            p1[at : at + rows] = jnp.where(even, high, low)
            p2[at : at + rows] = jnp.where(even, low, high)
            at += rows
    level = highest([level[...], level_of(y1)]) if fixed else level[...]
    pack(p1, out1, level)
    pack(p2, out2, level)


def loop(count, body, unroll):
    def step(k, carry):
        body(k)
        return carry

    lax.fori_loop(0, count, step, 0, unroll=unroll)


def aligned(row, count=16):
    return pl.ds(pl.multiple_of(row, count), count)


def make_tiles(pieces, loose, tiles, base):
    slots = sum(count for _, count in pieces)
    zero = jnp.zeros((8, VECS), F32)

    def clear(j):
        loose[aligned(j * 16 + 8, 8), :] = zero

    loop(slots, clear, 72)
    for b in range(ORB):
        at = 0
        for rows_of, count in pieces:
            loose[pl.ds(at * 16 + b, count, stride=16), :] = rows_of(b)
            at += count

    def split(j):
        value = loose[aligned(j * 16), :]
        high = value.astype(BF16)
        tiles[base + j, :, 0:128] = high
        if tiles.shape[2] == 256:
            tiles[base + j, :, 128:256] = (value - high.astype(F32)).astype(BF16)

    loop(slots, split, 72)


def front_pieces(own, plains):
    pieces = [(lambda b: own[b], ATOMS)]
    for plain, count in zip(plains, (NX, NX, NY, NY)):
        pieces.append((lambda b, plain=plain, count=count: plain[b * count : b * count + count], count))
    return pieces


def back_pieces(messages, plains):
    pieces = []
    for message, plain in zip(messages, plains):
        unpack(message, plain)
        pieces.append((lambda b, plain=plain: plain[b * NZ : b * NZ + NZ], NZ))
    return pieces


def back_tiles(front, messages, plains, loose, tiles):
    def copy(j):
        tiles[j] = front[j]

    loop(BEFORE_Z, copy, 72)
    make_tiles(back_pieces(messages, plains), loose, tiles, BEFORE_Z)


def middle(k):
    return 4 * (k >> 1) + 1 + (k & 1)


def outer(k):
    return 4 * (k >> 1) + 3 * (k & 1)


def fetch(slots, table, arrived):
    copy = pltpu.make_async_copy(slots, table, arrived)
    copy.start()
    return copy


def gather(slots, tiles, i):
    taken = [tiles[slots[m, i]] for m in range(NEIGH)]
    return jnp.concatenate(taken + taken[:1], axis=0)


def apply_atoms(slots, rows, tiles, applied, which, place):
    def atom(k):
        i = which(k)
        product = jnp.dot(rows[i], gather(slots, tiles, i), preferred_element_type=F32)
        if tiles.shape[2] == 256:
            product = product[:, 0:128] + product[:, 128:256]
        applied[aligned(place(k) * 16), :] = product

    loop(ATOMS // 2, atom, ATOMS // 2)


def densities(slots, noise_tiles, values, dense, which, place):
    def atom(k):
        i = which(k)
        value = values[aligned(i * 16), :]
        high = value.astype(BF16)
        low = (value - high.astype(F32)).astype(BF16)
        product = lax.dot_general(
            jnp.concatenate([high, low], axis=0),
            gather(slots, noise_tiles, i),
            (((1,), (1,)), ((), ())),
            preferred_element_type=F32,
        )
        product = product[0:16] + product[16:32]
        dense[0, aligned(place(k) * 16), :] = product[:, 0:128]
        dense[1, aligned(place(k) * 16), :] = product[:, 128:256]

    loop(ATOMS // 2, atom, ATOMS // 2)


def tiles_kernel(level, own, z1, z2, u1, u2, v1, v2, tiles, loose, *plains):
    make_tiles(front_pieces(own, (u1, u2, v1, v2)) + back_pieces((z1, z2), plains), loose, tiles, 0)


def spread_middle(half, applied):
    def put(k):
        applied[aligned(middle(k) * 16), :] = half[aligned(k * 16), :]

    loop(ATOMS // 2, put, ATOMS // 2)


def front_kernel(slots, rows, own, u1, u2, v1, v2, front, half, table, arrived, loose):
    copy = fetch(slots, table, arrived)
    make_tiles(front_pieces(own, (u1, u2, v1, v2)), loose, front, 0)
    copy.wait()
    apply_atoms(table, rows, front, half, middle, lambda k: k)


def front_third_kernel(coef, slots, rows, sum_in, noise_tiles, own, u1, u2, v1, v2, front, half, dense,
                       table, arrived, loose, applied):
    copy = fetch(slots, table, arrived)
    make_tiles(front_pieces(own, (u1, u2, v1, v2)), loose, front, 0)
    copy.wait()
    apply_atoms(table, rows, front, half, middle, lambda k: k)
    applied[...] = jnp.zeros_like(applied)
    spread_middle(half, applied)
    for a in range(ORB):
        at = pl.ds(a, ATOMS, stride=16)
        applied[at, :] = sum_in[a] + (2.0 * coef[3 : 4, :]) * applied[at, :]
    densities(table, noise_tiles, applied, dense, middle, lambda k: k)


def put_faces(now, out1, out2, level, p1, p2):
    even = odd("gx") == 0
    p1[ROWS_X - 16 :] = jnp.zeros((16, VECS), F32)
    p2[ROWS_X - 16 :] = jnp.zeros((16, VECS), F32)
    most = jnp.zeros((8, VECS), F32)
    for b in range(ORB):
        value = now[b]
        for row in range(0, ATOMS, 8):
            most = jnp.maximum(most, jnp.abs(value[row : row + 8]))
        for p in range(2):
            low, high = value[64 * p : 64 * p + 16], value[64 * p + 48 : 64 * p + 64]
            at = b * NX + 16 * p
            p1[at : at + 16] = jnp.where(even, high, low)
            p2[at : at + 16] = jnp.where(even, low, high)
    most = jnp.maximum(jnp.max(most, axis=0, keepdims=True), 1e-30)
    steps = jnp.ceil(jnp.log2(most) * 4.0 + 0.01)
    level[...] = jnp.broadcast_to(steps, (8, VECS))
    pack(p1, out1, level[...])
    pack(p2, out2, level[...])


def rest(slots, table, arrived, rows, front, half, messages, plains, loose, tiles, applied):
    copy = fetch(slots, table, arrived)
    back_tiles(front, messages, plains, loose, tiles)
    copy.wait()
    apply_atoms(table, rows, tiles, applied, outer, outer)
    spread_middle(half, applied)


def first_kernel(coef, slots, rows, own, front, half, z1, z2, now, total, out1, out2, level,
                 table, arrived, tiles, loose, applied, p1, p2, *plains):
    rest(slots, table, arrived, rows, front, half, (z1, z2), plains, loose, tiles, applied)
    for a in range(ORB):
        value = applied[pl.ds(a, ATOMS, stride=16), :]
        now[a] = value
        total[a] = coef[0 : 1, :] * own[a] + coef[1 : 2, :] * value
    put_faces(now, out1, out2, level, p1, p2)


def second_kernel(coef, slots, rows, prev, sum_in, first, front, half, z1, z2, now, total, out1, out2, level,
                  table, arrived, tiles, loose, applied, p1, p2, *plains):
    rest(slots, table, arrived, rows, front, half, (z1, z2), plains, loose, tiles, applied)
    for a in range(ORB):
        value = 2.0 * applied[pl.ds(a, ATOMS, stride=16), :] - prev[a]
        now[a] = value
        total[a] = sum_in[a] + coef[2 : 3, :] * value - coef[3 : 4, :] * first[a]
    put_faces(now, out1, out2, level, p1, p2)


def third_kernel(coef, slots, lanes, rows, sum_in, noise_tiles, deriv, front, half, dense_half, z1, z2,
                 total, forces, sent, table, arrived, tiles, loose, applied, dense, turned, stacked, slopes, loaded, written, left, *plains):
    load = pltpu.make_async_copy(deriv, slopes, loaded)
    load.start()
    rest(slots, table, arrived, rows, front, half, (z1, z2), plains, loose, tiles, applied)
    for a in range(ORB):
        at = pl.ds(a, ATOMS, stride=16)
        value = sum_in[a] + (2.0 * coef[3 : 4, :]) * applied[at, :]
        written[a] = value
        applied[at, :] = value
    leave = pltpu.make_async_copy(written, total, left)
    leave.start()
    densities(table, noise_tiles, applied, dense, outer, outer)
    for side in range(2):
        spread_middle(dense_half.at[side], dense.at[side])
    load.wait()
    pair = [jnp.zeros((NEIGH, ATOMS), F32) for _ in range(3)]
    for a in range(ORB):
        at = pl.ds(a, ATOMS, stride=16)
        turned[0:128] = dense[0, at, :].T
        turned[128:256] = dense[1, at, :].T
        for b in range(ORB):
            density = turned[pl.ds(b, NEIGH, stride=16), :]
            for c in range(3):
                pair[c] = pair[c] + slopes[c, a, b].astype(F32) * density
    others = lax.broadcasted_iota(jnp.int32, (NEIGH, ATOMS), 0) > 0
    stacked[...] = jnp.zeros_like(stacked)
    own_rows = []
    for c in range(3):
        value = jnp.where(others, pair[c] * (1.0 / VECS), 0.0)
        high = value.astype(BF16).astype(F32)
        stacked[pl.ds(c, NEIGH, stride=16), :] = high
        stacked[pl.ds(8 + c, NEIGH, stride=16), :] = value - high
        own_rows.append(jnp.sum(value, axis=0, keepdims=True))
    lane = lax.broadcasted_iota(jnp.int32, (LANES, ATOMS), 0)
    summed = jnp.zeros((16, LANES), F32)
    for m in range(1, NEIGH):
        hit = jnp.where(lane == lanes[m : m + 1, :], 1.0, 0.0).astype(BF16)
        summed = summed + lax.dot_general(
            stacked[16 * m : 16 * m + 16].astype(BF16), hit, (((1,), (1,)), ((), ())), preferred_element_type=F32
        )
    summed = summed[0:8] + summed[8:16]
    forces[...] = summed[:, 0:FIRST]
    for c in range(3):
        forces[c : c + 1, 0:ATOMS] = forces[c : c + 1, 0:ATOMS] - own_rows[c]
    send(sent, summed, FIRST_AT, FIRST_SIZE, place_of())
    leave.wait()


def place_of():
    return 4 * odd("gx") + 2 * odd("gy") + odd("gz")


def send(sent, value, starts, sizes, place):
    sent[...] = jnp.zeros_like(sent)
    for kind in KINDS:
        sent[place ^ kind, :, 0 : sizes[kind]] = value[:, starts[kind] : starts[kind] + sizes[kind]]


def spread(got, lanes, place, width):
    lane = lax.broadcasted_iota(jnp.int32, (width, VECS), 0)
    hits, terms = [], []
    for kind in KINDS:
        value = got[place ^ kind]
        parts = []
        for _ in range(3):
            parts.append(value.astype(BF16).astype(F32))
            value = value - parts[-1]
        terms.append(jnp.concatenate(parts, axis=0).astype(BF16))
        hits.append(jnp.where(lane == lanes[kind : kind + 1, :], 1.0, 0.0).astype(BF16))
    summed = lax.dot_general(
        jnp.concatenate(terms, axis=1), jnp.concatenate(hits, axis=1), (((1,), (1,)), ((), ())),
        preferred_element_type=F32,
    )
    return summed[0:8] + summed[8:16] + summed[16:24]


def merge_kernel(held, got, out, sent):
    value = held[...] + spread(got, landing_lanes(0), place_of(), FIRST)
    out[...] = value[:, 0:ATOMS]
    send(sent, value, SECOND_AT, SECOND_SIZE, 7 - place_of())


def finish_kernel(held, got, out):
    value = held[...] + spread(got, landing_lanes(1), 7 - place_of(), ATOMS)
    out[...] = value[0:3]


def blocks(second):
    sizes = [lax.axis_size(axis) for axis in AXES]
    pairs = [[((k + second) % n, (k + 1 + second) % n) for k in range(0, n, 2)] for n in sizes]
    return [
        [(x * sizes[1] + y) * sizes[2] + z for x in px for y in py for z in pz]
        for px in pairs[0] for py in pairs[1] for pz in pairs[2]
    ]


def trade_all(sent, second):
    return lax.all_to_all(sent, AXES, 0, 0, tiled=True, axis_index_groups=blocks(second))


def number(basis, digits, bases):
    for digit, base in zip(digits, bases):
        basis = basis * base + digit
    return basis


def start_of(kind, starts):
    return sum(jnp.where(kind == k, at, 0) for k, at in starts.items())


def second_lane(basis, cells, kinds):
    inner = number(basis, [jnp.where(k == 1, 0, c) for c, k in zip(cells, kinds)], [jnp.where(k == 1, 1, 4) for k in kinds])
    kind = 4 * kinds[0] + 2 * kinds[1] + kinds[2]
    return jnp.where(kind > 0, start_of(kind, SECOND_AT) + inner, number(basis, cells, (CX, CY, CZ)))


def landing_lanes(second):
    kind = lax.broadcasted_iota(jnp.int32, (8, VECS), 0)
    rest = lax.broadcasted_iota(jnp.int32, (8, VECS), 1)
    cells = [None] * 3
    for d in (2, 1, 0):
        traded = ((kind >> (2 - d)) & 1) == 1
        near = jnp.where(odd(AXES[d]) == second, CX - 1, 0)
        less = rest >> 2 if second else (rest * 205) >> 10
        cells[d] = jnp.where(traded, near, rest - (4 if second else 5) * less)
        rest = jnp.where(traded, rest, less)
    ghost = [jnp.where(c == CX, 1, 0) for c in cells]
    lane = second_lane(rest, cells, ghost)
    return jnp.where((rest < 2) & (kind > 0), lane, -1)


def slots_of(neighbours, parity):
    cells = CX * CY * CZ
    size_x, size_y, size_z = (lax.axis_size(axis) for axis in ("gx", "gy", "gz"))
    partner = neighbours.T
    domain = partner // ATOMS
    within = partner % ATOMS
    basis = within // cells
    remain = within % cells
    ex = domain // (size_y * size_z) * CX + remain // (CY * CZ) - lax.axis_index("gx") * CX + 1
    ey = domain // size_z % size_y * CY + remain // CZ % CY - lax.axis_index("gy") * CY + 1
    ez = domain % size_z * CZ + remain % CZ - lax.axis_index("gz") * CZ + 1
    ex = jnp.remainder(ex, CX * size_x)
    ey = jnp.remainder(ey, CY * size_y)
    ez = jnp.remainder(ez, CZ * size_z)
    x_out = (ex == 0) | (ex == CX + 1)
    y_out = (ey == 0) | (ey == CY + 1)
    z_out = (ez == 0) | (ez == CZ + 1)
    x_trade = ((ex == 0) == (parity[0] == 0)).astype(jnp.int32)
    y_trade = ((ey == 0) == (parity[1] == 0)).astype(jnp.int32)
    z_trade = ((ez == 0) == (parity[2] == 0)).astype(jnp.int32)
    q = jnp.where(x_out, 2 * CX + 2 * x_trade + basis, basis * CX + ex - 1)
    r_in = q * CY + ey - 1
    r_out = 2 * (CX + 2) * CY + y_trade * (2 * (CX + 2)) + q
    r = jnp.where(y_out, r_out, r_in)
    slots = jnp.where(z_out, BEFORE_Z + z_trade * NZ + r, r * CZ + ez - 1)
    cells = [e - 1 for e in (ex, ey, ez)]
    outside = (x_out, y_out, z_out)
    trades = (x_trade, y_trade, z_trade)
    firsts = [o & (t == 0) for o, t in zip(outside, trades)]
    seconds = [o & (t == 1) for o, t in zip(outside, trades)]
    kind = 4 * firsts[0] + 2 * firsts[1] + firsts[2]
    digits = [jnp.where(f, 0, jnp.where(s, 4, c)) for f, s, c in zip(firsts, seconds, cells)]
    inner = number(basis, digits, [jnp.where(f, 1, 5) for f in firsts])
    lanes = second_lane(basis, cells, [s.astype(jnp.int32) for s in seconds])
    lanes = jnp.where(kind > 0, start_of(kind, FIRST_AT) + inner, lanes)
    return slots.astype(jnp.int32), lanes.astype(jnp.int32)


def passing(kernel, count, held):
    def with_held(*refs):
        kernel(*refs[:count], *refs[count + len(held) :])

    return with_held


def plain(rows):
    return pltpu.VMEM((rows, VECS), F32)


BACK_PLAINS = [plain(ROWS_Z), plain(ROWS_Z)]


def exchange(level, own, out1, out2, work, held=()):
    dtype = out1.dtype
    rows_x, rows_y = ((ROWS_X, VECS), F32), ((ROWS_Y, VECS), F32)
    x2, x1 = swapped(out2, "gx", 1), swapped(out1, "gx", 0)
    out2, u1, u2, level = call(
        passing(second_y_kernel, 4, held), [((ROWS_Y, VECS), dtype), rows_x, rows_x, ((8, VECS), F32)],
        (x2, x1, level, own) + held, [plain(ROWS_Y)],
    )
    y2 = swapped(out2, "gy", 1)
    (out1,) = call(
        first_y_kernel, [((ROWS_Y, VECS), dtype)], (level, own, u1, u2),
        [plain(ROWS_Y)],
    )
    y1 = swapped(out1, "gy", 0)
    v2, level = call(unpack_kernel, [rows_y, ((8, VECS), F32)], (y2, level), flops=1 << 31)
    out1, out2, v1 = call(
        faces_z_kernel, [((ROWS_Z, VECS), dtype)] * 2 + [rows_y],
        (y1, level, own, u1, u2, v2), BACK_PLAINS,
    )
    z1, z2 = swapped(out1, "gz", 0), swapped(out2, "gz", 1)
    return work(own, u1, u2, v1, v2), (z1, z2), (u1, u2, v1, v2)


def shards(noise_vectors, hamiltonian, derivative, neighbours, coefficients):
    parity = jnp.stack([lax.axis_index(axis) % 2 for axis in AXES]).astype(jnp.int32)
    slots, lanes = slots_of(neighbours, parity)
    coefs = jnp.broadcast_to(coefficients[:, None], (4, VECS))
    lattice = noise_vectors.reshape(ORB, 2, CX, CY * CZ, VECS)
    low = lattice[:, :, 0].reshape(ORB * NX, VECS)
    high = lattice[:, :, CX - 1].reshape(ORB * NX, VECS)
    room = jnp.zeros((16, VECS), BF16)
    even = parity[0] == 0
    out1 = jnp.concatenate([jnp.where(even, high, low), room])
    out2 = jnp.concatenate([jnp.where(even, low, high), room])
    (rows,) = call(
        prep_kernel, [((ATOMS, 16, 256), BF16)], (hamiltonian.transpose(1, 2, 0, 3),),
        [plain(256), pltpu.VMEM((2, ATOMS * 16, 128), F32)], flops=1 << 22,
    )
    noise = noise_vectors.astype(F32)
    whole = ((ORB, ATOMS, VECS), F32)
    plane = ((ROWS_X, VECS), jnp.int16)
    tile = ((8, 128), F32)
    half = ((ATOMS // 2 * 16, VECS), F32)
    front_loose, loose, applied = plain(BEFORE_Z * 16), plain((SLOTS - BEFORE_Z) * 16), plain(ATOMS * 16)
    faces = [plain(ROWS_X), plain(ROWS_X)]
    table = [pltpu.SMEM((NEIGH, ATOMS), jnp.int32), pltpu.SemaphoreType.DMA]

    def work(*vectors, width=256):
        return call(
            front_kernel, [((BEFORE_Z, 16, width), BF16), half], (slots, rows) + vectors,
            table + [front_loose], flops=1 << 29,
        )

    fronts, ghosts, plains = exchange(jnp.zeros((8, VECS), F32), noise, out1, out2, functools.partial(work, width=128))
    first, total, out1, out2, level = call(
        first_kernel, [whole, whole, plane, plane, tile],
        (coefs, slots, rows, noise, *fronts, *ghosts),
        table + [pltpu.VMEM((SLOTS, 16, VECS), BF16), loose, applied] + faces + BACK_PLAINS, flops=1 << 29,
    )
    (noise_tiles,) = call(
        tiles_kernel, [((SLOTS, 16, VECS), BF16)], (level, noise, *ghosts, *plains), [plain(SLOTS * 16)] + BACK_PLAINS
    )
    fronts, ghosts, _ = exchange(level, first, out1, out2, work, (noise_tiles,))
    second, total, out1, out2, level = call(
        second_kernel, [whole, whole, plane, plane, tile],
        (coefs, slots, rows, noise, total, first, *fronts, *ghosts),
        table + [pltpu.VMEM((SLOTS, 16, 256), BF16), loose, applied] + faces + BACK_PLAINS, flops=1 << 29,
    )

    def last_work(*vectors):
        return call(
            front_third_kernel, [((BEFORE_Z, 16, 256), BF16), half, ((2,) + half[0], F32)],
            (coefs, slots, rows, total, noise_tiles) + vectors,
            table + [front_loose, applied], flops=1 << 30,
        )

    fronts, ghosts, _ = exchange(level, second, out1, out2, last_work)
    eight = ((8, 8, 128), F32)
    slopes = derivative.transpose(0, 2, 3, 1, 4)
    weighted, held, sent = call(
        third_kernel, [whole, ((8, FIRST), F32), eight],
        (coefs, slots, lanes, rows, total, noise_tiles, slopes, *fronts, *ghosts),
        table + [pltpu.VMEM((SLOTS, 16, 256), BF16), loose, applied, pltpu.VMEM((2, ATOMS * 16, 128), F32), plain(256),
         plain(NEIGH * 16), pltpu.VMEM(slopes.shape, BF16), pltpu.SemaphoreType.DMA,
         pltpu.VMEM((ORB, ATOMS, VECS), F32), pltpu.SemaphoreType.DMA] + BACK_PLAINS,
        flops=1 << 30, in_hbm=(6,), out_hbm=(0,),
    )
    held, sent = call(merge_kernel, [tile, eight], (held, trade_all(sent, 0)))
    (forces,) = call(finish_kernel, [((3, ATOMS), F32)], (held, trade_all(sent, 1)))
    return weighted, forces


def solution(mesh):
    in_specs = (
        P(None, ("gx", "gy", "gz"), None),
        P(None, None, None, ("gx", "gy", "gz")),
        P(None, None, None, None, ("gx", "gy", "gz")),
        P(("gx", "gy", "gz"), None),
        P(),
    )
    out_specs = (P(None, ("gx", "gy", "gz"), None), P(None, ("gx", "gy", "gz")))
    return jax.shard_map(shards, mesh=mesh, in_specs=in_specs, out_specs=out_specs, check_vma=False)
```

```python
import functools

import jax
import jax.numpy as jnp
from jax import lax
from jax.experimental import pallas as pl
from jax.experimental.pallas import tpu as pltpu
from jax.sharding import PartitionSpec as P

CX = 4
CY = 4
CZ = 4
ORB = 9
NEIGH = 15
ATOMS = 2 * CX * CY * CZ
VECS = 128
NX = 2 * CY * CZ
NY = 2 * (CX + 2) * CZ
NZ = 2 * (CX + 2) * (CY + 2)
BEFORE_Y = ATOMS + 2 * NX
BEFORE_Z = BEFORE_Y + 2 * NY
SLOTS = BEFORE_Z + 2 * NZ
ROWS_X = ORB * NX + 16
ROWS_Y = ORB * NY + 16
ROWS_Z = ORB * NZ + 8
KINDS = (1, 2, 4, 3, 5, 6, 7)
SECOND_SIZE = {kind: 2 * 4 ** (3 - kind.bit_count()) for kind in KINDS}
FIRST_SIZE = {kind: 2 * 5 ** (3 - kind.bit_count()) for kind in KINDS}
SECOND_AT = {kind: ATOMS + sum(SECOND_SIZE[k] for k in KINDS[:n]) for n, kind in enumerate(KINDS)}
FIRST = 256
FIRST_AT = {kind: FIRST + sum(FIRST_SIZE[k] for k in KINDS[:n]) for n, kind in enumerate(KINDS)}
LANES = 448
AXES = ("gx", "gy", "gz")
F32 = jnp.float32
BF16 = jnp.bfloat16
VMEM = pl.BlockSpec(memory_space=pltpu.VMEM)
HBM = pl.BlockSpec(memory_space=pltpu.HBM)


def call(kernel, outs, args, scratch=(), flops=0, mib=12, in_hbm=(), out_hbm=()):
    shapes = [jax.ShapeDtypeStruct(shape, dtype) for shape, dtype in outs]
    moved = sum(a.size * a.dtype.itemsize for a in args) + sum(s.size * s.dtype.itemsize for s in shapes)
    return pl.pallas_call(
        kernel,
        out_shape=shapes,
        in_specs=[HBM if k in in_hbm else VMEM for k in range(len(args))],
        out_specs=[HBM if k in out_hbm else VMEM for k in range(len(shapes))],
        scratch_shapes=list(scratch),
        compiler_params=pltpu.CompilerParams(vmem_limit_bytes=mib << 20),
        cost_estimate=pl.CostEstimate(flops=flops, bytes_accessed=moved, transcendentals=0),
    )(*args)


def odd(axis):
    return lax.axis_index(axis) & 1


def swapped(value, axis, second):
    count = lax.axis_size(axis)
    pairs = [((k + second) % count, (k + 1 + second) % count) for k in range(0, count, 2)]
    return lax.ppermute(value, axis, pairs + [(b, a) for a, b in pairs])


def prep_kernel(ham, rows, turned, wide):
    turned[...] = jnp.zeros_like(turned)
    wide[...] = jnp.zeros_like(wide)
    for a in range(ORB):
        for b in range(ORB):
            turned[pl.ds(b, NEIGH, stride=16), :] = ham[a, b].astype(F32)
        flat = turned[...].T
        wide[0, pl.ds(a, ATOMS, stride=16), :] = flat[:, 0:128]
        wide[1, pl.ds(a, ATOMS, stride=16), :] = flat[:, 128:256]

    def pack(i, carry):
        at = pl.ds(pl.multiple_of(i * 16, 16), 16)
        rows[i, :, 0:128] = wide[0, at, :].astype(BF16)
        rows[i, :, 128:256] = wide[1, at, :].astype(BF16)
        return carry

    lax.fori_loop(0, ATOMS, pack, 0, unroll=8)


def scale_of(level):
    return jnp.exp2(level * 0.25) * (1.0 / 32767.0)


def packed_of(level):
    return jnp.exp2(level * -0.25) * 32767.0


def level_of(message):
    rows = message.shape[0]
    return message[rows - 16 : rows, :].astype(jnp.int32).astype(F32)[8:16]


def pack(plain, message, level):
    fixed = message.dtype == jnp.int16
    rows = message.shape[0]
    if fixed:
        factor = jnp.concatenate([packed_of(level)] * 2, axis=0)
    for t in range(0, rows, 16):
        value = plain[t : t + 16, :]
        if fixed:
            value = jnp.round(value * factor)
            if t == rows - 16:
                value = jnp.concatenate([value[0:8], level], axis=0)
            message[t : t + 16, :] = value.astype(jnp.int32).astype(jnp.int16)
        else:
            message[t : t + 16, :] = value.astype(BF16)


def unpack(message, plain):
    if message.dtype != jnp.int16:
        for t in range(0, message.shape[0], 16):
            plain[t : t + 16, :] = message[t : t + 16, :].astype(F32)
        return
    factor = jnp.concatenate([scale_of(level_of(message))] * 2, axis=0)
    for t in range(0, message.shape[0], 16):
        plain[t : t + 16, :] = message[t : t + 16, :].astype(jnp.int32).astype(F32) * factor


def highest(levels):
    return functools.reduce(jnp.maximum, levels)


def pick_y(upper, own, u1, u2, picked):
    picked[ROWS_Y - 16 :] = jnp.zeros((16, VECS), F32)
    for b in range(ORB):
        take = [own[b, 16 * q : 16 * q + 16] for q in range(2 * CX)]
        take += [u[b * NX + 16 * q : b * NX + 16 * q + 16] for u in (u1, u2) for q in range(2)]
        for q, rows in enumerate(take):
            picked[b * NY + 4 * q : b * NY + 4 * q + 4] = jnp.where(upper, rows[12:16], rows[0:4])


def second_y_kernel(x2, x1, level, own, out, u1, u2, tall, picked):
    unpack(x1, u1)
    unpack(x2, u2)
    tall[...] = level[...]
    if out.dtype == jnp.int16:
        tall[...] = highest([level[...], level_of(x1), level_of(x2)])
    pick_y(odd("gy") == 1, own, u1, u2, picked)
    pack(picked, out, tall[...])


def first_y_kernel(tall, own, u1, u2, out, picked):
    pick_y(odd("gy") == 0, own, u1, u2, picked)
    pack(picked, out, tall[...])


def unpack_kernel(message, level, plain, tall):
    unpack(message, plain)
    tall[...] = highest([level[...], level_of(message)]) if message.dtype == jnp.int16 else level[...]


def faces_z_kernel(y1, level, own, u1, u2, v2, out1, out2, v1, p1, p2):
    fixed = out1.dtype == jnp.int16
    unpack(y1, v1)
    even = odd("gz") == 0
    p1[ROWS_Z - 8 :] = jnp.zeros((8, VECS), F32)
    p2[ROWS_Z - 8 :] = jnp.zeros((8, VECS), F32)
    ghosts = ((u1, NX), (u2, NX), (v1, NY), (v2, NY))
    for b in range(ORB):
        faces = []
        for z in (0, CZ - 1):
            at = pl.ds(z, ATOMS // CZ, stride=CZ)
            faces.append([own[b, at, :]])
            faces[-1] += [ref[pl.ds(b * rows + z, rows // CZ, stride=CZ), :] for ref, rows in ghosts]
        at = b * NZ
        for low, high in zip(*faces):
            rows = low.shape[0]
            p1[at : at + rows] = jnp.where(even, high, low)
            p2[at : at + rows] = jnp.where(even, low, high)
            at += rows
    level = highest([level[...], level_of(y1)]) if fixed else level[...]
    pack(p1, out1, level)
    pack(p2, out2, level)


def loop(count, body, unroll):
    def step(k, carry):
        body(k)
        return carry

    lax.fori_loop(0, count, step, 0, unroll=unroll)


def aligned(row, count=16):
    return pl.ds(pl.multiple_of(row, count), count)


def make_tiles(pieces, loose, tiles, base):
    slots = sum(count for _, count in pieces)
    zero = jnp.zeros((8, VECS), F32)

    def clear(j):
        loose[aligned(j * 16 + 8, 8), :] = zero

    loop(slots, clear, 72)
    for b in range(ORB):
        at = 0
        for rows_of, count in pieces:
            loose[pl.ds(at * 16 + b, count, stride=16), :] = rows_of(b)
            at += count

    def split(j):
        value = loose[aligned(j * 16), :]
        high = value.astype(BF16)
        tiles[base + j, :, 0:128] = high
        if tiles.shape[2] == 256:
            tiles[base + j, :, 128:256] = (value - high.astype(F32)).astype(BF16)

    loop(slots, split, 72)


def front_pieces(own, plains):
    pieces = [(lambda b: own[b], ATOMS)]
    for plain, count in zip(plains, (NX, NX, NY, NY)):
        pieces.append((lambda b, plain=plain, count=count: plain[b * count : b * count + count], count))
    return pieces


def back_pieces(messages, plains):
    pieces = []
    for message, plain in zip(messages, plains):
        unpack(message, plain)
        pieces.append((lambda b, plain=plain: plain[b * NZ : b * NZ + NZ], NZ))
    return pieces


def back_tiles(front, messages, plains, loose, tiles):
    def copy(j):
        tiles[j] = front[j]

    loop(BEFORE_Z, copy, 72)
    make_tiles(back_pieces(messages, plains), loose, tiles, BEFORE_Z)


def middle(k):
    return 4 * (k >> 1) + 1 + (k & 1)


def outer(k):
    return 4 * (k >> 1) + 3 * (k & 1)


def fetch(slots, table, arrived):
    copy = pltpu.make_async_copy(slots, table, arrived)
    copy.start()
    return copy


def gather(slots, tiles, i):
    taken = [tiles[slots[m, i]] for m in range(NEIGH)]
    return jnp.concatenate(taken + taken[:1], axis=0)


def apply_atoms(slots, rows, tiles, applied, which, place):
    def atom(k):
        i = which(k)
        product = jnp.dot(rows[i], gather(slots, tiles, i), preferred_element_type=F32)
        if tiles.shape[2] == 256:
            product = product[:, 0:128] + product[:, 128:256]
        applied[aligned(place(k) * 16), :] = product

    loop(ATOMS // 2, atom, ATOMS // 2)


def densities(slots, noise_tiles, values, dense, which, place):
    def atom(k):
        i = which(k)
        value = values[aligned(i * 16), :]
        high = value.astype(BF16)
        low = (value - high.astype(F32)).astype(BF16)
        product = lax.dot_general(
            jnp.concatenate([high, low], axis=0),
            gather(slots, noise_tiles, i),
            (((1,), (1,)), ((), ())),
            preferred_element_type=F32,
        )
        product = product[0:16] + product[16:32]
        dense[0, aligned(place(k) * 16), :] = product[:, 0:128]
        dense[1, aligned(place(k) * 16), :] = product[:, 128:256]

    loop(ATOMS // 2, atom, ATOMS // 2)


def tiles_kernel(level, own, z1, z2, u1, u2, v1, v2, tiles, loose, *plains):
    make_tiles(front_pieces(own, (u1, u2, v1, v2)) + back_pieces((z1, z2), plains), loose, tiles, 0)


def spread_middle(half, applied):
    def put(k):
        applied[aligned(middle(k) * 16), :] = half[aligned(k * 16), :]

    loop(ATOMS // 2, put, ATOMS // 2)


def front_kernel(slots, rows, own, u1, u2, v1, v2, front, half, table, arrived, loose):
    copy = fetch(slots, table, arrived)
    make_tiles(front_pieces(own, (u1, u2, v1, v2)), loose, front, 0)
    copy.wait()
    apply_atoms(table, rows, front, half, middle, lambda k: k)


def front_third_kernel(coef, slots, rows, sum_in, noise_tiles, own, u1, u2, v1, v2, front, half, dense,
                       table, arrived, loose, applied):
    copy = fetch(slots, table, arrived)
    make_tiles(front_pieces(own, (u1, u2, v1, v2)), loose, front, 0)
    copy.wait()
    apply_atoms(table, rows, front, half, middle, lambda k: k)
    applied[...] = jnp.zeros_like(applied)
    spread_middle(half, applied)
    for a in range(ORB):
        at = pl.ds(a, ATOMS, stride=16)
        applied[at, :] = sum_in[a] + (2.0 * coef[3 : 4, :]) * applied[at, :]
    densities(table, noise_tiles, applied, dense, middle, lambda k: k)


def put_faces(now, out1, out2, level, p1, p2):
    even = odd("gx") == 0
    p1[ROWS_X - 16 :] = jnp.zeros((16, VECS), F32)
    p2[ROWS_X - 16 :] = jnp.zeros((16, VECS), F32)
    most = jnp.zeros((8, VECS), F32)
    for b in range(ORB):
        value = now[b]
        for row in range(0, ATOMS, 8):
            most = jnp.maximum(most, jnp.abs(value[row : row + 8]))
        for p in range(2):
            low, high = value[64 * p : 64 * p + 16], value[64 * p + 48 : 64 * p + 64]
            at = b * NX + 16 * p
            p1[at : at + 16] = jnp.where(even, high, low)
            p2[at : at + 16] = jnp.where(even, low, high)
    most = jnp.maximum(jnp.max(most, axis=0, keepdims=True), 1e-30)
    steps = jnp.ceil(jnp.log2(most) * 4.0 + 0.01)
    level[...] = jnp.broadcast_to(steps, (8, VECS))
    pack(p1, out1, level[...])
    pack(p2, out2, level[...])


def rest(slots, table, arrived, rows, front, half, messages, plains, loose, tiles, applied):
    copy = fetch(slots, table, arrived)
    back_tiles(front, messages, plains, loose, tiles)
    copy.wait()
    apply_atoms(table, rows, tiles, applied, outer, outer)
    spread_middle(half, applied)


def first_kernel(coef, slots, rows, own, front, half, z1, z2, now, total, out1, out2, level,
                 table, arrived, tiles, loose, applied, p1, p2, *plains):
    rest(slots, table, arrived, rows, front, half, (z1, z2), plains, loose, tiles, applied)
    for a in range(ORB):
        value = applied[pl.ds(a, ATOMS, stride=16), :]
        now[a] = value
        total[a] = coef[0 : 1, :] * own[a] + coef[1 : 2, :] * value
    put_faces(now, out1, out2, level, p1, p2)


def second_kernel(coef, slots, rows, prev, sum_in, first, front, half, z1, z2, now, total, out1, out2, level,
                  table, arrived, tiles, loose, applied, p1, p2, *plains):
    rest(slots, table, arrived, rows, front, half, (z1, z2), plains, loose, tiles, applied)
    for a in range(ORB):
        value = 2.0 * applied[pl.ds(a, ATOMS, stride=16), :] - prev[a]
        now[a] = value
        total[a] = sum_in[a] + coef[2 : 3, :] * value - coef[3 : 4, :] * first[a]
    put_faces(now, out1, out2, level, p1, p2)


def third_kernel(coef, slots, lanes, rows, sum_in, noise_tiles, deriv, front, half, dense_half, z1, z2,
                 total, forces, sent, table, arrived, tiles, loose, applied, dense, turned, stacked, slopes, loaded, written, left, *plains):
    load = pltpu.make_async_copy(deriv, slopes, loaded)
    load.start()
    rest(slots, table, arrived, rows, front, half, (z1, z2), plains, loose, tiles, applied)
    for a in range(ORB):
        at = pl.ds(a, ATOMS, stride=16)
        value = sum_in[a] + (2.0 * coef[3 : 4, :]) * applied[at, :]
        written[a] = value
        applied[at, :] = value
    leave = pltpu.make_async_copy(written, total, left)
    leave.start()
    densities(table, noise_tiles, applied, dense, outer, outer)
    for side in range(2):
        spread_middle(dense_half.at[side], dense.at[side])
    load.wait()
    pair = [jnp.zeros((NEIGH, ATOMS), F32) for _ in range(3)]
    for a in range(ORB):
        at = pl.ds(a, ATOMS, stride=16)
        turned[0:128] = dense[0, at, :].T
        turned[128:256] = dense[1, at, :].T
        for b in range(ORB):
            density = turned[pl.ds(b, NEIGH, stride=16), :]
            for c in range(3):
                pair[c] = pair[c] + slopes[c, a, b].astype(F32) * density
    others = lax.broadcasted_iota(jnp.int32, (NEIGH, ATOMS), 0) > 0
    stacked[...] = jnp.zeros_like(stacked)
    own_rows = []
    for c in range(3):
        value = jnp.where(others, pair[c] * (1.0 / VECS), 0.0)
        high = value.astype(BF16).astype(F32)
        stacked[pl.ds(c, NEIGH, stride=16), :] = high
        stacked[pl.ds(8 + c, NEIGH, stride=16), :] = value - high
        own_rows.append(jnp.sum(value, axis=0, keepdims=True))
    lane = lax.broadcasted_iota(jnp.int32, (LANES, ATOMS), 0)
    summed = jnp.zeros((16, LANES), F32)
    for m in range(1, NEIGH):
        hit = jnp.where(lane == lanes[m : m + 1, :], 1.0, 0.0).astype(BF16)
        summed = summed + lax.dot_general(
            stacked[16 * m : 16 * m + 16].astype(BF16), hit, (((1,), (1,)), ((), ())), preferred_element_type=F32
        )
    summed = summed[0:8] + summed[8:16]
    forces[...] = summed[:, 0:FIRST]
    for c in range(3):
        forces[c : c + 1, 0:ATOMS] = forces[c : c + 1, 0:ATOMS] - own_rows[c]
    send(sent, summed, FIRST_AT, FIRST_SIZE, place_of())
    leave.wait()


def place_of():
    return 4 * odd("gx") + 2 * odd("gy") + odd("gz")


def send(sent, value, starts, sizes, place):
    sent[...] = jnp.zeros_like(sent)
    for kind in KINDS:
        sent[place ^ kind, :, 0 : sizes[kind]] = value[:, starts[kind] : starts[kind] + sizes[kind]]


def spread(got, lanes, place, width):
    lane = lax.broadcasted_iota(jnp.int32, (width, VECS), 0)
    hits, terms = [], []
    for kind in KINDS:
        value = got[place ^ kind]
        parts = []
        for _ in range(3):
            parts.append(value.astype(BF16).astype(F32))
            value = value - parts[-1]
        terms.append(jnp.concatenate(parts, axis=0).astype(BF16))
        hits.append(jnp.where(lane == lanes[kind : kind + 1, :], 1.0, 0.0).astype(BF16))
    summed = lax.dot_general(
        jnp.concatenate(terms, axis=1), jnp.concatenate(hits, axis=1), (((1,), (1,)), ((), ())),
        preferred_element_type=F32,
    )
    return summed[0:8] + summed[8:16] + summed[16:24]


def merge_kernel(held, got, out, sent):
    value = held[...] + spread(got, landing_lanes(0), place_of(), FIRST)
    out[...] = value[:, 0:ATOMS]
    send(sent, value, SECOND_AT, SECOND_SIZE, 7 - place_of())


def finish_kernel(held, got, out):
    value = held[...] + spread(got, landing_lanes(1), 7 - place_of(), ATOMS)
    out[...] = value[0:3]


def blocks(second):
    sizes = [lax.axis_size(axis) for axis in AXES]
    pairs = [[((k + second) % n, (k + 1 + second) % n) for k in range(0, n, 2)] for n in sizes]
    return [
        [(x * sizes[1] + y) * sizes[2] + z for x in px for y in py for z in pz]
        for px in pairs[0] for py in pairs[1] for pz in pairs[2]
    ]


def trade_all(sent, second):
    return lax.all_to_all(sent, AXES, 0, 0, tiled=True, axis_index_groups=blocks(second))


def number(basis, digits, bases):
    for digit, base in zip(digits, bases):
        basis = basis * base + digit
    return basis


def start_of(kind, starts):
    return sum(jnp.where(kind == k, at, 0) for k, at in starts.items())


def second_lane(basis, cells, kinds):
    inner = number(basis, [jnp.where(k == 1, 0, c) for c, k in zip(cells, kinds)], [jnp.where(k == 1, 1, 4) for k in kinds])
    kind = 4 * kinds[0] + 2 * kinds[1] + kinds[2]
    return jnp.where(kind > 0, start_of(kind, SECOND_AT) + inner, number(basis, cells, (CX, CY, CZ)))


def landing_lanes(second):
    kind = lax.broadcasted_iota(jnp.int32, (8, VECS), 0)
    rest = lax.broadcasted_iota(jnp.int32, (8, VECS), 1)
    cells = [None] * 3
    for d in (2, 1, 0):
        traded = ((kind >> (2 - d)) & 1) == 1
        near = jnp.where(odd(AXES[d]) == second, CX - 1, 0)
        less = rest >> 2 if second else (rest * 205) >> 10
        cells[d] = jnp.where(traded, near, rest - (4 if second else 5) * less)
        rest = jnp.where(traded, rest, less)
    ghost = [jnp.where(c == CX, 1, 0) for c in cells]
    lane = second_lane(rest, cells, ghost)
    return jnp.where((rest < 2) & (kind > 0), lane, -1)


def slots_of(neighbours, parity):
    cells = CX * CY * CZ
    size_x, size_y, size_z = (lax.axis_size(axis) for axis in ("gx", "gy", "gz"))
    partner = neighbours.T
    domain = partner // ATOMS
    within = partner % ATOMS
    basis = within // cells
    remain = within % cells
    ex = domain // (size_y * size_z) * CX + remain // (CY * CZ) - lax.axis_index("gx") * CX + 1
    ey = domain // size_z % size_y * CY + remain // CZ % CY - lax.axis_index("gy") * CY + 1
    ez = domain % size_z * CZ + remain % CZ - lax.axis_index("gz") * CZ + 1
    ex = jnp.remainder(ex, CX * size_x)
    ey = jnp.remainder(ey, CY * size_y)
    ez = jnp.remainder(ez, CZ * size_z)
    x_out = (ex == 0) | (ex == CX + 1)
    y_out = (ey == 0) | (ey == CY + 1)
    z_out = (ez == 0) | (ez == CZ + 1)
    x_trade = ((ex == 0) == (parity[0] == 0)).astype(jnp.int32)
    y_trade = ((ey == 0) == (parity[1] == 0)).astype(jnp.int32)
    z_trade = ((ez == 0) == (parity[2] == 0)).astype(jnp.int32)
    q = jnp.where(x_out, 2 * CX + 2 * x_trade + basis, basis * CX + ex - 1)
    r_in = q * CY + ey - 1
    r_out = 2 * (CX + 2) * CY + y_trade * (2 * (CX + 2)) + q
    r = jnp.where(y_out, r_out, r_in)
    slots = jnp.where(z_out, BEFORE_Z + z_trade * NZ + r, r * CZ + ez - 1)
    cells = [e - 1 for e in (ex, ey, ez)]
    outside = (x_out, y_out, z_out)
    trades = (x_trade, y_trade, z_trade)
    firsts = [o & (t == 0) for o, t in zip(outside, trades)]
    seconds = [o & (t == 1) for o, t in zip(outside, trades)]
    kind = 4 * firsts[0] + 2 * firsts[1] + firsts[2]
    digits = [jnp.where(f, 0, jnp.where(s, 4, c)) for f, s, c in zip(firsts, seconds, cells)]
    inner = number(basis, digits, [jnp.where(f, 1, 5) for f in firsts])
    lanes = second_lane(basis, cells, [s.astype(jnp.int32) for s in seconds])
    lanes = jnp.where(kind > 0, start_of(kind, FIRST_AT) + inner, lanes)
    return slots.astype(jnp.int32), lanes.astype(jnp.int32)


def passing(kernel, count, held):
    def with_held(*refs):
        kernel(*refs[:count], *refs[count + len(held) :])

    return with_held


def plain(rows):
    return pltpu.VMEM((rows, VECS), F32)


BACK_PLAINS = [plain(ROWS_Z), plain(ROWS_Z)]


def exchange(level, own, out1, out2, work, held=()):
    dtype = out1.dtype
    rows_x, rows_y = ((ROWS_X, VECS), F32), ((ROWS_Y, VECS), F32)
    x2, x1 = swapped(out2, "gx", 1), swapped(out1, "gx", 0)
    out2, u1, u2, level = call(
        passing(second_y_kernel, 4, held), [((ROWS_Y, VECS), dtype), rows_x, rows_x, ((8, VECS), F32)],
        (x2, x1, level, own) + held, [plain(ROWS_Y)],
    )
    y2 = swapped(out2, "gy", 1)
    (out1,) = call(
        first_y_kernel, [((ROWS_Y, VECS), dtype)], (level, own, u1, u2),
        [plain(ROWS_Y)],
    )
    y1 = swapped(out1, "gy", 0)
    v2, level = call(unpack_kernel, [rows_y, ((8, VECS), F32)], (y2, level), flops=1 << 31)
    out1, out2, v1 = call(
        faces_z_kernel, [((ROWS_Z, VECS), dtype)] * 2 + [rows_y],
        (y1, level, own, u1, u2, v2), BACK_PLAINS,
    )
    z1, z2 = swapped(out1, "gz", 0), swapped(out2, "gz", 1)
    return work(own, u1, u2, v1, v2), (z1, z2), (u1, u2, v1, v2)


def shards(noise_vectors, hamiltonian, derivative, neighbours, coefficients):
    parity = jnp.stack([lax.axis_index(axis) % 2 for axis in AXES]).astype(jnp.int32)
    slots, lanes = slots_of(neighbours, parity)
    coefs = jnp.broadcast_to(coefficients[:, None], (4, VECS))
    lattice = noise_vectors.reshape(ORB, 2, CX, CY * CZ, VECS)
    low = lattice[:, :, 0].reshape(ORB * NX, VECS)
    high = lattice[:, :, CX - 1].reshape(ORB * NX, VECS)
    room = jnp.zeros((16, VECS), BF16)
    even = parity[0] == 0
    out1 = jnp.concatenate([jnp.where(even, high, low), room])
    out2 = jnp.concatenate([jnp.where(even, low, high), room])
    (rows,) = call(
        prep_kernel, [((ATOMS, 16, 256), BF16)], (hamiltonian.transpose(1, 2, 0, 3),),
        [plain(256), pltpu.VMEM((2, ATOMS * 16, 128), F32)], flops=1 << 22,
    )
    noise = noise_vectors.astype(F32)
    whole = ((ORB, ATOMS, VECS), F32)
    plane = ((ROWS_X, VECS), jnp.int16)
    tile = ((8, 128), F32)
    half = ((ATOMS // 2 * 16, VECS), F32)
    front_loose, loose, applied = plain(BEFORE_Z * 16), plain((SLOTS - BEFORE_Z) * 16), plain(ATOMS * 16)
    faces = [plain(ROWS_X), plain(ROWS_X)]
    table = [pltpu.SMEM((NEIGH, ATOMS), jnp.int32), pltpu.SemaphoreType.DMA]

    def work(*vectors, width=256):
        return call(
            front_kernel, [((BEFORE_Z, 16, width), BF16), half], (slots, rows) + vectors,
            table + [front_loose], flops=1 << 29,
        )

    fronts, ghosts, plains = exchange(jnp.zeros((8, VECS), F32), noise, out1, out2, functools.partial(work, width=128))
    first, total, out1, out2, level = call(
        first_kernel, [whole, whole, plane, plane, tile],
        (coefs, slots, rows, noise, *fronts, *ghosts),
        table + [pltpu.VMEM((SLOTS, 16, VECS), BF16), loose, applied] + faces + BACK_PLAINS, flops=1 << 29,
    )
    (noise_tiles,) = call(
        tiles_kernel, [((SLOTS, 16, VECS), BF16)], (level, noise, *ghosts, *plains), [plain(SLOTS * 16)] + BACK_PLAINS
    )
    fronts, ghosts, _ = exchange(level, first, out1, out2, work, (noise_tiles,))
    second, total, out1, out2, level = call(
        second_kernel, [whole, whole, plane, plane, tile],
        (coefs, slots, rows, noise, total, first, *fronts, *ghosts),
        table + [pltpu.VMEM((SLOTS, 16, 256), BF16), loose, applied] + faces + BACK_PLAINS, flops=1 << 29,
    )

    def last_work(*vectors):
        return call(
            front_third_kernel, [((BEFORE_Z, 16, 256), BF16), half, ((2,) + half[0], F32)],
            (coefs, slots, rows, total, noise_tiles) + vectors,
            table + [front_loose, applied], flops=1 << 30,
        )

    fronts, ghosts, _ = exchange(level, second, out1, out2, last_work)
    eight = ((8, 8, 128), F32)
    slopes = derivative.transpose(0, 2, 3, 1, 4)
    weighted, held, sent = call(
        third_kernel, [whole, ((8, FIRST), F32), eight],
        (coefs, slots, lanes, rows, total, noise_tiles, slopes, *fronts, *ghosts),
        table + [pltpu.VMEM((SLOTS, 16, 256), BF16), loose, applied, pltpu.VMEM((2, ATOMS * 16, 128), F32), plain(256),
         plain(256), pltpu.VMEM(slopes.shape, BF16), pltpu.SemaphoreType.DMA,
         pltpu.VMEM((ORB, ATOMS, VECS), F32), pltpu.SemaphoreType.DMA] + BACK_PLAINS,
        flops=1 << 30, in_hbm=(6,), out_hbm=(0,),
    )
    held, sent = call(merge_kernel, [tile, eight], (held, trade_all(sent, 0)))
    (forces,) = call(finish_kernel, [((3, ATOMS), F32)], (held, trade_all(sent, 1)))
    return weighted, forces


def solution(mesh):
    in_specs = (
        P(None, ("gx", "gy", "gz"), None),
        P(None, None, None, ("gx", "gy", "gz")),
        P(None, None, None, None, ("gx", "gy", "gz")),
        P(("gx", "gy", "gz"), None),
        P(),
    )
    out_specs = (P(None, ("gx", "gy", "gz"), None), P(None, ("gx", "gy", "gz")))
    return jax.shard_map(shards, mesh=mesh, in_specs=in_specs, out_specs=out_specs, check_vma=False)
```
